128 devices in a mesh: gx: 8 (over y, core), gy: 16 (over x, z).
Axes of the slice: x: 4, y: 4, z: 4, core: 2. Of those that a mesh axis runs over, the one named last changes fastest.
Arguments:
- outline: float32 [256, 1024, 512], P('gx', 'gy'), may hold values from -0.7 to 0.7, as said below
- centres: float32 [256, 1024, 2], P('gx', 'gy'), may hold values from -0.75 to 0.75
- velocity: float32 [256, 1024, 2], P('gx', 'gy'), may hold values from -6 to 6
- mass: float32 [256, 1024], P('gx', 'gy'), may hold values from 0.5 to 4
- response: float32 [256, 1024, 64], P('gx', 'gy'), may hold values from -0.75 to 0.75
- pairs: int32 [8, 16, 512, 4], P('gx', 'gy'), may hold values from 0 to 2047, as said below
- pair_count: int32 [8, 16], P('gx', 'gy'), may hold values from 1 to 512, as said below
- forcing: float32 [262144, 128], P(('gx', 'gy')), may hold values from -6 to 6
- ocean_dest: int32 [262144, 1], P(('gx', 'gy')), may hold values from 0 to 127; in each aligned block of 2048 rows (0 to 2047, 2048 to 4095, ...) at most 40 rows name the same one
- ocean_floe: int32 [262144], P(('gx', 'gy')), may hold values from 0 to 2047
Outputs:
- final_velocity: float32 [256, 1024, 2], P('gx', 'gy')
- final_centres: float32 [256, 1024, 2], P('gx', 'gy')
The draws below stay inside these ranges and needn't reach their ends.
Inputs may be any that keep to these rules, and one draw needn't show every extreme that they name: `pairs`: each slot holds a local floe below 2048, a neighbour code below 8, and two tiles below 2; slots from pair_count on are padding. `pair_count`: some block's list is full. `ocean_dest`: the rows of one block name any one block at most 40 times. `outline`: polygon vertices lie at radii 0.3 to 0.7 around the centre, in order of angle.
All inputs are finite; a program needn't handle non-finite values.
Results may differ from the reference program's by a relative error of at most 0.0003.
Values sent between devices are 32-bit elements; how exact they have to be, the bound alone decides.
No kernel may reach another device: no remote copies, remote signals or barrier semaphores. Data moves between devices by JAX's collectives and lax.ppermute only.
A program may use at most 128 MiB of HBM per device.

```python
import math
import jax
import jax.numpy as jnp
import numpy as np
from jax import lax

FX = 32
FY = 64
V = 256
TILE = 128
NB = 64
PMAX = 512
ROWS_DEV = 2048
STEPS = 3
NTILE = 2
F_DEV = 2048
NXF = 256
NYF = 1024
BLKX = 8
BLKY = 16
CAP = 40
ROWS = 262144
N_GX = 8
N_GY = 16


def draw_outline(key, part):
    key = jax.random.fold_in(key, 11)
    first, second = jax.random.split(key)
    spread = 0.25
    angle_noise = jax.random.uniform(first, (NXF, NYF, V), jnp.float32, -1.0, 1.0)
    radius = 0.5 * (1.0 + spread * jax.random.uniform(second, (NXF, NYF, V), jnp.float32, -1.0, 1.0))
    theta = (jnp.arange(V, dtype=jnp.float32) + 0.3 * angle_noise) * (2.0 * math.pi / V)
    return jnp.concatenate([radius * jnp.cos(theta), radius * jnp.sin(theta)], axis=2)


def draw_pairs(key, part):
    key = jax.random.fold_in(key, 23)
    keys = jax.random.split(key, 4)
    shape = (BLKX, BLKY, PMAX, 1)
    local = jax.random.randint(keys[0], shape, 0, F_DEV)
    code = jax.random.randint(keys[1], shape, 0, 8)
    tile_own = jax.random.randint(keys[2], shape, 0, NTILE)
    tile_other = jax.random.randint(keys[3], shape, 0, NTILE)
    return jnp.concatenate([local, code, tile_own, tile_other], axis=3).astype(jnp.int32)


def draw_pair_count(key, part):
    key = jax.random.fold_in(key, 37)
    first, second = jax.random.split(key)
    counts = jax.random.randint(first, (BLKX, BLKY), max(1, PMAX // 8), PMAX // 2 + 1)
    chosen = jax.random.randint(second, (), 0, BLKX * BLKY)
    number = jnp.arange(BLKX * BLKY, dtype=jnp.int32).reshape(BLKX, BLKY)
    return jnp.where(number == chosen, PMAX, counts).astype(jnp.int32)


def touch_ends(entries, rng, smallest, high):
    place = [jax.random.randint(jax.random.fold_in(rng, axis), (), 0, length) for axis, length in enumerate(entries.shape)]
    longest = entries.shape.index(max(entries.shape))
    beside = place[:longest] + [(place[longest] + 1) % entries.shape[longest]] + place[longest + 1:]
    return entries.at[tuple(place)].set(smallest).at[tuple(beside)].set(high)


def block_scale(key, shape, cuts, smallest, top_value):
    def one(dim, parts):
        draws = jax.random.uniform(jax.random.fold_in(jax.random.fold_in(key, 6), dim), (parts,), jnp.float32, smallest / len(cuts), top_value / len(cuts))
        return jnp.repeat(jnp.exp(draws), shape[dim] // parts).reshape((-1,) + (1,) * (len(shape) - dim - 1))

    level = one(*cuts[0])
    for cut in cuts[1:]:
        level = level * one(*cut)
    return level


def shared_out(key, own, number, rows, count, top, most, slope):
    sequence = jax.random.permutation(key, count)
    heavy_load, usual = portions_of(count, rows * top, most, slope, True), portions_of(count, rows * top, most, slope, False)
    places = jnp.arange(count)

    def named(lengths, turn):
        used = int((lengths > 0).sum())
        fixed = max(1, used // 4)
        shifted = fixed + (places - fixed + turn * (used - fixed)) % max(1, count - fixed)
        return jnp.zeros((count,), jnp.int32).at[sequence[jnp.where(places < fixed, places, shifted)]].set(jnp.asarray(lengths, jnp.int32))

    lengths = jnp.where(number % 4 == 0, named(heavy_load, number // 4), named(usual, number - number // 4 - 1))
    mixed = jax.random.permutation(jax.random.fold_in(own, 3), count)
    giver, sink = mixed[0:count // 2 * 2:2], mixed[1:count // 2 * 2:2]
    slack = jnp.minimum(lengths[giver] - 1, most - lengths[sink]) // 2
    slack = jnp.where((giver == sequence[0]) | (sink == sequence[0]) | (lengths[sink] == 0), 0, jnp.maximum(slack, 0))
    shifted = jax.random.randint(jax.random.fold_in(own, 4), (count // 2,), 0, 1 << 20) % (slack + 1)
    lengths = lengths.at[giver].add(-shifted).at[sink].add(shifted)
    members = jnp.searchsorted(jnp.cumsum(lengths), jnp.arange(rows * top), side="right").astype(jnp.int32)
    grid = members.reshape(top, rows).T
    grid = grid[jax.random.permutation(jax.random.fold_in(own, 1), rows)]
    turn = jax.random.randint(jax.random.fold_in(own, 2), (rows, 1), 0, top)
    return jnp.take_along_axis(grid, (jnp.arange(top)[None, :] + turn) % top, axis=1)


def portions_of(number_of, total, reach, slope, full):
    loads = [(1 << 20) // math.isqrt(rank ** slope) + 1 for rank in range(1, number_of + 1)]
    largest = reach if full else min(reach, max(-(-total // number_of), total * loads[0] // sum(loads)))
    least = 1 if total - largest >= number_of - 1 else 0
    given, spare = [largest] + [least] * (number_of - 1), total - largest - least * (number_of - 1)
    while spare > 0:
        candidates = [i for i in range(1, number_of) if given[i] < largest] or [i for i in range(1, number_of) if given[i] < reach]
        pool, remaining = sum([loads[i] for i in candidates]), spare
        for i in candidates:
            more = min(reach - given[i], max(1, remaining * loads[i] // pool), spare)
            given[i] = given[i] + more
            spare = spare - more
    return np.array(given)


def normal_values(stream_key, dims, scale, reach, shards=(), kind=jnp.bfloat16):
    loudness = block_scale(stream_key, dims, shards, -0.22, 0.18) if shards else 1.0
    array = jax.random.normal(stream_key, dims, jnp.float32) * scale * loudness
    return jnp.minimum(jnp.maximum(array, -reach), reach).astype(kind)


def setup_inputs(seed: int = 0) -> dict:
    seeds = jax.random.split(jax.random.key(seed), 11)
    outline = draw_outline(jax.random.fold_in(seeds[10], 71), 0)
    centres = normal_values(seeds[1], (NXF, NYF, 2), 0.05, 0.75, ((0, 8), (1, 16)), jnp.float32)
    velocity = normal_values(seeds[2], (NXF, NYF, 2), 0.5, 6.0, ((0, 8), (1, 16)), jnp.float32)
    mass = jnp.clip(jnp.exp(math.log(4.0) - 2.0794415 * jax.random.uniform(seeds[3], (NXF, NYF), jnp.float32) ** block_scale(seeds[3], (NXF, NYF), ((0, 8), (1, 16)), -0.2, 0.2)), 0.5, 4.0)
    response = normal_values(seeds[4], (NXF, NYF, NB), NB ** -0.5, 0.75, ((0, 8), (1, 16)), jnp.float32)
    pairs = draw_pairs(jax.random.fold_in(seeds[10], 71), 0)
    pair_count = draw_pair_count(jax.random.fold_in(seeds[10], 71), 0)
    forcing = normal_values(seeds[7], (ROWS, 2 * NB), 1.0, 6.0, ((0, 128),), jnp.float32)
    ocean_dest_keys = jax.random.split(jax.random.fold_in(seeds[8], 1), ROWS // ROWS_DEV)
    ocean_dest_turns = jax.random.permutation(jax.random.fold_in(seeds[8], 3), ROWS // ROWS_DEV)
    ocean_dest = jax.vmap(lambda own, number: shared_out(jax.random.fold_in(seeds[8], 2), own, number, ROWS_DEV, N_GX * N_GY, 1, CAP, 2))(ocean_dest_keys, ocean_dest_turns).reshape((ROWS, 1))
    ocean_floe = touch_ends(jax.random.randint(seeds[9], (ROWS,), 0, F_DEV), jax.random.fold_in(seeds[9], 1), 0, F_DEV - 1).astype(jnp.int32)
    return dict(outline=outline, centres=centres, velocity=velocity, mass=mass, response=response, pairs=pairs, pair_count=pair_count, forcing=forcing, ocean_dest=ocean_dest, ocean_floe=ocean_floe)


DIRX = (-1, -1, -1, 0, 0, 1, 1, 1)
DIRY = (-1, 0, 1, -1, 1, -1, 0, 1)
KAPPA = 1.0
INV_WIDTH = 100.0
DT = 0.1
DRAG = 0.5


def tile_force(own, other, step_x, step_y):
    diff_x = (own[:, 0, :, None] - other[:, 0, None, :]) - step_x[:, None, None]
    diff_y = (own[:, 1, :, None] - other[:, 1, None, :]) - step_y[:, None, None]
    weight = jnp.exp(-(diff_x * diff_x + diff_y * diff_y) * INV_WIDTH)
    return KAPPA * jnp.stack([jnp.sum(weight * diff_x, axis=(1, 2)), jnp.sum(weight * diff_y, axis=(1, 2))], axis=1)


def contact_forces(positions, pairs, pair_count):
    width = NYF + 2
    flat = jnp.pad(positions, ((1, 1), (1, 1), (0, 0))).reshape(-1, 2, NTILE, TILE)
    blk_x = jnp.arange(BLKX, dtype=jnp.int32)[:, None, None]
    blk_y = jnp.arange(BLKY, dtype=jnp.int32)[None, :, None]
    local = pairs[..., 0]
    code = pairs[..., 1]
    step_x = jnp.asarray(DIRX, dtype=jnp.int32)[code]
    step_y = jnp.asarray(DIRY, dtype=jnp.int32)[code]
    row = blk_x * FX + local // FY
    col = blk_y * FY + local % FY
    prow = row + step_x
    pcol = col + step_y
    slot = jnp.arange(PMAX, dtype=jnp.int32)[None, None, :]
    valid = (slot < pair_count[..., None]) & (prow >= 0) & (prow < NXF) & (pcol >= 0) & (pcol < NYF)
    own_idx = ((row + 1) * width + col + 1).reshape(-1, PMAX)
    other_idx = ((prow + 1) * width + pcol + 1).reshape(-1, PMAX)

    def block(items):
        oi, ot, pi, pt, sx, sy, ok = items
        own = flat[oi, :, ot, :]
        other = flat[pi, :, pt, :]
        return tile_force(own, other, sx.astype(jnp.float32), sy.astype(jnp.float32)) * ok.astype(jnp.float32)[:, None]

    forces = lax.map(block, (own_idx, pairs[..., 2].reshape(-1, PMAX), other_idx, pairs[..., 3].reshape(-1, PMAX),
                             step_x.reshape(-1, PMAX), step_y.reshape(-1, PMAX), valid.reshape(-1, PMAX)))
    forces = forces.reshape(-1, 2)
    accum = jnp.zeros(((NXF + 2) * width, 2), jnp.float32)
    accum = accum.at[own_idx.reshape(-1)].add(forces).at[other_idx.reshape(-1)].add(-forces)
    return accum.reshape(NXF + 2, width, 2)[1:-1, 1:-1]


def reference(outline, centres, velocity, mass, response, pairs, pair_count, forcing, ocean_dest, ocean_floe):
    dest = ocean_dest[:, 0]
    row = (dest // BLKY) * FX + ocean_floe // FY
    col = (dest % BLKY) * FY + ocean_floe % FY
    cell = row * NYF + col
    ocean_sum = jax.ops.segment_sum(forcing, cell, num_segments=NXF * NYF).reshape(NXF, NYF, 2, NB)
    ocean_force = jnp.einsum('xycb,xyb->xyc', ocean_sum, response, precision=lax.Precision.HIGHEST)
    shift = centres
    vel = velocity
    for step in range(STEPS):
        positions = outline + jnp.repeat(shift, V, axis=2)
        contact = contact_forces(positions, pairs, pair_count)
        vel = vel + DT * ((contact + ocean_force) - DRAG * vel) / mass[..., None]
        shift = shift + DT * vel
    return vel, shift
```

```python
import math

import jax
import jax.numpy as jnp
from jax import lax
from jax.experimental import pallas as pl
from jax.experimental.pallas import tpu as pltpu
from jax.sharding import PartitionSpec as P

FX, FY, V, TILE, NB, PMAX = 32, 64, 256, 128, 64, 512
DEVS, CAP, BLK = 128, 40, 48
STEPS = 3
DT, DRAG = 0.1, 0.5
H = 2
R = FX + 2 * H
NF = R * 128
TW = FY + 16
PADC = 8 - H
NLIST = 9
NCH = NLIST * PMAX // 128
NEIGH = ((0, 0), (-1, 0), (1, 0), (-1, -1), (0, -1), (1, -1), (-1, 1), (0, 1), (1, 1))
SC = math.sqrt(100.0 * math.log2(math.e))
F32, BF16, I32 = jnp.float32, jnp.bfloat16, jnp.int32
VMEM_BYTES = 52 * 1024 * 1024


def params():
    return pltpu.CompilerParams(vmem_limit_bytes=VMEM_BYTES)


def vspec():
    return pl.BlockSpec(memory_space=pltpu.VMEM)


def sspec():
    return pl.BlockSpec(memory_space=pltpu.SMEM)


def aspec():
    return pl.BlockSpec(memory_space=pl.ANY)


def nt(a, b):
    return lax.dot_general(a, b, (((1,), (1,)), ((), ())), preferred_element_type=F32)


def nn(a, b):
    return jnp.dot(a, b, preferred_element_type=F32)


def split3(x):
    a = x.astype(BF16).astype(F32)
    b = (x - a).astype(BF16).astype(F32)
    return a, b, (x - a - b).astype(BF16).astype(F32)


def send_kernel(dest_ref, floe_ref, rows_ref, out_ref, place_v, ids_v, place_s, sem):
    upper = (
        lax.broadcasted_iota(I32, (128, 128), 0) < lax.broadcasted_iota(I32, (128, 128), 1)
    ).astype(F32).astype(BF16)
    ones = jnp.ones((128, 128), BF16)
    index = lax.broadcasted_iota(I32, (128, 128), 0)
    carry = jnp.zeros((128, 128), F32)
    ids = jnp.zeros((128, 128), F32)
    for blk in range(dest_ref.shape[0]):
        dest = dest_ref[blk : blk + 1, :]
        floe = floe_ref[blk : blk + 1, :] + 1
        hot = (index == dest).astype(F32)
        hot16 = hot.astype(BF16)
        rank = jnp.sum(hot * (nn(hot16, upper) + carry), axis=0, keepdims=True)
        carry = carry + nn(hot16, ones)
        rank = rank.astype(I32)
        place_v[blk : blk + 1, :] = dest * BLK + rank
        slot = (index == rank).astype(F32).astype(BF16)
        high = (floe >> 6).astype(F32)
        low = (floe & 63).astype(F32)
        ids = ids + 64.0 * nt((hot * high).astype(BF16), slot) + nt((hot * low).astype(BF16), slot)
    ids_v[...] = ids
    copy = pltpu.make_async_copy(place_v, place_s, sem)
    copy.start()

    @pl.loop(0, out_ref.shape[0] // 128)
    def _(i):
        out_ref[pl.ds(pl.multiple_of(i * 128, 128), 128), :] = jnp.zeros((128, 128), F32)

    copy.wait()

    @pl.loop(0, rows_ref.shape[0] // 16)
    def _(i):
        for j in range(16):
            r = i * 16 + j
            out_ref[pl.ds(place_s[r >> 7, r & 127], 1), :] = rows_ref[pl.ds(r, 1), :]

    @pl.loop(0, DEVS // 8)
    def _(i):
        for j in range(8):
            d = i * 8 + j
            out_ref[pl.ds(d * BLK + CAP, 1), :] = ids_v[pl.ds(d, 1), :]


def ocean_kernel(rows_ref, resp_ref, out_ref, acc_ref, ids_ref):
    groups = rows_ref.shape[0] // 384
    lane = lax.broadcasted_iota(I32, (groups, 128), 1)
    blocks = [jnp.zeros((groups, 128), F32) for _ in range(3)]
    for j in range(8):
        ids = rows_ref[pl.ds(j * BLK + CAP, groups, stride=8 * BLK), :]
        shift = (BLK * j) % 128
        if shift:
            ids = pltpu.roll(ids, shift, 1)
        for b in range(3):
            place = lane + 128 * b - BLK * j
            blocks[b] = jnp.where((place >= 0) & (place < CAP), ids, blocks[b])
    for b in range(3):
        ids_ref[b] = blocks[b]
    acc_ref[...] = jnp.zeros_like(acc_ref)
    base16 = lax.broadcasted_iota(I32, (16, 128), 0).astype(F32)
    one, zero = jnp.ones((16, 128), BF16), jnp.zeros((16, 128), BF16)

    @pl.loop(0, groups)
    def _(g):
        rows = rows_ref[pl.ds(pl.multiple_of(g * 384, 128), 384), :]
        high = rows.astype(BF16)
        low = (rows - high.astype(F32)).astype(BF16)
        both = jnp.concatenate([high, low], axis=1)
        ids = [ids_ref[b, pl.ds(g, 1), :] for b in range(3)]
        for part in range(8):
            cols = []
            for b in range(3):
                rel = jnp.broadcast_to(ids[b] - (part * 256 + 1.0), (16, 128)).astype(BF16)
                cols.append(
                    jnp.concatenate(
                        [jnp.where((base16 + 16.0 * k).astype(BF16) == rel, one, zero) for k in range(16)], axis=0
                    )
                )
            hot = jnp.concatenate(cols, axis=1)
            acc_ref[part * 256 : part * 256 + 256, :] += nn(hot, both)

    out_ref[...] = jnp.zeros_like(out_ref)
    srow = lax.broadcasted_iota(I32, (16, 128), 0)
    slane = lax.broadcasted_iota(I32, (16, 128), 1)
    pick = (((srow == 0) & (slane < NB)) | ((srow == 1) & (slane >= NB))).astype(F32).astype(BF16)
    inner = (slane >= H) & (slane < H + FY)

    @pl.loop(0, 8)
    def _(part):
        at = pl.multiple_of(part * 256, 256)
        total = acc_ref[pl.ds(at, 256), 0:128] + acc_ref[pl.ds(at, 256), 128:256]
        resp = resp_ref[pl.ds(at, 256), :]
        a, b, c = split3(total * jnp.concatenate([resp, resp], axis=1))
        force = nt(pick, a.astype(BF16)) + nt(pick, b.astype(BF16)) + nt(pick, c.astype(BF16))
        for j in range(4):
            piece = force[:, (j // 2) * 128 : (j // 2) * 128 + 128]
            piece = pltpu.roll(piece, (H - 64 * (j % 2)) % 128, 1)
            piece = jnp.where(inner, piece, 0.0)
            out_ref[:, pl.ds(pl.multiple_of((part * 4 + j + H) * 128, 128), 128)] = piece[0:8]


def put_shift(split_ref, sx, sy):
    for k, row in enumerate(split3(sx) + split3(sy)):
        split_ref[k : k + 1, :] = row


def contact_chunk(c, live, words_ref, tiles_ref, split16, hot_ref, b_ref, acc_ref):
    word = words_ref[pl.ds(c, 1), :]
    lane = lax.broadcasted_iota(I32, (1, 128), 1)
    ok = (word >= 0) & (c * 128 + lane < live)
    own = jnp.where(ok, word & 8191, -1)
    other = jnp.where(ok, (word >> 13) & 8191, -1)
    code = (word >> 28) & 7
    code9 = code + (code >= 4).astype(I32)
    step = (code9 >= 3).astype(I32) + (code9 >= 6).astype(I32)
    dirx = (step - 1).astype(F32)
    diry = (code9 - 3 * step - 1).astype(F32)
    index = lax.broadcasted_iota(I32, (128, 128), 0)

    @pl.loop(0, R // 4)
    def _(i):
        for j in range(4):
            r = i * 4 + j
            hot = jnp.where(index == own - r * 128, 1.0, jnp.where(index == other - r * 128, -1.0, 0.0))
            hot_ref[pl.ds(pl.multiple_of(r * 128, 128), 128), :] = hot.astype(BF16)

    hot = hot_ref[...]
    diff = nn(split16, hot)
    dx = (dirx - (diff[0:1] + diff[1:2] + diff[2:3])) * SC
    dy = (diry - (diff[3:4] + diff[4:5] + diff[5:6])) * SC
    px = tiles_ref[c, 2] + dx
    py = tiles_ref[c, 3] + dy
    b_ref[0] = 2.0 * px
    b_ref[1] = 2.0 * py
    b_ref[2] = -(px * px + py * py)
    force_x = jnp.zeros((8, 128), F32)
    force_y = jnp.zeros((8, 128), F32)
    back_x = jnp.zeros((8, 128), F32)
    back_y = jnp.zeros((8, 128), F32)
    for half in range(2):
        ax = [tiles_ref[c, 0, half * 64 + 8 * k : half * 64 + 8 * k + 8, :] for k in range(8)]
        ay = [tiles_ref[c, 1, half * 64 + 8 * k : half * 64 + 8 * k + 8, :] for k in range(8)]
        na = [-(x * x + y * y) for x, y in zip(ax, ay)]

        def body(i, carry):
            sums, bx_sum, by_sum = carry
            sums = list(sums)
            for j in range(4):
                w = i * 4 + j
                bx = jnp.broadcast_to(b_ref[0, pl.ds(w, 1), :], (8, 128))
                by = jnp.broadcast_to(b_ref[1, pl.ds(w, 1), :], (8, 128))
                nb = jnp.broadcast_to(b_ref[2, pl.ds(w, 1), :], (8, 128))
                weights = [jnp.exp2((ax[k] * bx + ay[k] * by) + (na[k] + nb)) for k in range(8)]
                sums = [s + t for s, t in zip(sums, weights)]
                while len(weights) > 1:
                    weights = [weights[k] + weights[k + 1] for k in range(0, len(weights), 2)]
                bx_sum = bx_sum + weights[0] * bx
                by_sum = by_sum + weights[0] * by
            return tuple(sums), bx_sum, by_sum

        sums, back_x, back_y = lax.fori_loop(
            0, TILE // 4, body, (tuple(jnp.zeros((8, 128), F32) for _ in range(8)), back_x, back_y)
        )
        for k in range(8):
            force_x = force_x + ax[k] * sums[k]
            force_y = force_y + ay[k] * sums[k]
    fx = jnp.sum(force_x - 0.5 * back_x, axis=0, keepdims=True) * (1.0 / SC)
    fy = jnp.sum(force_y - 0.5 * back_y, axis=0, keepdims=True) * (1.0 / SC)
    parts = split3(jnp.where(ok, fx, 0.0)) + split3(jnp.where(ok, fy, 0.0))
    srow = lax.broadcasted_iota(I32, (16, 128), 0)
    stacked = jnp.zeros((16, 128), F32)
    for k, row in enumerate(parts):
        stacked = jnp.where(srow == k, jnp.broadcast_to(row, (16, 128)), stacked)
    acc_ref[...] += nt(stacked.astype(BF16), hot)


def chunks(n):
    return (n + 127) >> 7


def acc_rows(acc_ref):
    ax = acc_ref[0:1, :] + acc_ref[1:2, :] + acc_ref[2:3, :]
    ay = acc_ref[3:4, :] + acc_ref[4:5, :] + acc_ref[5:6, :]
    return ax, ay


def first_kernel(
    info_ref, lists_ref, state_ref, outline_ref, north_ref, south_ref, west_ref, east_ref,
    tiles_out, words_out, count_out, force_out,
    table, tiles, stage, raw_v, raw_s, words_s, hot_ref, b_ref, split_ref, acc_ref, sems, tile_sems,
):
    copies = []
    for q in range(4):
        lanes = slice(q * 128, q * 128 + 128)
        for k, (source, target) in enumerate((
            (outline_ref, table.at[q, H : H + FX, 8 : 8 + FY, :]),
            (north_ref, table.at[q, 0:H, 8 : 8 + FY, :]),
            (south_ref, table.at[q, H + FX : R, 8 : 8 + FY, :]),
            (west_ref, table.at[q, :, 0:8, :]),
            (east_ref, table.at[q, :, 8 + FY : 16 + FY, :]),
        )):
            copies.append(pltpu.make_async_copy(source.at[:, :, lanes], target, sems.at[5 * q + k]))
    for copy in copies:
        copy.start()
    row0 = info_ref[0]
    col0 = info_ref[1]
    rows_all = info_ref[2]
    cols_all = info_ref[3]
    slot = lax.broadcasted_iota(I32, (1, PMAX), 1)
    for k, (di, dj) in enumerate(NEIGH):
        local = lists_ref[4 * k : 4 * k + 1, :].astype(I32)
        code = lists_ref[4 * k + 1 : 4 * k + 2, :].astype(I32)
        mine = lists_ref[4 * k + 2 : 4 * k + 3, :].astype(I32)
        theirs = lists_ref[4 * k + 3 : 4 * k + 4, :].astype(I32)
        code9 = code + (code >= 4).astype(I32)
        step = (code9 >= 3).astype(I32) + (code9 >= 6).astype(I32)
        row = (local >> 6) + di * FX
        col = (local & 63) + dj * FY
        prow = row + step - 1
        pcol = col + code9 - 3 * step - 1
        ok = (slot < info_ref[4 + k]) & (prow + row0 >= 0) & (prow + row0 < rows_all)
        ok = ok & (pcol + col0 >= 0) & (pcol + col0 < cols_all)
        if k:
            near = (row >= -1) & (row <= FX) & (col >= -1) & (col <= FY)
            pnear = (prow >= -1) & (prow <= FX) & (pcol >= -1) & (pcol <= FY)
            ok = ok & (near | pnear)
        word = (row + H) * 128 + col + H + (((prow + H) * 128 + pcol + H) << 13)
        word = word + (mine << 26) + (theirs << 27) + (code << 28)
        word = jnp.where(ok, word, -1)
        for b in range(4):
            raw_v[4 * k + b : 4 * k + b + 1, :] = word[:, 128 * b : 128 * b + 128]
    copy = pltpu.make_async_copy(raw_v, raw_s, sems.at[20])
    copy.start()
    copy.wait()

    def scan_list(k, n):
        def scan(i, n):
            for j in range(8):
                at = i * 8 + j
                word = raw_s[k * 4 + (at >> 7), at & 127]
                words_s[n >> 7, n & 127] = word
                n = n + (word >= 0).astype(I32)
            return n

        return lax.fori_loop(0, (info_ref[4 + k] + 7) >> 3, scan, n)

    mine = scan_list(0, jnp.int32(0))
    total = lax.fori_loop(1, NLIST, scan_list, mine)

    def blank(i, carry):
        words_s[i >> 7, i & 127] = jnp.int32(-1)
        return carry

    lax.fori_loop(total, chunks(total + 1) * 128, blank, 0)
    count_out[0] = total
    count_out[1] = mine
    copy = pltpu.make_async_copy(words_s, words_out, sems.at[20])
    copy.start()
    for piece in copies:
        piece.wait()

    @pl.loop(0, chunks(total))
    def _(c):
        @pl.loop(0, 16)
        def _(i):
            for j in range(8):
                at = i * 8 + j
                word = jnp.maximum(words_s[c, at], 0)
                own = word & 8191
                other = (word >> 13) & 8191
                mine = (word >> 26) & 1
                theirs = (word >> 27) & 1
                orow, ocol = own >> 7, (own & 127) + PADC
                prow, pcol = other >> 7, (other & 127) + PADC
                stage[0, pl.ds(at, 1), :] = table[mine, orow, pl.ds(ocol, 1), :]
                stage[1, pl.ds(at, 1), :] = table[mine + 2, orow, pl.ds(ocol, 1), :]
                stage[2, pl.ds(at, 1), :] = table[theirs, prow, pl.ds(pcol, 1), :]
                stage[3, pl.ds(at, 1), :] = table[theirs + 2, prow, pl.ds(pcol, 1), :]

        for k in range(4):
            tiles[c, k] = jnp.transpose(stage[k]) * SC
        pltpu.make_async_copy(tiles.at[c], tiles_out.at[c], tile_sems.at[c]).start()

    copy.wait()
    split_ref[...] = jnp.zeros_like(split_ref)
    put_shift(split_ref, state_ref[0:1, :], state_ref[1:2, :])
    split16 = split_ref[...].astype(BF16)
    acc_ref[...] = jnp.zeros_like(acc_ref)

    @pl.loop(0, chunks(mine))
    def _(c):
        contact_chunk(c, mine, words_out, tiles, split16, hot_ref, b_ref, acc_ref)

    ax, ay = acc_rows(acc_ref)
    force_out[...] = jnp.zeros_like(force_out)
    force_out[0:1, :] = ax
    force_out[1:2, :] = ay

    @pl.loop(0, chunks(total))
    def _(c):
        pltpu.make_async_copy(tiles.at[c], tiles_out.at[c], tile_sems.at[c]).wait()


def later_kernel(
    count_ref, force_ref, state_ref, words_ref, tiles_in, vel_out, shift_out,
    tiles, hot_ref, b_ref, split_ref, acc_ref, now_ref, tile_sems,
):
    total = count_ref[0]

    @pl.loop(0, chunks(total))
    def _(c):
        pltpu.make_async_copy(tiles_in.at[c], tiles.at[c], tile_sems.at[c]).start()

    now_ref[...] = state_ref[...]

    def update(fx, fy):
        scale = DT / now_ref[4:5, :]
        vx = now_ref[2:3, :]
        vy = now_ref[3:4, :]
        vx = vx + (fx - DRAG * vx) * scale
        vy = vy + (fy - DRAG * vy) * scale
        now_ref[2:3, :] = vx
        now_ref[3:4, :] = vy
        now_ref[0:1, :] = now_ref[0:1, :] + DT * vx
        now_ref[1:2, :] = now_ref[1:2, :] + DT * vy

    update(force_ref[0:1, :], force_ref[1:2, :])
    split_ref[...] = jnp.zeros_like(split_ref)

    @pl.loop(0, chunks(total))
    def _(c):
        pltpu.make_async_copy(tiles_in.at[c], tiles.at[c], tile_sems.at[c]).wait()

    @pl.loop(1, STEPS)
    def _(step):
        put_shift(split_ref, now_ref[0:1, :], now_ref[1:2, :])
        split16 = split_ref[...].astype(BF16)
        acc_ref[...] = jnp.zeros_like(acc_ref)

        @pl.loop(0, chunks(total))
        def _(c):
            contact_chunk(c, total, words_ref, tiles, split16, hot_ref, b_ref, acc_ref)

        ax, ay = acc_rows(acc_ref)
        update(ax + force_ref[2:3, :], ay + force_ref[3:4, :])

    for out, base in ((shift_out, 0), (vel_out, 2)):
        for k in range(2):
            for r in range(FX):
                row = now_ref[base + k : base + k + 1, (r + H) * 128 : (r + H) * 128 + 128]
                out[r, k : k + 1, :] = pltpu.roll(row, 128 - H, 1)[:, 0:FY]


def moved(x, axis, up):
    count = lax.axis_size(axis)
    pairs = [(i, i + 1) if up else (i + 1, i) for i in range(count - 1)]
    return lax.ppermute(x, axis, pairs)


def as_rows(x, rows):
    flat = x.reshape(-1)
    return jnp.pad(flat, (0, rows * 512 - flat.shape[0])).reshape(rows, 512)


def shards(
    outline, centres, velocity, mass, response, pairs, pair_count, forcing, ocean_dest, ocean_floe
):
    rows_dev = forcing.shape[0]
    send = pl.pallas_call(
        send_kernel,
        out_shape=jax.ShapeDtypeStruct((DEVS * BLK, 128), F32),
        in_specs=[vspec()] * 3,
        out_specs=vspec(),
        scratch_shapes=[
            pltpu.VMEM((rows_dev // 128, 128), I32),
            pltpu.VMEM((DEVS, 128), F32),
            pltpu.SMEM((rows_dev // 128, 128), I32),
            pltpu.SemaphoreType.DMA,
        ],
        compiler_params=params(),
        cost_estimate=pl.CostEstimate(flops=100000000, bytes_accessed=4 << 20, transcendentals=0),
    )(ocean_dest.reshape(rows_dev // 128, 128), ocean_floe.reshape(rows_dev // 128, 128), forcing)
    got = lax.all_to_all(
        send.reshape(DEVS, BLK, 128), ("gx", "gy"), split_axis=0, concat_axis=0, tiled=True
    )

    state = jnp.concatenate(
        [jnp.transpose(centres, (2, 0, 1)), jnp.transpose(velocity, (2, 0, 1)), mass[None]], axis=0
    )
    lists = jnp.transpose(pairs[0, 0], (1, 0)).astype(F32)
    count = jnp.broadcast_to(pair_count.astype(F32), (1, 512))

    def pack_x(lo):
        return jnp.concatenate(
            [outline[lo : lo + H].reshape(H * FY, 512), as_rows(state[:, lo : lo + H], 2), lists, count,
             jnp.zeros((1, 512), F32)], axis=0
        )

    def unpack_x(got):
        return (
            got[: H * FY].reshape(H, FY, 512),
            got[H * FY : H * FY + 2].reshape(-1)[: 5 * H * FY].reshape(5, H, FY),
            got[H * FY + 2 : H * FY + 7],
        )

    north_o, north_s, north_l = unpack_x(moved(pack_x(FX - H), "gx", True))
    south_o, south_s, south_l = unpack_x(moved(pack_x(0), "gx", False))
    tall = jnp.concatenate([north_s, state, south_s], axis=1)
    own_l = jnp.concatenate([lists, count], axis=0)

    def pack_y(lo):
        cols = jnp.concatenate(
            [north_o[:, lo : lo + H], outline[:, lo : lo + H], south_o[:, lo : lo + H]], axis=0
        )
        return jnp.concatenate(
            [cols.reshape(R * H, 512), as_rows(tall[:, :, lo : lo + H], 1), north_l, own_l, south_l], axis=0
        )

    def unpack_y(got):
        return (
            got[: R * H].reshape(R, H, 512),
            got[R * H].reshape(-1)[: 5 * R * H].reshape(5, R, H),
            got[R * H + 1 : R * H + 16],
        )

    west_o, west_s, west_l = unpack_y(moved(pack_y(FY - H), "gy", True))
    east_o, east_s, east_l = unpack_y(moved(pack_y(0), "gy", False))
    west_o = jnp.pad(west_o, ((0, 0), (8 - H, 0), (0, 0)))
    east_o = jnp.pad(east_o, ((0, 0), (0, 8 - H), (0, 0)))
    wide = jnp.concatenate([west_s, tall, east_s], axis=2)
    wide = jnp.pad(wide, ((0, 0), (0, 0), (0, 128 - FY - 2 * H)))
    weight = jnp.where(wide[4:5] == 0.0, 1.0, wide[4:5])
    wide = jnp.concatenate([wide[:4], weight, jnp.zeros((3, R, 128), F32)], axis=0).reshape(8, NF)

    every = [own_l, north_l, south_l] + [
        block[5 * k : 5 * k + 5] for block in (west_l, east_l) for k in (0, 1, 2)
    ]
    lists36 = jnp.concatenate([block[:4] for block in every], axis=0)
    gx, gy = lax.axis_index("gx"), lax.axis_index("gy")
    info = jnp.concatenate(
        [
            jnp.stack([gx * FX, gy * FY, lax.axis_size("gx") * FX, lax.axis_size("gy") * FY]).astype(I32),
            jnp.stack([block[4, 0] for block in every]).astype(I32),
            jnp.zeros((3,), I32),
        ]
    )
    chunk_scratch = [
        pltpu.VMEM((NF, 128), BF16),
        pltpu.VMEM((3, 128, 128), F32),
        pltpu.VMEM((16, NF), F32),
        pltpu.VMEM((16, NF), F32),
    ]
    tiles, words, counts, contact = pl.pallas_call(
        first_kernel,
        out_shape=[
            jax.ShapeDtypeStruct((NCH, 4, 128, 128), F32),
            jax.ShapeDtypeStruct((NCH + 1, 128), I32),
            jax.ShapeDtypeStruct((2,), I32),
            jax.ShapeDtypeStruct((8, NF), F32),
        ],
        in_specs=[sspec(), vspec(), vspec()] + [aspec()] * 5,
        out_specs=[aspec(), vspec(), sspec(), vspec()],
        scratch_shapes=[
            pltpu.VMEM((4, R, TW, 128), F32),
            pltpu.VMEM((NCH, 4, 128, 128), F32),
            pltpu.VMEM((4, 128, 128), F32),
            pltpu.VMEM((NCH, 128), I32),
            pltpu.SMEM((NCH, 128), I32),
            pltpu.SMEM((NCH + 1, 128), I32),
            *chunk_scratch,
            pltpu.SemaphoreType.DMA((21,)),
            pltpu.SemaphoreType.DMA((NCH,)),
        ],
        compiler_params=params(),
        cost_estimate=pl.CostEstimate(flops=500000000, bytes_accessed=8 << 20, transcendentals=8 << 20),
    )(info, lists36, wide, outline, north_o, south_o, west_o, east_o)

    ocean = pl.pallas_call(
        ocean_kernel,
        out_shape=jax.ShapeDtypeStruct((8, NF), F32),
        in_specs=[vspec()] * 2,
        out_specs=vspec(),
        scratch_shapes=[
            pltpu.VMEM((FX * FY, 256), F32),
            pltpu.VMEM((3, DEVS * BLK // 384, 128), F32),
        ],
        compiler_params=params(),
        cost_estimate=pl.CostEstimate(flops=5000000000, bytes_accessed=5 << 20, transcendentals=0),
    )(got.reshape(DEVS * BLK, 128), response.reshape(FX * FY, NB))

    force = jnp.concatenate([contact[:2] + ocean[:2], ocean[:2]], axis=0).reshape(4, R, 128)
    w = 2 * H - 1
    low, high = moved(force[:, FX : FX + w], "gx", True), moved(force[:, 1 : 1 + w], "gx", False)
    force = force + jnp.pad(low, ((0, 0), (0, R - w), (0, 0))) + jnp.pad(high, ((0, 0), (R - w, 0), (0, 0)))
    low, high = moved(force[:, :, FY : FY + w], "gy", True), moved(force[:, :, 1 : 1 + w], "gy", False)
    c = FY + 2 * H
    force = force + jnp.pad(low, ((0, 0), (0, 0), (0, 128 - w))) + jnp.pad(high, ((0, 0), (0, 0), (c - w, 128 - c)))
    force = jnp.pad(force.reshape(4, NF), ((0, 4), (0, 0)))

    vel, shift = pl.pallas_call(
        later_kernel,
        out_shape=[jax.ShapeDtypeStruct((FX, 2, FY), F32)] * 2,
        in_specs=[sspec(), vspec(), vspec(), vspec(), aspec()],
        out_specs=[vspec()] * 2,
        scratch_shapes=[
            pltpu.VMEM((NCH, 4, 128, 128), F32),
            *chunk_scratch,
            pltpu.VMEM((8, NF), F32),
            pltpu.SemaphoreType.DMA((NCH,)),
        ],
        compiler_params=params(),
        cost_estimate=pl.CostEstimate(flops=500000000, bytes_accessed=4 << 20, transcendentals=16 << 20),
    )(counts, force, wide, words, tiles)
    return jnp.transpose(vel, (0, 2, 1)), jnp.transpose(shift, (0, 2, 1))


def solution(mesh):
    return jax.shard_map(
        shards,
        mesh=mesh,
        in_specs=(
            P("gx", "gy", None),
            P("gx", "gy", None),
            P("gx", "gy", None),
            P("gx", "gy"),
            P("gx", "gy", None),
            P("gx", "gy", None, None),
            P("gx", "gy"),
            P(("gx", "gy"), None),
            P(("gx", "gy"), None),
            P(("gx", "gy")),
        ),
        out_specs=(P("gx", "gy", None), P("gx", "gy", None)),
        check_vma=False,
    )
```

```python
import math

import jax
import jax.numpy as jnp
from jax import lax
from jax.experimental import pallas as pl
from jax.experimental.pallas import tpu as pltpu
from jax.sharding import PartitionSpec as P

FX, FY, V, TILE, NB, PMAX = 32, 64, 256, 128, 64, 512
DEVS, CAP, BLK = 128, 40, 48
STEPS = 3
DT, DRAG = 0.1, 0.5
H = 2
R = FX + 2 * H
RP = 40
TW = FY + 16
PADC = 8 - H
NCH = 9 * PMAX // 128
NEIGH = ((-1, 0), (1, 0), (-1, -1), (0, -1), (1, -1), (-1, 1), (0, 1), (1, 1))
SC = math.sqrt(100.0 * math.log2(math.e))
F32, BF16, I32 = jnp.float32, jnp.bfloat16, jnp.int32
VMEM_BYTES = 52 * 1024 * 1024


def params():
    return pltpu.CompilerParams(vmem_limit_bytes=VMEM_BYTES)


def vspec():
    return pl.BlockSpec(memory_space=pltpu.VMEM)


def sspec():
    return pl.BlockSpec(memory_space=pltpu.SMEM)


def aspec():
    return pl.BlockSpec(memory_space=pl.ANY)


def nt(a, b):
    return lax.dot_general(a, b, (((1,), (1,)), ((), ())), preferred_element_type=F32)


def nn(a, b):
    return jnp.dot(a, b, preferred_element_type=F32)


def split3(x):
    a = x.astype(BF16).astype(F32)
    b = (x - a).astype(BF16).astype(F32)
    return a, b, (x - a - b).astype(BF16).astype(F32)


def send_kernel(dest_ref, floe_ref, rows_ref, out_ref, place_v, ids_v, place_s, sem):
    upper = (
        lax.broadcasted_iota(I32, (128, 128), 0) < lax.broadcasted_iota(I32, (128, 128), 1)
    ).astype(F32).astype(BF16)
    ones = jnp.ones((128, 128), BF16)
    index = lax.broadcasted_iota(I32, (128, 128), 0)
    blocks = dest_ref.shape[0]
    hots = [(index == dest_ref[k : k + 1, :]).astype(F32) for k in range(blocks)]
    hot16 = jnp.concatenate([hot.astype(BF16) for hot in hots], axis=0)
    before = nn(hot16, upper)
    full = nn(hot16, ones)
    carry = jnp.zeros((128, 128), F32)
    high, low, slots = [], [], []
    for k in range(blocks):
        rank = jnp.sum(hots[k] * (before[128 * k : 128 * k + 128] + carry), axis=0, keepdims=True)
        carry = carry + full[128 * k : 128 * k + 128]
        rank = rank.astype(I32)
        place_v[k : k + 1, :] = dest_ref[k : k + 1, :] * BLK + rank
        floe = floe_ref[k : k + 1, :] + 1
        slots.append((index == rank).astype(F32).astype(BF16))
        high.append((hots[k] * (floe >> 6).astype(F32)).astype(BF16))
        low.append((hots[k] * (floe & 63).astype(F32)).astype(BF16))
    slots = jnp.concatenate(slots, axis=1)
    ids = 64.0 * nt(jnp.concatenate(high, axis=1), slots) + nt(jnp.concatenate(low, axis=1), slots)
    ids_v[...] = ids
    copy = pltpu.make_async_copy(place_v, place_s, sem)
    copy.start()

    @pl.loop(0, out_ref.shape[0] // 128)
    def _(i):
        out_ref[pl.ds(pl.multiple_of(i * 128, 128), 128), :] = jnp.zeros((128, 128), F32)

    copy.wait()

    @pl.loop(0, rows_ref.shape[0] // 16)
    def _(i):
        for j in range(16):
            r = i * 16 + j
            out_ref[pl.ds(place_s[r >> 7, r & 127], 1), :] = rows_ref[pl.ds(r, 1), :]

    @pl.loop(0, DEVS // 8)
    def _(i):
        for j in range(8):
            d = i * 8 + j
            out_ref[pl.ds(d * BLK + CAP, 1), :] = ids_v[pl.ds(d, 1), :]


def ocean_kernel(rows_ref, resp_ref, out_ref, acc_ref, ids_ref):
    groups = rows_ref.shape[0] // 384
    lane = lax.broadcasted_iota(I32, (groups, 128), 1)
    blocks = [jnp.zeros((groups, 128), F32) for _ in range(3)]
    for j in range(8):
        ids = rows_ref[pl.ds(j * BLK + CAP, groups, stride=8 * BLK), :]
        shift = (BLK * j) % 128
        if shift:
            ids = pltpu.roll(ids, shift, 1)
        for b in range(3):
            place = lane + 128 * b - BLK * j
            blocks[b] = jnp.where((place >= 0) & (place < CAP), ids, blocks[b])
    for b in range(3):
        ids_ref[b] = blocks[b]
    acc_ref[...] = jnp.zeros_like(acc_ref)
    base16 = lax.broadcasted_iota(I32, (16, 128), 0).astype(F32)
    one, zero = jnp.ones((16, 128), BF16), jnp.zeros((16, 128), BF16)

    @pl.loop(0, groups // 2)
    def _(g):
        rows = rows_ref[pl.ds(pl.multiple_of(g * 768, 128), 768), :]
        high = rows.astype(BF16)
        low = (rows - high.astype(F32)).astype(BF16)
        both = jnp.concatenate([high, low], axis=1)
        ids = [ids_ref[b, pl.ds(2 * g + h, 1), :] for h in range(2) for b in range(3)]
        for part in range(8):
            cols = []
            for b in range(6):
                rel = jnp.broadcast_to(ids[b] - (part * 256 + 1.0), (16, 128)).astype(BF16)
                cols.append(
                    jnp.concatenate(
                        [jnp.where((base16 + 16.0 * k).astype(BF16) == rel, one, zero) for k in range(16)], axis=0
                    )
                )
            hot = jnp.concatenate(cols, axis=1)
            acc_ref[part * 256 : part * 256 + 256, :] += nn(hot, both)

    out_ref[...] = jnp.zeros_like(out_ref)
    srow = lax.broadcasted_iota(I32, (16, 128), 0)
    slane = lax.broadcasted_iota(I32, (16, 128), 1)
    pick = (((srow == 0) & (slane < NB)) | ((srow == 1) & (slane >= NB))).astype(F32).astype(BF16)
    inner = (slane >= H) & (slane < H + FY)

    @pl.loop(0, 8)
    def _(part):
        at = pl.multiple_of(part * 256, 256)
        total = acc_ref[pl.ds(at, 256), 0:128] + acc_ref[pl.ds(at, 256), 128:256]
        resp = resp_ref[pl.ds(at, 256), :]
        a, b, c = split3(total * jnp.concatenate([resp, resp], axis=1))
        force = nt(pick, a.astype(BF16)) + nt(pick, b.astype(BF16)) + nt(pick, c.astype(BF16))
        for j in range(4):
            piece = force[:, (j // 2) * 128 : (j // 2) * 128 + 128]
            piece = pltpu.roll(piece, (H - 64 * (j % 2)) % 128, 1)
            piece = jnp.where(inner, piece, 0.0)
            for k in range(2):
                out_ref[k, pl.ds(part * 4 + j + H, 1), :] = piece[k : k + 1]


def put_shift(left_ref, plane_ref, now_ref):
    for k in range(2):
        plane_ref[0:R, :] = now_ref[k]
        for j, part in enumerate(split3(jnp.transpose(plane_ref[...]))):
            at = (3 * k + j) * 128
            left_ref[at : at + 128, :] = part.astype(BF16)


def contact_chunk(c, words_ref, tiles_ref, left_ref, b_ref, acc_ref):
    word = words_ref[pl.ds(c, 1), :]
    ok = word >= 0
    rows = jnp.concatenate([(word >> 7) & 63, (word >> 20) & 63], axis=1)
    cols = jnp.concatenate([word & 127, (word >> 13) & 127], axis=1)
    code = (word >> 28) & 7
    code9 = code + (code >= 4).astype(I32)
    step = (code9 >= 3).astype(I32) + (code9 >= 6).astype(I32)
    dirx = (step - 1).astype(F32)
    diry = (code9 - 3 * step - 1).astype(F32)
    index = lax.broadcasted_iota(I32, (128, 256), 0)
    row_hot = (index == rows).astype(F32)
    row_hot16 = row_hot.astype(BF16)
    col_hot = index == cols
    diffs = []
    for k in range(2):
        part = nn(left_ref[384 * k : 384 * k + 384, :], row_hot16)
        part = part[0:128] + part[128:256] + part[256:384]
        part = jnp.sum(jnp.where(col_hot, part, 0.0), axis=0, keepdims=True)
        diffs.append(part[:, 0:128] - part[:, 128:256])
    dx = (dirx - diffs[0]) * SC
    dy = (diry - diffs[1]) * SC
    px = tiles_ref[c, 2] + dx
    py = tiles_ref[c, 3] + dy
    b_ref[0] = 2.0 * px
    b_ref[1] = 2.0 * py
    b_ref[2] = -(px * px + py * py)
    force_x = jnp.zeros((8, 128), F32)
    force_y = jnp.zeros((8, 128), F32)
    back_x = jnp.zeros((8, 128), F32)
    back_y = jnp.zeros((8, 128), F32)
    for half in range(2):
        ax = [tiles_ref[c, 0, half * 64 + 8 * k : half * 64 + 8 * k + 8, :] for k in range(8)]
        ay = [tiles_ref[c, 1, half * 64 + 8 * k : half * 64 + 8 * k + 8, :] for k in range(8)]
        na = [-(x * x + y * y) for x, y in zip(ax, ay)]

        def body(i, carry):
            sums, bx_sum, by_sum = carry
            sums = list(sums)
            for j in range(8):
                w = i * 8 + j
                bx = jnp.broadcast_to(b_ref[0, pl.ds(w, 1), :], (8, 128))
                by = jnp.broadcast_to(b_ref[1, pl.ds(w, 1), :], (8, 128))
                nb = jnp.broadcast_to(b_ref[2, pl.ds(w, 1), :], (8, 128))
                weights = [jnp.exp2((ax[k] * bx + ay[k] * by) + (na[k] + nb)) for k in range(8)]
                sums = [s + t for s, t in zip(sums, weights)]
                while len(weights) > 1:
                    weights = [weights[k] + weights[k + 1] for k in range(0, len(weights), 2)]
                bx_sum = bx_sum + weights[0] * bx
                by_sum = by_sum + weights[0] * by
            return tuple(sums), bx_sum, by_sum

        sums, back_x, back_y = lax.fori_loop(
            0, TILE // 8, body, (tuple(jnp.zeros((8, 128), F32) for _ in range(8)), back_x, back_y)
        )
        for k in range(8):
            force_x = force_x + ax[k] * sums[k]
            force_y = force_y + ay[k] * sums[k]
    fx = jnp.sum(force_x - 0.5 * back_x, axis=0, keepdims=True) * (1.0 / SC)
    fy = jnp.sum(force_y - 0.5 * back_y, axis=0, keepdims=True) * (1.0 / SC)
    parts = split3(jnp.where(ok, fx, 0.0)) + split3(jnp.where(ok, fy, 0.0))
    spread = [row_hot[0:RP] * jnp.concatenate([part, -part], axis=1) for part in parts]
    acc_ref[...] += nt(jnp.concatenate(spread, axis=0).astype(BF16), col_hot.astype(F32).astype(BF16))


def acc_plane(acc_ref, k):
    at = 3 * RP * k
    return acc_ref[at : at + R, :] + acc_ref[at + RP : at + RP + R, :] + acc_ref[at + 2 * RP : at + 2 * RP + R, :]


def code_steps(code):
    code9 = code + (code >= 4).astype(I32)
    step = (code9 >= 3).astype(I32) + (code9 >= 6).astype(I32)
    return step - 1, code9 - 3 * step - 1


def pair_words(local, code, mine, theirs, count, di, dj, extra):
    step_x, step_y = code_steps(code)
    row = (local >> 6) + di * FX
    col = (local & 63) + dj * FY
    prow = row + step_x
    pcol = col + step_y
    row_all = prow + lax.axis_index("gx") * FX
    col_all = pcol + lax.axis_index("gy") * FY
    ok = lax.broadcasted_iota(I32, local.shape, 1) < count
    ok = ok & (row_all >= 0) & (row_all < lax.axis_size("gx") * FX)
    ok = ok & (col_all >= 0) & (col_all < lax.axis_size("gy") * FY)
    if extra:
        near = (row >= -1) & (row <= FX) & (col >= -1) & (col <= FY)
        ok = ok & (near | ((prow >= -1) & (prow <= FX) & (pcol >= -1) & (pcol <= FY)))
    word = (row + H) * 128 + col + H + (((prow + H) * 128 + pcol + H) << 13)
    return jnp.where(ok, word + (mine << 26) + (theirs << 27) + (code << 28), -1)


def first_kernel(
    count_ref, own_ref, lists_ref, state_ref, outline_ref, north_ref, south_ref, west_ref, east_ref,
    tiles_out, words_out, count_out, force_out,
    table, tiles, stage, place_v, place_s, left_ref, plane_ref, b_ref, acc_ref, sems, tile_sems,
):
    copies = []
    for q in range(4):
        lanes = slice(q * 128, q * 128 + 128)
        for k, (source, target) in enumerate((
            (outline_ref, table.at[q, H : H + FX, 8 : 8 + FY, :]),
            (north_ref, table.at[q, 0:H, 8 : 8 + FY, :]),
            (south_ref, table.at[q, H + FX : R, 8 : 8 + FY, :]),
            (west_ref, table.at[q, :, 0:8, :]),
            (east_ref, table.at[q, :, 8 + FY : 16 + FY, :]),
        )):
            copies.append(pltpu.make_async_copy(source.at[:, :, lanes], target, sems.at[5 * q + k]))
    for copy in copies:
        copy.start()
    live = count_ref[0, 0]
    word = pair_words(*[own_ref[k : k + 1, :] for k in range(4)], live, 0, 0, False)
    words_out[...] = jnp.full(words_out.shape, -1, I32)
    for b in range(4):
        words_out[b : b + 1, :] = word[:, 128 * b : 128 * b + 128]
    mine = (live + 127) >> 7
    number = lax.broadcasted_iota(I32, (8, PMAX), 0)
    di, dj = jnp.zeros((8, PMAX), I32), jnp.zeros((8, PMAX), I32)
    for k, (i, j) in enumerate(NEIGH):
        di = jnp.where(number == k, i, di)
        dj = jnp.where(number == k, j, dj)
    word = pair_words(*[lists_ref[k].astype(I32) for k in range(5)], di, dj, True)
    flags = (word >= 0).astype(F32)
    upper = (
        lax.broadcasted_iota(I32, (PMAX, PMAX), 0) < lax.broadcasted_iota(I32, (PMAX, PMAX), 1)
    ).astype(F32).astype(BF16)
    rank = nn(flags.astype(BF16), upper)
    base = jnp.zeros((1, 1), F32)
    ranks = []
    for k in range(8):
        ranks.append(jnp.where(flags[k : k + 1] > 0.0, rank[k : k + 1] + base, -1.0).astype(I32))
        base = base + jnp.sum(flags[k : k + 1], axis=1, keepdims=True)
    extra = (jnp.sum(flags).astype(I32) + 127) >> 7
    total = mine + extra
    slot = lax.broadcasted_iota(I32, (128, PMAX), 0)
    srow = lax.broadcasted_iota(I32, (16, PMAX), 0)
    pieces = []
    for k in range(8):
        one = word[k : k + 1]
        piece = jnp.where(srow == 0, one & 255, jnp.where(srow == 1, (one >> 8) & 255, 0))
        piece = jnp.where(srow == 2, (one >> 16) & 255, jnp.where(srow == 3, (one >> 24) & 127, piece))
        piece = jnp.where(srow == 4, 1, piece)
        pieces.append(piece.astype(F32).astype(BF16))

    @pl.loop(0, extra)
    def _(i):
        found = jnp.zeros((16, 128), F32)
        for k in range(8):
            found = found + nt(pieces[k], (slot == ranks[k] - i * 128).astype(F32).astype(BF16))
        found = found.astype(I32)
        value = found[0:1] + (found[1:2] << 8) + (found[2:3] << 16) + (found[3:4] << 24)
        words_out[pl.ds(mine + i, 1), :] = jnp.where(found[4:5] > 0, value, -1)

    word = jnp.maximum(words_out[...], 0)
    own = ((word >> 7) & 63) * TW + (word & 127) + PADC
    other = ((word >> 20) & 63) * TW + ((word >> 13) & 127) + PADC
    place_v[0] = own + ((word >> 26) & 1) * (R * TW)
    place_v[1] = other + ((word >> 27) & 1) * (R * TW)
    copy = pltpu.make_async_copy(place_v, place_s, sems.at[20])
    copy.start()
    count_out[0] = total
    for piece in copies:
        piece.wait()
    copy.wait()
    flat = table.reshape(4 * R * TW, 128)

    @pl.loop(0, total)
    def _(c):
        @pl.loop(0, 16)
        def _(i):
            for j in range(8):
                at = i * 8 + j
                own = place_s[0, c, at]
                other = place_s[1, c, at]
                stage[0, pl.ds(at, 1), :] = flat[pl.ds(own, 1), :]
                stage[1, pl.ds(at, 1), :] = flat[pl.ds(own + 2 * R * TW, 1), :]
                stage[2, pl.ds(at, 1), :] = flat[pl.ds(other, 1), :]
                stage[3, pl.ds(at, 1), :] = flat[pl.ds(other + 2 * R * TW, 1), :]

        for k in range(4):
            tiles[c, k] = jnp.transpose(stage[k]) * SC
        pltpu.make_async_copy(tiles.at[c], tiles_out.at[c], tile_sems.at[c]).start()

    plane_ref[...] = jnp.zeros_like(plane_ref)
    put_shift(left_ref, plane_ref, state_ref)
    acc_ref[...] = jnp.zeros_like(acc_ref)

    @pl.loop(0, mine)
    def _(c):
        contact_chunk(c, words_out, tiles, left_ref, b_ref, acc_ref)

    for k in range(2):
        force_out[k] = acc_plane(acc_ref, k)

    @pl.loop(0, total)
    def _(c):
        pltpu.make_async_copy(tiles.at[c], tiles_out.at[c], tile_sems.at[c]).wait()


def later_kernel(
    count_ref, force_ref, state_ref, words_ref, tiles_in, vel_out, shift_out,
    tiles, left_ref, plane_ref, b_ref, acc_ref, now_ref, tile_sems,
):
    total = count_ref[0]

    @pl.loop(0, total)
    def _(c):
        pltpu.make_async_copy(tiles_in.at[c], tiles.at[c], tile_sems.at[c]).start()

    now_ref[...] = state_ref[...]

    def update(forces):
        scale = DT / now_ref[4]
        for k in range(2):
            vel = now_ref[2 + k]
            vel = vel + (forces[k] - DRAG * vel) * scale
            now_ref[2 + k] = vel
            now_ref[k] = now_ref[k] + DT * vel

    update([force_ref[0], force_ref[1]])
    plane_ref[...] = jnp.zeros_like(plane_ref)

    @pl.loop(0, total)
    def _(c):
        pltpu.make_async_copy(tiles_in.at[c], tiles.at[c], tile_sems.at[c]).wait()

    @pl.loop(1, STEPS)
    def _(step):
        put_shift(left_ref, plane_ref, now_ref)
        acc_ref[...] = jnp.zeros_like(acc_ref)

        @pl.loop(0, total)
        def _(c):
            contact_chunk(c, words_ref, tiles, left_ref, b_ref, acc_ref)

        update([acc_plane(acc_ref, k) + force_ref[2 + k] for k in range(2)])

    for out, base in ((shift_out, 0), (vel_out, 2)):
        for k in range(2):
            plane_ref[0:R, :] = pltpu.roll(now_ref[base + k], 128 - H, 1)
            for r in range(FX):
                out[r, k : k + 1, :] = plane_ref[r + H : r + H + 1, 0:FY]


def moved(x, axis, up):
    count = lax.axis_size(axis)
    pairs = [(i, i + 1) if up else (i + 1, i) for i in range(count - 1)]
    return lax.ppermute(x, axis, pairs)


def as_rows(x, rows):
    flat = x.reshape(-1)
    return jnp.pad(flat, (0, rows * 512 - flat.shape[0])).reshape(rows, 512)


def shards(
    outline, centres, velocity, mass, response, pairs, pair_count, forcing, ocean_dest, ocean_floe
):
    rows_dev = forcing.shape[0]
    send = pl.pallas_call(
        send_kernel,
        name="send_rows",
        out_shape=jax.ShapeDtypeStruct((DEVS * BLK, 128), F32),
        in_specs=[vspec()] * 3,
        out_specs=vspec(),
        scratch_shapes=[
            pltpu.VMEM((rows_dev // 128, 128), I32),
            pltpu.VMEM((DEVS, 128), F32),
            pltpu.SMEM((rows_dev // 128, 128), I32),
            pltpu.SemaphoreType.DMA,
        ],
        compiler_params=params(),
        cost_estimate=pl.CostEstimate(flops=100000000, bytes_accessed=4 << 20, transcendentals=0),
    )(ocean_dest.reshape(rows_dev // 128, 128), ocean_floe.reshape(rows_dev // 128, 128), forcing)
    state = jnp.concatenate(
        [jnp.transpose(centres, (2, 0, 1)), jnp.transpose(velocity, (2, 0, 1)), mass[None]], axis=0
    )
    lists = jnp.transpose(pairs[0, 0], (1, 0)).astype(F32)
    count = jnp.broadcast_to(pair_count.astype(F32), (1, 512))

    def pack_x(lo):
        return jnp.concatenate(
            [outline[lo : lo + H].reshape(H * FY, 512), as_rows(state[:, lo : lo + H], 2), lists, count,
             jnp.zeros((1, 512), F32)], axis=0
        )

    def unpack_x(got):
        return (
            got[: H * FY].reshape(H, FY, 512),
            got[H * FY : H * FY + 2].reshape(-1)[: 5 * H * FY].reshape(5, H, FY),
            got[H * FY + 2 : H * FY + 7],
        )

    north_o, north_s, north_l = unpack_x(moved(pack_x(FX - H), "gx", True))
    south_o, south_s, south_l = unpack_x(moved(pack_x(0), "gx", False))
    tall = jnp.concatenate([north_s, state, south_s], axis=1)
    own_l = jnp.concatenate([lists, count], axis=0)

    def pack_y(lo):
        cols = jnp.concatenate(
            [north_o[:, lo : lo + H], outline[:, lo : lo + H], south_o[:, lo : lo + H]], axis=0
        )
        return jnp.concatenate(
            [cols.reshape(R * H, 512), as_rows(tall[:, :, lo : lo + H], 1), north_l, own_l, south_l], axis=0
        )

    def unpack_y(got):
        return (
            got[: R * H].reshape(R, H, 512),
            got[R * H].reshape(-1)[: 5 * R * H].reshape(5, R, H),
            got[R * H + 1 : R * H + 16],
        )

    west, east, send = lax.optimization_barrier(
        (moved(pack_y(FY - H), "gy", True), moved(pack_y(0), "gy", False), send)
    )
    got = lax.all_to_all(
        send.reshape(DEVS, BLK, 128), ("gx", "gy"), split_axis=0, concat_axis=0, tiled=True
    )
    west_o, west_s, west_l = unpack_y(west)
    east_o, east_s, east_l = unpack_y(east)
    west_o = jnp.pad(west_o, ((0, 0), (8 - H, 0), (0, 0)))
    east_o = jnp.pad(east_o, ((0, 0), (0, 8 - H), (0, 0)))
    wide = jnp.concatenate([west_s, tall, east_s], axis=2)
    wide = jnp.pad(wide, ((0, 0), (0, 0), (0, 128 - FY - 2 * H)))
    weight = jnp.where(wide[4:5] == 0.0, 1.0, wide[4:5])
    wide = jnp.concatenate([wide[:4], weight], axis=0)
    others = [north_l, south_l] + [block[5 * k : 5 * k + 5] for block in (west_l, east_l) for k in (0, 1, 2)]
    others = jnp.stack(others, axis=1)
    chunk_scratch = [
        pltpu.VMEM((6 * 128, 128), BF16),
        pltpu.VMEM((128, 128), F32),
        pltpu.VMEM((3, 128, 128), F32),
        pltpu.VMEM((6 * RP, 128), F32),
    ]
    tiles, words, counts, contact = pl.pallas_call(
        first_kernel,
        out_shape=[
            jax.ShapeDtypeStruct((NCH, 4, 128, 128), F32),
            jax.ShapeDtypeStruct((NCH, 128), I32),
            jax.ShapeDtypeStruct((1,), I32),
            jax.ShapeDtypeStruct((2, R, 128), F32),
        ],
        in_specs=[sspec(), vspec(), vspec(), vspec()] + [aspec()] * 5,
        out_specs=[aspec(), vspec(), sspec(), vspec()],
        scratch_shapes=[
            pltpu.VMEM((4, R, TW, 128), F32),
            pltpu.VMEM((NCH, 4, 128, 128), F32),
            pltpu.VMEM((4, 128, 128), F32),
            pltpu.VMEM((2, NCH, 128), I32),
            pltpu.SMEM((2, NCH, 128), I32),
            *chunk_scratch,
            pltpu.SemaphoreType.DMA((21,)),
            pltpu.SemaphoreType.DMA((NCH,)),
        ],
        compiler_params=params(),
        name="first_step",
        cost_estimate=pl.CostEstimate(flops=500000000, bytes_accessed=8 << 20, transcendentals=8 << 20),
    )(pair_count, jnp.transpose(pairs[0, 0], (1, 0)), others, wide, outline, north_o, south_o, west_o, east_o)

    ocean = pl.pallas_call(
        ocean_kernel,
        name="ocean_sum",
        out_shape=jax.ShapeDtypeStruct((2, R, 128), F32),
        in_specs=[vspec()] * 2,
        out_specs=vspec(),
        scratch_shapes=[
            pltpu.VMEM((FX * FY, 256), F32),
            pltpu.VMEM((3, DEVS * BLK // 384, 128), F32),
        ],
        compiler_params=params(),
        cost_estimate=pl.CostEstimate(flops=5000000000, bytes_accessed=5 << 20, transcendentals=0),
    )(got.reshape(DEVS * BLK, 128), response.reshape(FX * FY, NB))

    force = jnp.concatenate([contact + ocean, ocean], axis=0)
    w = 2 * H - 1
    low, high = moved(force[:, FX : FX + w], "gx", True), moved(force[:, 1 : 1 + w], "gx", False)
    force = force + jnp.pad(low, ((0, 0), (0, R - w), (0, 0))) + jnp.pad(high, ((0, 0), (R - w, 0), (0, 0)))
    low, high = moved(force[:, :, FY : FY + w], "gy", True), moved(force[:, :, 1 : 1 + w], "gy", False)
    c = FY + 2 * H
    force = force + jnp.pad(low, ((0, 0), (0, 0), (0, 128 - w))) + jnp.pad(high, ((0, 0), (0, 0), (c - w, 128 - c)))

    vel, shift = pl.pallas_call(
        later_kernel,
        name="later_steps",
        out_shape=[jax.ShapeDtypeStruct((FX, 2, FY), F32)] * 2,
        in_specs=[sspec(), vspec(), vspec(), vspec(), aspec()],
        out_specs=[vspec()] * 2,
        scratch_shapes=[
            pltpu.VMEM((NCH, 4, 128, 128), F32),
            *chunk_scratch,
            pltpu.VMEM((5, R, 128), F32),
            pltpu.SemaphoreType.DMA((NCH,)),
        ],
        compiler_params=params(),
        cost_estimate=pl.CostEstimate(flops=500000000, bytes_accessed=4 << 20, transcendentals=16 << 20),
    )(counts, force, wide, words, tiles)
    return jnp.transpose(vel, (0, 2, 1)), jnp.transpose(shift, (0, 2, 1))


def solution(mesh):
    return jax.shard_map(
        shards,
        mesh=mesh,
        in_specs=(
            P("gx", "gy", None),
            P("gx", "gy", None),
            P("gx", "gy", None),
            P("gx", "gy"),
            P("gx", "gy", None),
            P("gx", "gy", None, None),
            P("gx", "gy"),
            P(("gx", "gy"), None),
            P(("gx", "gy"), None),
            P(("gx", "gy")),
        ),
        out_specs=(P("gx", "gy", None), P("gx", "gy", None)),
        check_vma=False,
    )
```

```python
import math

import jax
import jax.numpy as jnp
from jax import lax
from jax.experimental import pallas as pl
from jax.experimental.pallas import tpu as pltpu
from jax.sharding import PartitionSpec as P

FX, FY, V, TILE, NB, PMAX = 32, 64, 256, 128, 64, 512
DEVS, CAP, BLK = 128, 40, 41
STEPS = 3
DT, DRAG = 0.1, 0.5
H = 2
R = FX + 2 * H
RP = 40
RK = 48
CP = 72
TW = FY + 16
PADC = 8 - H
NCH = 9 * PMAX // 128
NEIGH = ((-1, 0), (1, 0), (-1, -1), (0, -1), (1, -1), (-1, 1), (0, 1), (1, 1))
SC = math.sqrt(100.0 * math.log2(math.e))
F32, BF16, I32 = jnp.float32, jnp.bfloat16, jnp.int32
VMEM_BYTES = 52 * 1024 * 1024


def params():
    return pltpu.CompilerParams(vmem_limit_bytes=VMEM_BYTES)


def vspec():
    return pl.BlockSpec(memory_space=pltpu.VMEM)


def sspec():
    return pl.BlockSpec(memory_space=pltpu.SMEM)


def aspec():
    return pl.BlockSpec(memory_space=pl.ANY)


def nt(a, b):
    return lax.dot_general(a, b, (((1,), (1,)), ((), ())), preferred_element_type=F32)


def nn(a, b):
    return jnp.dot(a, b, preferred_element_type=F32)


def split3(x):
    a = x.astype(BF16).astype(F32)
    b = (x - a).astype(BF16).astype(F32)
    return a, b, (x - a - b).astype(BF16).astype(F32)


def send_kernel(dest_ref, floe_ref, rows_ref, out_ref, place_v, ids_v, place_s, sem):
    upper = (
        lax.broadcasted_iota(I32, (128, 128), 0) < lax.broadcasted_iota(I32, (128, 128), 1)
    ).astype(F32).astype(BF16)
    ones = jnp.ones((128, 128), BF16)
    index = lax.broadcasted_iota(I32, (128, 128), 0)
    blocks = dest_ref.shape[0]
    hots = [(index == dest_ref[k : k + 1, :]).astype(F32) for k in range(blocks)]
    hot16 = jnp.concatenate([hot.astype(BF16) for hot in hots], axis=0)
    before = nn(hot16, upper)
    full = nn(hot16, ones)
    carry = jnp.zeros((128, 128), F32)
    high, low, slots = [], [], []
    for k in range(blocks):
        rank = jnp.sum(hots[k] * (before[128 * k : 128 * k + 128] + carry), axis=0, keepdims=True)
        carry = carry + full[128 * k : 128 * k + 128]
        rank = rank.astype(I32)
        place_v[k : k + 1, :] = dest_ref[k : k + 1, :] * BLK + rank
        floe = floe_ref[k : k + 1, :] + 1
        slots.append((index == rank).astype(F32).astype(BF16))
        high.append((hots[k] * (floe >> 6).astype(F32)).astype(BF16))
        low.append((hots[k] * (floe & 63).astype(F32)).astype(BF16))
    slots = jnp.concatenate(slots, axis=1)
    ids = 64.0 * nt(jnp.concatenate(high, axis=1), slots) + nt(jnp.concatenate(low, axis=1), slots)
    ids_v[...] = ids
    copy = pltpu.make_async_copy(place_v, place_s, sem)
    copy.start()

    @pl.loop(0, out_ref.shape[0] // 128)
    def _(i):
        out_ref[pl.ds(pl.multiple_of(i * 128, 128), 128), :] = jnp.zeros((128, 128), F32)

    copy.wait()

    @pl.loop(0, rows_ref.shape[0] // 16)
    def _(i):
        for j in range(16):
            r = i * 16 + j
            out_ref[pl.ds(place_s[r >> 7, r & 127], 1), :] = rows_ref[pl.ds(r, 1), :]

    @pl.loop(0, DEVS // 8)
    def _(i):
        for j in range(8):
            d = i * 8 + j
            out_ref[pl.ds(d * BLK + CAP, 1), :] = ids_v[pl.ds(d, 1), :]


def ocean_kernel(rows_ref, resp_ref, out_ref, acc_ref, ids_ref):
    groups = DEVS // 16
    lane = lax.broadcasted_iota(I32, (groups, 128), 1)
    blocks = [jnp.zeros((groups, 128), F32) for _ in range(5)]
    for j in range(16):
        ids = rows_ref[pl.ds(j * BLK + CAP, groups, stride=16 * BLK), :]
        shift = (CAP * j) % 128
        if shift:
            ids = pltpu.roll(ids, shift, 1)
        for b in range(5):
            if CAP * j < 128 * b + 128 and CAP * j + CAP > 128 * b:
                place = lane + (128 * b - CAP * j)
                blocks[b] = jnp.where((place >= 0) & (place < CAP), ids, blocks[b])
    for b in range(5):
        ids_ref[b] = blocks[b]
    acc_ref[...] = jnp.zeros_like(acc_ref)
    base16 = lax.broadcasted_iota(I32, (16, 128), 0).astype(F32)
    one, zero = jnp.ones((16, 128), BF16), jnp.zeros((16, 128), BF16)

    @pl.loop(0, groups // 2)
    def _(g):
        at = g * (32 * BLK)
        rows = jnp.concatenate([rows_ref[pl.ds(at + BLK * j, CAP), :] for j in range(32)], axis=0)
        high = rows.astype(BF16)
        low = (rows - high.astype(F32)).astype(BF16)
        both = jnp.concatenate([high, low], axis=1)
        ids = [ids_ref[b, pl.ds(2 * g + h, 1), :] for h in range(2) for b in range(5)]
        for part in range(8):
            cols = []
            for b in range(10):
                rel = jnp.broadcast_to(ids[b] - (part * 256 + 1.0), (16, 128)).astype(BF16)
                cols.append(
                    jnp.concatenate(
                        [jnp.where((base16 + 16.0 * k).astype(BF16) == rel, one, zero) for k in range(16)], axis=0
                    )
                )
            hot = jnp.concatenate(cols, axis=1)
            acc_ref[part * 256 : part * 256 + 256, :] += nn(hot, both)

    out_ref[...] = jnp.zeros_like(out_ref)
    srow = lax.broadcasted_iota(I32, (16, 128), 0)
    slane = lax.broadcasted_iota(I32, (16, 128), 1)
    pick = (((srow == 0) & (slane < NB)) | ((srow == 1) & (slane >= NB))).astype(F32).astype(BF16)
    inner = (slane >= H) & (slane < H + FY)

    @pl.loop(0, 8)
    def _(part):
        at = pl.multiple_of(part * 256, 256)
        total = acc_ref[pl.ds(at, 256), 0:128] + acc_ref[pl.ds(at, 256), 128:256]
        resp = resp_ref[pl.ds(at, 256), :]
        a, b, c = split3(total * jnp.concatenate([resp, resp], axis=1))
        force = nt(pick, a.astype(BF16)) + nt(pick, b.astype(BF16)) + nt(pick, c.astype(BF16))
        for j in range(4):
            piece = force[:, (j // 2) * 128 : (j // 2) * 128 + 128]
            piece = pltpu.roll(piece, (H - 64 * (j % 2)) % 128, 1)
            piece = jnp.where(inner, piece, 0.0)
            for k in range(2):
                out_ref[k, pl.ds(part * 4 + j + H, 1), :] = piece[k : k + 1]


def put_shift(left_ref, plane_ref, now_ref):
    for k in range(2):
        plane_ref[0:R, :] = now_ref[k]
        for j, part in enumerate(split3(jnp.transpose(plane_ref[...])[0:CP])):
            left_ref[3 * k + j] = part


def contact_chunk(c, half_at, words_ref, tiles_ref, left_ref, b_ref, acc_ref):
    word = words_ref[pl.ds(c, 1), :]
    ok = word >= 0
    rows = jnp.concatenate([(word >> 7) & 63, (word >> 20) & 63], axis=1)
    cols = jnp.concatenate([word & 127, (word >> 13) & 127], axis=1)
    code = (word >> 28) & 7
    code9 = code + (code >= 4).astype(I32)
    step = (code9 >= 3).astype(I32) + (code9 >= 6).astype(I32)
    dirx = (step - 1).astype(F32)
    diry = (code9 - 3 * step - 1).astype(F32)
    row_hot = (lax.broadcasted_iota(I32, (RK, 256), 0) == rows).astype(F32)
    row_hot16 = row_hot.astype(BF16)
    col_hot = lax.broadcasted_iota(I32, (CP, 256), 0) == cols
    lanes = lax.broadcasted_iota(I32, (128, 256), 0) == cols
    diffs = []
    for k in range(2):
        left = jnp.concatenate([left_ref[3 * k + j, :, 0:RK] for j in range(3)], axis=0)
        part = nn(left.astype(BF16), row_hot16)
        part = part[0:CP] + part[CP : 2 * CP] + part[2 * CP : 3 * CP]
        part = jnp.sum(jnp.where(col_hot, part, 0.0), axis=0, keepdims=True)
        diffs.append(part[:, 0:128] - part[:, 128:256])
    dx = (dirx - diffs[0]) * SC
    dy = (diry - diffs[1]) * SC
    px = tiles_ref[c, 2] + dx
    py = tiles_ref[c, 3] + dy
    b_ref[0] = 2.0 * px
    b_ref[1] = 2.0 * py
    b_ref[2] = -(px * px + py * py)
    turns = jnp.where(c == half_at, TILE // 32, TILE // 16)

    @pl.when(c == half_at)
    def _():
        left_half = lax.broadcasted_iota(I32, (64, 128), 1) < 64
        for k in range(3):
            b_ref[k, 0:64, :] = jnp.where(left_half, b_ref[k, 0:64, :], b_ref[k, 64:128, :])

    force_x = jnp.zeros((8, 128), F32)
    force_y = jnp.zeros((8, 128), F32)
    back_x = jnp.zeros((8, 128), F32)
    back_y = jnp.zeros((8, 128), F32)
    for half in range(2):
        ax = [tiles_ref[c, 0, half * 64 + 8 * k : half * 64 + 8 * k + 8, :] for k in range(8)]
        ay = [tiles_ref[c, 1, half * 64 + 8 * k : half * 64 + 8 * k + 8, :] for k in range(8)]
        na = [-(x * x + y * y) for x, y in zip(ax, ay)]

        def body(i, carry):
            sums, bx_sum, by_sum = carry
            sums = list(sums)
            for j in range(16):
                w = i * 16 + j
                bx = jnp.broadcast_to(b_ref[0, pl.ds(w, 1), :], (8, 128))
                by = jnp.broadcast_to(b_ref[1, pl.ds(w, 1), :], (8, 128))
                nb = jnp.broadcast_to(b_ref[2, pl.ds(w, 1), :], (8, 128))
                weights = [jnp.exp2((ax[k] * bx + ay[k] * by) + (na[k] + nb)) for k in range(8)]
                sums = [s + t for s, t in zip(sums, weights)]
                while len(weights) > 1:
                    weights = [weights[k] + weights[k + 1] for k in range(0, len(weights), 2)]
                bx_sum = bx_sum + weights[0] * bx
                by_sum = by_sum + weights[0] * by
            return tuple(sums), bx_sum, by_sum

        sums, back_x, back_y = lax.fori_loop(
            0, turns, body, (tuple(jnp.zeros((8, 128), F32) for _ in range(8)), back_x, back_y)
        )
        for k in range(8):
            force_x = force_x + ax[k] * sums[k]
            force_y = force_y + ay[k] * sums[k]
    fx = jnp.sum(force_x - 0.5 * back_x, axis=0, keepdims=True) * (1.0 / SC)
    fy = jnp.sum(force_y - 0.5 * back_y, axis=0, keepdims=True) * (1.0 / SC)
    parts = split3(jnp.where(ok, fx, 0.0)) + split3(jnp.where(ok, fy, 0.0))
    spread = [row_hot[0:RP] * jnp.concatenate([part, -part], axis=1) for part in parts]
    acc_ref[...] += nt(jnp.concatenate(spread, axis=0).astype(BF16), lanes.astype(F32).astype(BF16))


def acc_plane(acc_ref, k):
    at = 3 * RP * k
    return acc_ref[at : at + R, :] + acc_ref[at + RP : at + RP + R, :] + acc_ref[at + 2 * RP : at + 2 * RP + R, :]


def code_steps(code):
    code9 = code + (code >= 4).astype(I32)
    step = (code9 >= 3).astype(I32) + (code9 >= 6).astype(I32)
    return step - 1, code9 - 3 * step - 1


def pair_words(local, code, mine, theirs, count, di, dj, extra):
    step_x, step_y = code_steps(code)
    row = (local >> 6) + di * FX
    col = (local & 63) + dj * FY
    prow = row + step_x
    pcol = col + step_y
    row_all = prow + lax.axis_index("gx") * FX
    col_all = pcol + lax.axis_index("gy") * FY
    ok = lax.broadcasted_iota(I32, local.shape, 1) < count
    ok = ok & (row_all >= 0) & (row_all < lax.axis_size("gx") * FX)
    ok = ok & (col_all >= 0) & (col_all < lax.axis_size("gy") * FY)
    if extra:
        near = (row >= -1) & (row <= FX) & (col >= -1) & (col <= FY)
        ok = ok & (near | ((prow >= -1) & (prow <= FX) & (pcol >= -1) & (pcol <= FY)))
    word = (row + H) * 128 + col + H + (((prow + H) * 128 + pcol + H) << 13)
    return jnp.where(ok, word + (mine << 26) + (theirs << 27) + (code << 28), -1)


def first_kernel(
    count_ref, own_ref, lists_ref, state_ref, outline_ref, north_ref, south_ref, west_ref, east_ref,
    tiles_out, words_out, count_out, force_out,
    table, tiles, stage, place_v, place_s, left_ref, plane_ref, b_ref, acc_ref, sems, tile_sems,
):
    copies = []
    for q in range(4):
        lanes = slice(q * 128, q * 128 + 128)
        for k, (source, target) in enumerate((
            (outline_ref, table.at[q, H : H + FX, 8 : 8 + FY, :]),
            (north_ref, table.at[q, 0:H, 8 : 8 + FY, :]),
            (south_ref, table.at[q, H + FX : R, 8 : 8 + FY, :]),
            (west_ref, table.at[q, :, 0:8, :]),
            (east_ref, table.at[q, :, 8 + FY : 16 + FY, :]),
        )):
            copies.append(pltpu.make_async_copy(source.at[:, :, lanes], target, sems.at[5 * q + k]))
    for copy in copies:
        copy.start()
    live = count_ref[0, 0]
    word = pair_words(*[own_ref[k : k + 1, :] for k in range(4)], live, 0, 0, False)
    words_out[...] = jnp.full(words_out.shape, -1, I32)
    for b in range(4):
        words_out[b : b + 1, :] = word[:, 128 * b : 128 * b + 128]
    mine = (live + 127) >> 7
    number = lax.broadcasted_iota(I32, (8, PMAX), 0)
    di, dj = jnp.zeros((8, PMAX), I32), jnp.zeros((8, PMAX), I32)
    for k, (i, j) in enumerate(NEIGH):
        di = jnp.where(number == k, i, di)
        dj = jnp.where(number == k, j, dj)
    word = pair_words(*[lists_ref[k].astype(I32) for k in range(5)], di, dj, True)
    flags = (word >= 0).astype(F32)
    upper = (
        lax.broadcasted_iota(I32, (PMAX, PMAX), 0) < lax.broadcasted_iota(I32, (PMAX, PMAX), 1)
    ).astype(F32).astype(BF16)
    rank = nn(flags.astype(BF16), upper)
    base = jnp.zeros((1, 1), F32)
    ranks = []
    for k in range(8):
        ranks.append(jnp.where(flags[k : k + 1] > 0.0, rank[k : k + 1] + base, -1.0).astype(I32))
        base = base + jnp.sum(flags[k : k + 1], axis=1, keepdims=True)
    found_all = jnp.sum(flags).astype(I32)
    extra = (found_all + 127) >> 7
    total = mine + extra
    whole = (found_all + 63) >> 7
    slot = lax.broadcasted_iota(I32, (128, PMAX), 0)
    srow = lax.broadcasted_iota(I32, (16, PMAX), 0)
    pieces = []
    for k in range(8):
        one = word[k : k + 1]
        piece = jnp.where(srow == 0, one & 255, jnp.where(srow == 1, (one >> 8) & 255, 0))
        piece = jnp.where(srow == 2, (one >> 16) & 255, jnp.where(srow == 3, (one >> 24) & 127, piece))
        piece = jnp.where(srow == 4, 1, piece)
        pieces.append(piece.astype(F32).astype(BF16))

    @pl.loop(0, extra)
    def _(i):
        found = jnp.zeros((16, 128), F32)
        want = jnp.where(i >= whole, slot & 63, slot)
        for k in range(8):
            found = found + nt(pieces[k], (want == ranks[k] - i * 128).astype(F32).astype(BF16))
        found = found.astype(I32)
        value = found[0:1] + (found[1:2] << 8) + (found[2:3] << 16) + (found[3:4] << 24)
        words_out[pl.ds(mine + i, 1), :] = jnp.where(found[4:5] > 0, value, -1)

    word = jnp.maximum(words_out[...], 0)
    own = ((word >> 7) & 63) * TW + (word & 127) + PADC
    other = ((word >> 20) & 63) * TW + ((word >> 13) & 127) + PADC
    place_v[0] = own + ((word >> 26) & 1) * (R * TW)
    place_v[1] = other + ((word >> 27) & 1) * (R * TW)
    copy = pltpu.make_async_copy(place_v, place_s, sems.at[20])
    copy.start()
    count_out[0] = total
    count_out[1] = jnp.where(extra > whole, total - 1, -1)
    for piece in copies:
        piece.wait()
    copy.wait()
    flat = table.reshape(4 * R * TW, 128)

    @pl.loop(0, total)
    def _(c):
        @pl.loop(0, 16)
        def _(i):
            for j in range(8):
                at = i * 8 + j
                own = place_s[0, c, at]
                other = place_s[1, c, at]
                stage[0, pl.ds(at, 1), :] = flat[pl.ds(own, 1), :]
                stage[1, pl.ds(at, 1), :] = flat[pl.ds(own + 2 * R * TW, 1), :]
                stage[2, pl.ds(at, 1), :] = flat[pl.ds(other, 1), :]
                stage[3, pl.ds(at, 1), :] = flat[pl.ds(other + 2 * R * TW, 1), :]

        for k in range(4):
            tiles[c, k] = jnp.transpose(stage[k]) * SC
        pltpu.make_async_copy(tiles.at[c], tiles_out.at[c], tile_sems.at[c]).start()

    plane_ref[...] = jnp.zeros_like(plane_ref)
    put_shift(left_ref, plane_ref, state_ref)
    acc_ref[...] = jnp.zeros_like(acc_ref)

    @pl.loop(0, mine)
    def _(c):
        contact_chunk(c, -1, words_out, tiles, left_ref, b_ref, acc_ref)

    for k in range(2):
        force_out[k] = acc_plane(acc_ref, k)

    @pl.loop(0, total)
    def _(c):
        pltpu.make_async_copy(tiles.at[c], tiles_out.at[c], tile_sems.at[c]).wait()


def later_kernel(
    count_ref, force_ref, state_ref, words_ref, tiles_in, vel_out, shift_out,
    tiles, left_ref, plane_ref, b_ref, acc_ref, now_ref, tile_sems,
):
    total = count_ref[0]
    half_at = count_ref[1]

    @pl.loop(0, total)
    def _(c):
        pltpu.make_async_copy(tiles_in.at[c], tiles.at[c], tile_sems.at[c]).start()

    now_ref[...] = state_ref[...]

    def update(forces):
        scale = DT / now_ref[4]
        for k in range(2):
            vel = now_ref[2 + k]
            vel = vel + (forces[k] - DRAG * vel) * scale
            now_ref[2 + k] = vel
            now_ref[k] = now_ref[k] + DT * vel

    update([force_ref[0], force_ref[1]])
    plane_ref[...] = jnp.zeros_like(plane_ref)

    @pl.loop(0, total)
    def _(c):
        pltpu.make_async_copy(tiles_in.at[c], tiles.at[c], tile_sems.at[c]).wait()

    @pl.loop(1, STEPS)
    def _(step):
        put_shift(left_ref, plane_ref, now_ref)
        acc_ref[...] = jnp.zeros_like(acc_ref)

        @pl.loop(0, total)
        def _(c):
            contact_chunk(c, half_at, words_ref, tiles, left_ref, b_ref, acc_ref)

        update([acc_plane(acc_ref, k) + force_ref[2 + k] for k in range(2)])

    for out, base in ((shift_out, 0), (vel_out, 2)):
        for k in range(2):
            plane_ref[0:R, :] = pltpu.roll(now_ref[base + k], 128 - H, 1)
            for r in range(FX):
                out[r, k : k + 1, :] = plane_ref[r + H : r + H + 1, 0:FY]


def moved(x, axis, up):
    count = lax.axis_size(axis)
    pairs = [(i, i + 1) if up else (i + 1, i) for i in range(count - 1)]
    return lax.ppermute(x, axis, pairs)


def as_rows(x, rows):
    flat = x.reshape(-1)
    return jnp.pad(flat, (0, rows * 512 - flat.shape[0])).reshape(rows, 512)


def shards(
    outline, centres, velocity, mass, response, pairs, pair_count, forcing, ocean_dest, ocean_floe
):
    rows_dev = forcing.shape[0]
    send = pl.pallas_call(
        send_kernel,
        name="send_rows",
        out_shape=jax.ShapeDtypeStruct((DEVS * BLK, 128), F32),
        in_specs=[vspec()] * 3,
        out_specs=vspec(),
        scratch_shapes=[
            pltpu.VMEM((rows_dev // 128, 128), I32),
            pltpu.VMEM((DEVS, 128), F32),
            pltpu.SMEM((rows_dev // 128, 128), I32),
            pltpu.SemaphoreType.DMA,
        ],
        compiler_params=params(),
        cost_estimate=pl.CostEstimate(flops=100000000, bytes_accessed=4 << 20, transcendentals=0),
    )(ocean_dest.reshape(rows_dev // 128, 128), ocean_floe.reshape(rows_dev // 128, 128), forcing)
    state = jnp.concatenate(
        [jnp.transpose(centres, (2, 0, 1)), jnp.transpose(velocity, (2, 0, 1)), mass[None]], axis=0
    )
    lists = jnp.transpose(pairs[0, 0], (1, 0)).astype(F32)
    count = jnp.broadcast_to(pair_count.astype(F32), (1, 512))

    def pack_x(lo):
        return jnp.concatenate(
            [outline[lo : lo + H].reshape(H * FY, 512), as_rows(state[:, lo : lo + H], 2), lists, count,
             jnp.zeros((1, 512), F32)], axis=0
        )

    def unpack_x(got):
        return (
            got[: H * FY].reshape(H, FY, 512),
            got[H * FY : H * FY + 2].reshape(-1)[: 5 * H * FY].reshape(5, H, FY),
            got[H * FY + 2 : H * FY + 7],
        )

    north_o, north_s, north_l = unpack_x(moved(pack_x(FX - H), "gx", True))
    south_o, south_s, south_l = unpack_x(moved(pack_x(0), "gx", False))
    tall = jnp.concatenate([north_s, state, south_s], axis=1)
    own_l = jnp.concatenate([lists, count], axis=0)

    def pack_y(lo):
        cols = jnp.concatenate(
            [north_o[:, lo : lo + H], outline[:, lo : lo + H], south_o[:, lo : lo + H]], axis=0
        )
        return jnp.concatenate(
            [cols.reshape(R * H, 512), as_rows(tall[:, :, lo : lo + H], 1), north_l, own_l, south_l], axis=0
        )

    def unpack_y(got):
        return (
            got[: R * H].reshape(R, H, 512),
            got[R * H].reshape(-1)[: 5 * R * H].reshape(5, R, H),
            got[R * H + 1 : R * H + 16],
        )

    west, east, send = lax.optimization_barrier(
        (moved(pack_y(FY - H), "gy", True), moved(pack_y(0), "gy", False), send)
    )
    got = lax.all_to_all(
        send.reshape(DEVS, 1, BLK * 128), ("gx", "gy"), split_axis=0, concat_axis=0, tiled=True
    )
    west_o, west_s, west_l = unpack_y(west)
    east_o, east_s, east_l = unpack_y(east)
    west_o = jnp.pad(west_o, ((0, 0), (8 - H, 0), (0, 0)))
    east_o = jnp.pad(east_o, ((0, 0), (0, 8 - H), (0, 0)))
    wide = jnp.concatenate([west_s, tall, east_s], axis=2)
    wide = jnp.pad(wide, ((0, 0), (0, 0), (0, 128 - FY - 2 * H)))
    weight = jnp.where(wide[4:5] == 0.0, 1.0, wide[4:5])
    wide = jnp.concatenate([wide[:4], weight], axis=0)
    others = [north_l, south_l] + [block[5 * k : 5 * k + 5] for block in (west_l, east_l) for k in (0, 1, 2)]
    others = jnp.stack(others, axis=1)
    chunk_scratch = [
        pltpu.VMEM((6, CP, 128), F32),
        pltpu.VMEM((128, 128), F32),
        pltpu.VMEM((3, 128, 128), F32),
        pltpu.VMEM((6 * RP, 128), F32),
    ]
    tiles, words, counts, contact = pl.pallas_call(
        first_kernel,
        out_shape=[
            jax.ShapeDtypeStruct((NCH, 4, 128, 128), F32),
            jax.ShapeDtypeStruct((NCH, 128), I32),
            jax.ShapeDtypeStruct((2,), I32),
            jax.ShapeDtypeStruct((2, R, 128), F32),
        ],
        in_specs=[sspec(), vspec(), vspec(), vspec()] + [aspec()] * 5,
        out_specs=[aspec(), vspec(), sspec(), vspec()],
        scratch_shapes=[
            pltpu.VMEM((4, R, TW, 128), F32),
            pltpu.VMEM((NCH, 4, 128, 128), F32),
            pltpu.VMEM((4, 128, 128), F32),
            pltpu.VMEM((2, NCH, 128), I32),
            pltpu.SMEM((2, NCH, 128), I32),
            *chunk_scratch,
            pltpu.SemaphoreType.DMA((21,)),
            pltpu.SemaphoreType.DMA((NCH,)),
        ],
        compiler_params=params(),
        name="first_step",
        cost_estimate=pl.CostEstimate(flops=500000000, bytes_accessed=8 << 20, transcendentals=8 << 20),
    )(pair_count, jnp.transpose(pairs[0, 0], (1, 0)), others, wide, outline, north_o, south_o, west_o, east_o)

    ocean = pl.pallas_call(
        ocean_kernel,
        name="ocean_sum",
        out_shape=jax.ShapeDtypeStruct((2, R, 128), F32),
        in_specs=[vspec()] * 2,
        out_specs=vspec(),
        scratch_shapes=[
            pltpu.VMEM((FX * FY, 256), F32),
            pltpu.VMEM((5, DEVS // 16, 128), F32),
        ],
        compiler_params=params(),
        cost_estimate=pl.CostEstimate(flops=5000000000, bytes_accessed=5 << 20, transcendentals=0),
    )(got.reshape(DEVS * BLK, 128), response.reshape(FX * FY, NB))

    force = jnp.concatenate([contact + ocean, ocean], axis=0)
    w = 2 * H - 1
    low, high = moved(force[:, FX : FX + w], "gx", True), moved(force[:, 1 : 1 + w], "gx", False)
    force = force + jnp.pad(low, ((0, 0), (0, R - w), (0, 0))) + jnp.pad(high, ((0, 0), (R - w, 0), (0, 0)))
    low, high = moved(force[:, :, FY : FY + w], "gy", True), moved(force[:, :, 1 : 1 + w], "gy", False)
    c = FY + 2 * H
    force = force + jnp.pad(low, ((0, 0), (0, 0), (0, 128 - w))) + jnp.pad(high, ((0, 0), (0, 0), (c - w, 128 - c)))

    vel, shift = pl.pallas_call(
        later_kernel,
        name="later_steps",
        out_shape=[jax.ShapeDtypeStruct((FX, 2, FY), F32)] * 2,
        in_specs=[sspec(), vspec(), vspec(), vspec(), aspec()],
        out_specs=[vspec()] * 2,
        scratch_shapes=[
            pltpu.VMEM((NCH, 4, 128, 128), F32),
            *chunk_scratch,
            pltpu.VMEM((5, R, 128), F32),
            pltpu.SemaphoreType.DMA((NCH,)),
        ],
        compiler_params=params(),
        cost_estimate=pl.CostEstimate(flops=500000000, bytes_accessed=4 << 20, transcendentals=16 << 20),
    )(counts, force, wide, words, tiles)
    return jnp.transpose(vel, (0, 2, 1)), jnp.transpose(shift, (0, 2, 1))


def solution(mesh):
    return jax.shard_map(
        shards,
        mesh=mesh,
        in_specs=(
            P("gx", "gy", None),
            P("gx", "gy", None),
            P("gx", "gy", None),
            P("gx", "gy"),
            P("gx", "gy", None),
            P("gx", "gy", None, None),
            P("gx", "gy"),
            P(("gx", "gy"), None),
            P(("gx", "gy"), None),
            P(("gx", "gy")),
        ),
        out_specs=(P("gx", "gy", None), P("gx", "gy", None)),
        check_vma=False,
    )
```

```python
import math

import jax
import jax.numpy as jnp
from jax import lax
from jax.experimental import pallas as pl
from jax.experimental.pallas import tpu as pltpu
from jax.sharding import PartitionSpec as P

FX, FY, V, TILE, NB, PMAX = 32, 64, 256, 128, 64, 512
DEVS, CAP, BLK = 128, 40, 41
STEPS = 3
DT, DRAG = 0.1, 0.5
H = 2
R = FX + 2 * H
RP = 40
RK = 48
CP = 72
TW = FY + 16
PADC = 8 - H
NCH = 9 * PMAX // 128
NEIGH = ((-1, 0), (1, 0), (-1, -1), (0, -1), (1, -1), (-1, 1), (0, 1), (1, 1))
SC = math.sqrt(100.0 * math.log2(math.e))
F32, BF16, I32 = jnp.float32, jnp.bfloat16, jnp.int32
VMEM_BYTES = 52 * 1024 * 1024


def params():
    return pltpu.CompilerParams(vmem_limit_bytes=VMEM_BYTES)


def vspec():
    return pl.BlockSpec(memory_space=pltpu.VMEM)


def sspec():
    return pl.BlockSpec(memory_space=pltpu.SMEM)


def aspec():
    return pl.BlockSpec(memory_space=pl.ANY)


def nt(a, b):
    return lax.dot_general(a, b, (((1,), (1,)), ((), ())), preferred_element_type=F32)


def nn(a, b):
    return jnp.dot(a, b, preferred_element_type=F32)


def split3(x):
    a = x.astype(BF16).astype(F32)
    b = (x - a).astype(BF16).astype(F32)
    return a, b, (x - a - b).astype(BF16).astype(F32)


def send_kernel(dest_ref, floe_ref, rows_ref, out_ref, place_v, ids_v, place_s, sem):
    upper = (
        lax.broadcasted_iota(I32, (128, 128), 0) < lax.broadcasted_iota(I32, (128, 128), 1)
    ).astype(F32).astype(BF16)
    ones = jnp.ones((128, 128), BF16)
    index = lax.broadcasted_iota(I32, (128, 128), 0)
    blocks = dest_ref.shape[0]
    hots = [(index == dest_ref[k : k + 1, :]).astype(F32) for k in range(blocks)]
    hot16 = jnp.concatenate([hot.astype(BF16) for hot in hots], axis=0)
    before = nn(hot16, upper)
    full = nn(hot16, ones)
    carry = jnp.zeros((128, 128), F32)
    high, low, slots = [], [], []
    for k in range(blocks):
        rank = jnp.sum(hots[k] * (before[128 * k : 128 * k + 128] + carry), axis=0, keepdims=True)
        carry = carry + full[128 * k : 128 * k + 128]
        rank = rank.astype(I32)
        place_v[k : k + 1, :] = dest_ref[k : k + 1, :] * BLK + rank
        floe = floe_ref[k : k + 1, :] + 1
        slots.append((index == rank).astype(F32).astype(BF16))
        high.append((hots[k] * (floe >> 6).astype(F32)).astype(BF16))
        low.append((hots[k] * (floe & 63).astype(F32)).astype(BF16))
    slots = jnp.concatenate(slots, axis=1)
    ids = 64.0 * nt(jnp.concatenate(high, axis=1), slots) + nt(jnp.concatenate(low, axis=1), slots)
    ids_v[...] = ids
    copy = pltpu.make_async_copy(place_v, place_s, sem)
    copy.start()

    @pl.loop(0, out_ref.shape[0] // 128)
    def _(i):
        out_ref[pl.ds(pl.multiple_of(i * 128, 128), 128), :] = jnp.zeros((128, 128), F32)

    copy.wait()

    @pl.loop(0, rows_ref.shape[0] // 128)
    def _(k):
        for j in range(128):
            out_ref[pl.ds(place_s[k, j], 1), :] = rows_ref[pl.ds(k * 128 + j, 1), :]

    for d in range(DEVS):
        out_ref[d * BLK + CAP : d * BLK + CAP + 1, :] = ids_v[d : d + 1, :]


def ocean_kernel(rows_ref, resp_ref, out_ref, acc_ref, ids_ref):
    groups = DEVS // 16
    lane = lax.broadcasted_iota(I32, (groups, 128), 1)
    blocks = [jnp.zeros((groups, 128), F32) for _ in range(5)]
    for j in range(16):
        ids = rows_ref[pl.ds(j * BLK + CAP, groups, stride=16 * BLK), :]
        shift = (CAP * j) % 128
        if shift:
            ids = pltpu.roll(ids, shift, 1)
        for b in range(5):
            if CAP * j < 128 * b + 128 and CAP * j + CAP > 128 * b:
                place = lane + (128 * b - CAP * j)
                blocks[b] = jnp.where((place >= 0) & (place < CAP), ids, blocks[b])
    for b in range(5):
        ids_ref[b] = blocks[b]
    acc_ref[...] = jnp.zeros_like(acc_ref)
    base16 = lax.broadcasted_iota(I32, (16, 128), 0).astype(F32)
    one, zero = jnp.ones((16, 128), BF16), jnp.zeros((16, 128), BF16)

    @pl.loop(0, groups // 4)
    def _(g):
        at = g * (64 * BLK)
        rows = jnp.concatenate([rows_ref[pl.ds(at + BLK * j, CAP), :] for j in range(64)], axis=0)
        high = rows.astype(BF16)
        low = (rows - high.astype(F32)).astype(BF16)
        both = jnp.concatenate([high, low], axis=1)
        ids = [ids_ref[b, pl.ds(4 * g + h, 1), :] for h in range(4) for b in range(5)]
        for part in range(8):
            cols = []
            for b in range(20):
                rel = jnp.broadcast_to(ids[b] - (part * 256 + 1.0), (16, 128)).astype(BF16)
                cols.append(
                    jnp.concatenate(
                        [jnp.where((base16 + 16.0 * k).astype(BF16) == rel, one, zero) for k in range(16)], axis=0
                    )
                )
            hot = jnp.concatenate(cols, axis=1)
            acc_ref[part * 256 : part * 256 + 256, :] += nn(hot, both)

    out_ref[...] = jnp.zeros_like(out_ref)
    srow = lax.broadcasted_iota(I32, (16, 128), 0)
    slane = lax.broadcasted_iota(I32, (16, 128), 1)
    pick = (((srow == 0) & (slane < NB)) | ((srow == 1) & (slane >= NB))).astype(F32).astype(BF16)
    inner = (slane >= H) & (slane < H + FY)

    for part in range(8):
        at = part * 256
        total = acc_ref[pl.ds(at, 256), 0:128] + acc_ref[pl.ds(at, 256), 128:256]
        resp = resp_ref[pl.ds(at, 256), :]
        a, b, c = split3(total * jnp.concatenate([resp, resp], axis=1))
        force = nt(pick, a.astype(BF16)) + nt(pick, b.astype(BF16)) + nt(pick, c.astype(BF16))
        for j in range(4):
            piece = force[:, (j // 2) * 128 : (j // 2) * 128 + 128]
            piece = pltpu.roll(piece, (H - 64 * (j % 2)) % 128, 1)
            piece = jnp.where(inner, piece, 0.0)
            for k in range(2):
                out_ref[k, part * 4 + j + H : part * 4 + j + H + 1, :] = piece[k : k + 1]


def put_shift(left_ref, plane_ref, now_ref):
    for k in range(2):
        plane_ref[0:R, :] = now_ref[k]
        for j, part in enumerate(split3(jnp.transpose(plane_ref[...])[0:CP])):
            left_ref[3 * k + j] = part


def contact_chunk(c, half_at, words_ref, tiles_ref, left_ref, b_ref, acc_ref):
    word = words_ref[pl.ds(c, 1), :]
    ok = word >= 0
    rows = jnp.concatenate([(word >> 7) & 63, (word >> 20) & 63], axis=1)
    cols = jnp.concatenate([word & 127, (word >> 13) & 127], axis=1)
    code = (word >> 28) & 7
    code9 = code + (code >= 4).astype(I32)
    step = (code9 >= 3).astype(I32) + (code9 >= 6).astype(I32)
    dirx = (step - 1).astype(F32)
    diry = (code9 - 3 * step - 1).astype(F32)
    row_hot = (lax.broadcasted_iota(I32, (RK, 256), 0) == rows).astype(F32)
    row_hot16 = row_hot.astype(BF16)
    col_hot = lax.broadcasted_iota(I32, (CP, 256), 0) == cols
    lanes = lax.broadcasted_iota(I32, (128, 256), 0) == cols
    diffs = []
    for k in range(2):
        left = jnp.concatenate([left_ref[3 * k + j, :, 0:RK] for j in range(3)], axis=0)
        part = nn(left.astype(BF16), row_hot16)
        part = part[0:CP] + part[CP : 2 * CP] + part[2 * CP : 3 * CP]
        part = jnp.sum(jnp.where(col_hot, part, 0.0), axis=0, keepdims=True)
        diffs.append(part[:, 0:128] - part[:, 128:256])
    dx = (dirx - diffs[0]) * SC
    dy = (diry - diffs[1]) * SC
    px = tiles_ref[c, 2] + dx
    py = tiles_ref[c, 3] + dy
    b_ref[0] = 2.0 * px
    b_ref[1] = 2.0 * py
    b_ref[2] = -(px * px + py * py)
    turns = jnp.where(c == half_at, TILE // 32, TILE // 16)

    @pl.when(c == half_at)
    def _():
        left_half = lax.broadcasted_iota(I32, (64, 128), 1) < 64
        for k in range(3):
            b_ref[k, 0:64, :] = jnp.where(left_half, b_ref[k, 0:64, :], b_ref[k, 64:128, :])

    force_x = jnp.zeros((8, 128), F32)
    force_y = jnp.zeros((8, 128), F32)
    back_x = jnp.zeros((8, 128), F32)
    back_y = jnp.zeros((8, 128), F32)
    for half in range(2):
        ax = [tiles_ref[c, 0, half * 64 + 8 * k : half * 64 + 8 * k + 8, :] for k in range(8)]
        ay = [tiles_ref[c, 1, half * 64 + 8 * k : half * 64 + 8 * k + 8, :] for k in range(8)]
        na = [-(x * x + y * y) for x, y in zip(ax, ay)]

        def body(i, carry):
            sums, bx_sum, by_sum = carry
            sums = list(sums)
            for j in range(16):
                w = i * 16 + j
                bx = jnp.broadcast_to(b_ref[0, pl.ds(w, 1), :], (8, 128))
                by = jnp.broadcast_to(b_ref[1, pl.ds(w, 1), :], (8, 128))
                nb = jnp.broadcast_to(b_ref[2, pl.ds(w, 1), :], (8, 128))
                weights = [jnp.exp2((ax[k] * bx + ay[k] * by) + (na[k] + nb)) for k in range(8)]
                sums = [s + t for s, t in zip(sums, weights)]
                while len(weights) > 1:
                    weights = [weights[k] + weights[k + 1] for k in range(0, len(weights), 2)]
                bx_sum = bx_sum + weights[0] * bx
                by_sum = by_sum + weights[0] * by
            return tuple(sums), bx_sum, by_sum

        sums, back_x, back_y = lax.fori_loop(
            0, turns, body, (tuple(jnp.zeros((8, 128), F32) for _ in range(8)), back_x, back_y)
        )
        for k in range(8):
            force_x = force_x + ax[k] * sums[k]
            force_y = force_y + ay[k] * sums[k]
    fx = jnp.sum(force_x - 0.5 * back_x, axis=0, keepdims=True) * (1.0 / SC)
    fy = jnp.sum(force_y - 0.5 * back_y, axis=0, keepdims=True) * (1.0 / SC)
    parts = split3(jnp.where(ok, fx, 0.0)) + split3(jnp.where(ok, fy, 0.0))
    spread = [row_hot[0:RP] * jnp.concatenate([part, -part], axis=1) for part in parts]
    acc_ref[...] += nt(jnp.concatenate(spread, axis=0).astype(BF16), lanes.astype(F32).astype(BF16))


def acc_plane(acc_ref, k):
    at = 3 * RP * k
    return acc_ref[at : at + R, :] + acc_ref[at + RP : at + RP + R, :] + acc_ref[at + 2 * RP : at + 2 * RP + R, :]


def code_steps(code):
    code9 = code + (code >= 4).astype(I32)
    step = (code9 >= 3).astype(I32) + (code9 >= 6).astype(I32)
    return step - 1, code9 - 3 * step - 1


def pair_words(local, code, mine, theirs, count, di, dj, extra):
    step_x, step_y = code_steps(code)
    row = (local >> 6) + di * FX
    col = (local & 63) + dj * FY
    prow = row + step_x
    pcol = col + step_y
    row_all = prow + lax.axis_index("gx") * FX
    col_all = pcol + lax.axis_index("gy") * FY
    ok = lax.broadcasted_iota(I32, local.shape, 1) < count
    ok = ok & (row_all >= 0) & (row_all < lax.axis_size("gx") * FX)
    ok = ok & (col_all >= 0) & (col_all < lax.axis_size("gy") * FY)
    if extra:
        near = (row >= -1) & (row <= FX) & (col >= -1) & (col <= FY)
        ok = ok & (near | ((prow >= -1) & (prow <= FX) & (pcol >= -1) & (pcol <= FY)))
    word = (row + H) * 128 + col + H + (((prow + H) * 128 + pcol + H) << 13)
    return jnp.where(ok, word + (mine << 26) + (theirs << 27) + (code << 28), -1)


def first_kernel(
    count_ref, own_ref, lists_ref, state_ref, outline_ref, north_ref, south_ref, west_ref, east_ref,
    tiles_out, words_out, count_out, force_out,
    table, tiles, stage, place_v, place_s, left_ref, plane_ref, b_ref, acc_ref, sems, tile_sems,
):
    copies = []
    for q in range(4):
        lanes = slice(q * 128, q * 128 + 128)
        for k, (source, target) in enumerate((
            (outline_ref, table.at[q, H : H + FX, 8 : 8 + FY, :]),
            (north_ref, table.at[q, 0:H, 8 : 8 + FY, :]),
            (south_ref, table.at[q, H + FX : R, 8 : 8 + FY, :]),
            (west_ref, table.at[q, :, 0:8, :]),
            (east_ref, table.at[q, :, 8 + FY : 16 + FY, :]),
        )):
            copies.append(pltpu.make_async_copy(source.at[:, :, lanes], target, sems.at[5 * q + k]))
    for copy in copies:
        copy.start()
    live = count_ref[0, 0]
    word = pair_words(*[own_ref[k : k + 1, :] for k in range(4)], live, 0, 0, False)
    words_out[...] = jnp.full(words_out.shape, -1, I32)
    for b in range(4):
        words_out[b : b + 1, :] = word[:, 128 * b : 128 * b + 128]
    mine = (live + 127) >> 7
    number = lax.broadcasted_iota(I32, (8, PMAX), 0)
    di, dj = jnp.zeros((8, PMAX), I32), jnp.zeros((8, PMAX), I32)
    for k, (i, j) in enumerate(NEIGH):
        di = jnp.where(number == k, i, di)
        dj = jnp.where(number == k, j, dj)
    word = pair_words(*[lists_ref[k].astype(I32) for k in range(5)], di, dj, True)
    flags = (word >= 0).astype(F32)
    upper = (
        lax.broadcasted_iota(I32, (PMAX, PMAX), 0) < lax.broadcasted_iota(I32, (PMAX, PMAX), 1)
    ).astype(F32).astype(BF16)
    rank = nn(flags.astype(BF16), upper)
    base = jnp.zeros((1, 1), F32)
    ranks = []
    for k in range(8):
        ranks.append(jnp.where(flags[k : k + 1] > 0.0, rank[k : k + 1] + base, -1.0).astype(I32))
        base = base + jnp.sum(flags[k : k + 1], axis=1, keepdims=True)
    found_all = jnp.sum(flags).astype(I32)
    extra = (found_all + 127) >> 7
    total = mine + extra
    whole = (found_all + 63) >> 7
    slot = lax.broadcasted_iota(I32, (128, PMAX), 0)
    srow = lax.broadcasted_iota(I32, (16, PMAX), 0)
    pieces = []
    for k in range(8):
        one = word[k : k + 1]
        piece = jnp.where(srow == 0, one & 255, jnp.where(srow == 1, (one >> 8) & 255, 0))
        piece = jnp.where(srow == 2, (one >> 16) & 255, jnp.where(srow == 3, (one >> 24) & 127, piece))
        piece = jnp.where(srow == 4, 1, piece)
        pieces.append(piece.astype(F32).astype(BF16))

    @pl.loop(0, extra)
    def _(i):
        found = jnp.zeros((16, 128), F32)
        want = jnp.where(i >= whole, slot & 63, slot)
        for k in range(8):
            found = found + nt(pieces[k], (want == ranks[k] - i * 128).astype(F32).astype(BF16))
        found = found.astype(I32)
        value = found[0:1] + (found[1:2] << 8) + (found[2:3] << 16) + (found[3:4] << 24)
        words_out[pl.ds(mine + i, 1), :] = jnp.where(found[4:5] > 0, value, -1)

    word = jnp.maximum(words_out[...], 0)
    own = ((word >> 7) & 63) * TW + (word & 127) + PADC
    other = ((word >> 20) & 63) * TW + ((word >> 13) & 127) + PADC
    place_v[0] = own + ((word >> 26) & 1) * (R * TW)
    place_v[1] = other + ((word >> 27) & 1) * (R * TW)
    copy = pltpu.make_async_copy(place_v, place_s, sems.at[20])
    copy.start()
    count_out[0] = total
    count_out[1] = jnp.where(extra > whole, total - 1, -1)
    for piece in copies:
        piece.wait()
    copy.wait()
    flat = table.reshape(4 * R * TW, 128)

    @pl.loop(0, total)
    def _(c):
        @pl.loop(0, 16)
        def _(i):
            for j in range(8):
                at = i * 8 + j
                own = place_s[0, c, at]
                other = place_s[1, c, at]
                stage[0, pl.ds(at, 1), :] = flat[pl.ds(own, 1), :]
                stage[1, pl.ds(at, 1), :] = flat[pl.ds(own + 2 * R * TW, 1), :]
                stage[2, pl.ds(at, 1), :] = flat[pl.ds(other, 1), :]
                stage[3, pl.ds(at, 1), :] = flat[pl.ds(other + 2 * R * TW, 1), :]

        for k in range(4):
            tiles[c, k] = jnp.transpose(stage[k]) * SC
        pltpu.make_async_copy(tiles.at[c], tiles_out.at[c], tile_sems.at[c]).start()

    plane_ref[...] = jnp.zeros_like(plane_ref)
    put_shift(left_ref, plane_ref, state_ref)
    acc_ref[...] = jnp.zeros_like(acc_ref)

    @pl.loop(0, mine)
    def _(c):
        contact_chunk(c, -1, words_out, tiles, left_ref, b_ref, acc_ref)

    for k in range(2):
        force_out[k] = acc_plane(acc_ref, k)

    @pl.loop(0, total)
    def _(c):
        pltpu.make_async_copy(tiles.at[c], tiles_out.at[c], tile_sems.at[c]).wait()


def later_kernel(
    count_ref, force_ref, state_ref, words_ref, tiles_in, vel_out, shift_out,
    tiles, left_ref, plane_ref, b_ref, acc_ref, now_ref, tile_sems,
):
    total = count_ref[0]
    half_at = count_ref[1]

    @pl.loop(0, total)
    def _(c):
        pltpu.make_async_copy(tiles_in.at[c], tiles.at[c], tile_sems.at[c]).start()

    now_ref[...] = state_ref[...]

    def update(forces):
        scale = DT / now_ref[4]
        for k in range(2):
            vel = now_ref[2 + k]
            vel = vel + (forces[k] - DRAG * vel) * scale
            now_ref[2 + k] = vel
            now_ref[k] = now_ref[k] + DT * vel

    update([force_ref[0], force_ref[1]])
    plane_ref[...] = jnp.zeros_like(plane_ref)

    @pl.loop(0, total)
    def _(c):
        pltpu.make_async_copy(tiles_in.at[c], tiles.at[c], tile_sems.at[c]).wait()

    @pl.loop(1, STEPS)
    def _(step):
        put_shift(left_ref, plane_ref, now_ref)
        acc_ref[...] = jnp.zeros_like(acc_ref)

        @pl.loop(0, total)
        def _(c):
            contact_chunk(c, half_at, words_ref, tiles, left_ref, b_ref, acc_ref)

        update([acc_plane(acc_ref, k) + force_ref[2 + k] for k in range(2)])

    for out, base in ((shift_out, 0), (vel_out, 2)):
        for k in range(2):
            plane_ref[0:R, :] = pltpu.roll(now_ref[base + k], 128 - H, 1)
            for r in range(FX):
                out[r, k : k + 1, :] = plane_ref[r + H : r + H + 1, 0:FY]


def moved(x, axis, up):
    count = lax.axis_size(axis)
    pairs = [(i, i + 1) if up else (i + 1, i) for i in range(count - 1)]
    return lax.ppermute(x, axis, pairs)


def as_rows(x, rows):
    flat = x.reshape(-1)
    return jnp.pad(flat, (0, rows * 512 - flat.shape[0])).reshape(rows, 512)


def shards(
    outline, centres, velocity, mass, response, pairs, pair_count, forcing, ocean_dest, ocean_floe
):
    rows_dev = forcing.shape[0]
    send = pl.pallas_call(
        send_kernel,
        name="send_rows",
        out_shape=jax.ShapeDtypeStruct((DEVS * BLK, 128), F32),
        in_specs=[vspec()] * 3,
        out_specs=vspec(),
        scratch_shapes=[
            pltpu.VMEM((rows_dev // 128, 128), I32),
            pltpu.VMEM((DEVS, 128), F32),
            pltpu.SMEM((rows_dev // 128, 128), I32),
            pltpu.SemaphoreType.DMA,
        ],
        compiler_params=params(),
        cost_estimate=pl.CostEstimate(flops=100000000, bytes_accessed=4 << 20, transcendentals=0),
    )(ocean_dest.reshape(rows_dev // 128, 128), ocean_floe.reshape(rows_dev // 128, 128), forcing)
    state = jnp.concatenate(
        [jnp.transpose(centres, (2, 0, 1)), jnp.transpose(velocity, (2, 0, 1)), mass[None]], axis=0
    )
    lists = jnp.transpose(pairs[0, 0], (1, 0)).astype(F32)
    count = jnp.broadcast_to(pair_count.astype(F32), (1, 512))

    def pack_x(lo):
        return jnp.concatenate(
            [outline[lo : lo + H].reshape(H * FY, 512), as_rows(state[:, lo : lo + H], 2), lists, count,
             jnp.zeros((1, 512), F32)], axis=0
        )

    def unpack_x(got):
        return (
            got[: H * FY].reshape(H, FY, 512),
            got[H * FY : H * FY + 2].reshape(-1)[: 5 * H * FY].reshape(5, H, FY),
            got[H * FY + 2 : H * FY + 7],
        )

    north_o, north_s, north_l = unpack_x(moved(pack_x(FX - H), "gx", True))
    south_o, south_s, south_l = unpack_x(moved(pack_x(0), "gx", False))
    tall = jnp.concatenate([north_s, state, south_s], axis=1)
    own_l = jnp.concatenate([lists, count], axis=0)

    def pack_y(lo):
        cols = jnp.concatenate(
            [north_o[:, lo : lo + H], outline[:, lo : lo + H], south_o[:, lo : lo + H]], axis=0
        )
        return jnp.concatenate(
            [cols.reshape(R * H, 512), as_rows(tall[:, :, lo : lo + H], 1), north_l, own_l, south_l], axis=0
        )

    def unpack_y(got):
        return (
            got[: R * H].reshape(R, H, 512),
            got[R * H].reshape(-1)[: 5 * R * H].reshape(5, R, H),
            got[R * H + 1 : R * H + 16],
        )

    west, east, send = lax.optimization_barrier(
        (moved(pack_y(FY - H), "gy", True), moved(pack_y(0), "gy", False), send)
    )
    got = lax.all_to_all(
        send.reshape(DEVS, 1, BLK * 128), ("gx", "gy"), split_axis=0, concat_axis=0, tiled=True
    )
    west_o, west_s, west_l = unpack_y(west)
    east_o, east_s, east_l = unpack_y(east)
    west_o = jnp.pad(west_o, ((0, 0), (8 - H, 0), (0, 0)))
    east_o = jnp.pad(east_o, ((0, 0), (0, 8 - H), (0, 0)))
    wide = jnp.concatenate([west_s, tall, east_s], axis=2)
    wide = jnp.pad(wide, ((0, 0), (0, 0), (0, 128 - FY - 2 * H)))
    weight = jnp.where(wide[4:5] == 0.0, 1.0, wide[4:5])
    wide = jnp.concatenate([wide[:4], weight], axis=0)
    others = [north_l, south_l] + [block[5 * k : 5 * k + 5] for block in (west_l, east_l) for k in (0, 1, 2)]
    others = jnp.stack(others, axis=1)
    chunk_scratch = [
        pltpu.VMEM((6, CP, 128), F32),
        pltpu.VMEM((128, 128), F32),
        pltpu.VMEM((3, 128, 128), F32),
        pltpu.VMEM((6 * RP, 128), F32),
    ]
    tiles, words, counts, contact = pl.pallas_call(
        first_kernel,
        out_shape=[
            jax.ShapeDtypeStruct((NCH, 4, 128, 128), F32),
            jax.ShapeDtypeStruct((NCH, 128), I32),
            jax.ShapeDtypeStruct((2,), I32),
            jax.ShapeDtypeStruct((2, R, 128), F32),
        ],
        in_specs=[sspec(), vspec(), vspec(), vspec()] + [aspec()] * 5,
        out_specs=[aspec(), vspec(), sspec(), vspec()],
        scratch_shapes=[
            pltpu.VMEM((4, R, TW, 128), F32),
            pltpu.VMEM((NCH, 4, 128, 128), F32),
            pltpu.VMEM((4, 128, 128), F32),
            pltpu.VMEM((2, NCH, 128), I32),
            pltpu.SMEM((2, NCH, 128), I32),
            *chunk_scratch,
            pltpu.SemaphoreType.DMA((21,)),
            pltpu.SemaphoreType.DMA((NCH,)),
        ],
        compiler_params=params(),
        name="first_step",
        cost_estimate=pl.CostEstimate(flops=500000000, bytes_accessed=8 << 20, transcendentals=8 << 20),
    )(pair_count, jnp.transpose(pairs[0, 0], (1, 0)), others, wide, outline, north_o, south_o, west_o, east_o)

    ocean = pl.pallas_call(
        ocean_kernel,
        name="ocean_sum",
        out_shape=jax.ShapeDtypeStruct((2, R, 128), F32),
        in_specs=[vspec()] * 2,
        out_specs=vspec(),
        scratch_shapes=[
            pltpu.VMEM((FX * FY, 256), F32),
            pltpu.VMEM((5, DEVS // 16, 128), F32),
        ],
        compiler_params=params(),
        cost_estimate=pl.CostEstimate(flops=5000000000, bytes_accessed=5 << 20, transcendentals=0),
    )(got.reshape(DEVS * BLK, 128), response.reshape(FX * FY, NB))

    force = jnp.concatenate([contact + ocean, ocean], axis=0)
    w = 2 * H - 1
    low, high = moved(force[:, FX : FX + w], "gx", True), moved(force[:, 1 : 1 + w], "gx", False)
    force = force + jnp.pad(low, ((0, 0), (0, R - w), (0, 0))) + jnp.pad(high, ((0, 0), (R - w, 0), (0, 0)))
    low, high = moved(force[:, :, FY : FY + w], "gy", True), moved(force[:, :, 1 : 1 + w], "gy", False)
    c = FY + 2 * H
    force = force + jnp.pad(low, ((0, 0), (0, 0), (0, 128 - w))) + jnp.pad(high, ((0, 0), (0, 0), (c - w, 128 - c)))

    vel, shift = pl.pallas_call(
        later_kernel,
        name="later_steps",
        out_shape=[jax.ShapeDtypeStruct((FX, 2, FY), F32)] * 2,
        in_specs=[sspec(), vspec(), vspec(), vspec(), aspec()],
        out_specs=[vspec()] * 2,
        scratch_shapes=[
            pltpu.VMEM((NCH, 4, 128, 128), F32),
            *chunk_scratch,
            pltpu.VMEM((5, R, 128), F32),
            pltpu.SemaphoreType.DMA((NCH,)),
        ],
        compiler_params=params(),
        cost_estimate=pl.CostEstimate(flops=500000000, bytes_accessed=4 << 20, transcendentals=16 << 20),
    )(counts, force, wide, words, tiles)
    return jnp.transpose(vel, (0, 2, 1)), jnp.transpose(shift, (0, 2, 1))


def solution(mesh):
    return jax.shard_map(
        shards,
        mesh=mesh,
        in_specs=(
            P("gx", "gy", None),
            P("gx", "gy", None),
            P("gx", "gy", None),
            P("gx", "gy"),
            P("gx", "gy", None),
            P("gx", "gy", None, None),
            P("gx", "gy"),
            P(("gx", "gy"), None),
            P(("gx", "gy"), None),
            P(("gx", "gy")),
        ),
        out_specs=(P("gx", "gy", None), P("gx", "gy", None)),
        check_vma=False,
    )
```

```python
import math

import jax
import jax.numpy as jnp
from jax import lax
from jax.experimental import pallas as pl
from jax.experimental.pallas import tpu as pltpu
from jax.sharding import PartitionSpec as P

FX, FY, V, TILE, NB, PMAX = 32, 64, 256, 128, 64, 512
DEVS, CAP, BLK = 128, 40, 41
STEPS = 3
DT, DRAG = 0.1, 0.5
H = 2
R = FX + 2 * H
RP = 40
PACK = H * FY + 16
RK = 48
CP = 72
TW = FY + 16
PADC = 8 - H
NCH = 9 * PMAX // 128
NEIGH = ((-1, 0), (1, 0), (-1, -1), (0, -1), (1, -1), (-1, 1), (0, 1), (1, 1))
SC = math.sqrt(100.0 * math.log2(math.e))
F32, BF16, I32 = jnp.float32, jnp.bfloat16, jnp.int32
VMEM_BYTES = 52 * 1024 * 1024


def params():
    return pltpu.CompilerParams(vmem_limit_bytes=VMEM_BYTES)


def vspec():
    return pl.BlockSpec(memory_space=pltpu.VMEM)


def sspec():
    return pl.BlockSpec(memory_space=pltpu.SMEM)


def aspec():
    return pl.BlockSpec(memory_space=pl.ANY)


def nt(a, b):
    return lax.dot_general(a, b, (((1,), (1,)), ((), ())), preferred_element_type=F32)


def nn(a, b):
    return jnp.dot(a, b, preferred_element_type=F32)


def split3(x):
    a = x.astype(BF16).astype(F32)
    b = (x - a).astype(BF16).astype(F32)
    return a, b, (x - a - b).astype(BF16).astype(F32)


def pack_kernel(count_ref, pairs_ref, centres_ref, velocity_ref, mass_ref, outline_ref, up_ref, down_ref, state_ref, sems):
    copies = []
    for k, (out, lo) in enumerate(((up_ref, FX - H), (down_ref, 0))):
        for h in range(H):
            target = out.at[h * FY : h * FY + FY, :]
            copies.append(pltpu.make_async_copy(outline_ref.at[lo + h], target, sems.at[k * H + h]))
    for copy in copies:
        copy.start()
    at = H * FY
    tail = jnp.zeros((11, 512), F32)
    count = jnp.full((1, 512), count_ref[0, 0], I32).astype(F32)
    for k in range(2):
        state_ref[k] = centres_ref[:, k, :]
        state_ref[2 + k] = velocity_ref[:, k, :]
    state_ref[4] = mass_ref[...]
    for out, lo in ((up_ref, FX - H), (down_ref, 0)):
        out[at : at + 4, :] = pairs_ref[...].astype(F32)
        out[at + 4 : at + 5, :] = count
        out[at + 5 : at + 16, :] = tail
        for k in range(5):
            out[at + 5 + k * H : at + 5 + k * H + H, 0:FY] = state_ref[k, lo : lo + H, :]
    for copy in copies:
        copy.wait()


def send_kernel(dest_ref, floe_ref, rows_ref, out_ref, place_v, ids_v, place_s, sem):
    upper = (
        lax.broadcasted_iota(I32, (128, 128), 0) < lax.broadcasted_iota(I32, (128, 128), 1)
    ).astype(F32).astype(BF16)
    ones = jnp.ones((128, 128), BF16)
    index = lax.broadcasted_iota(I32, (128, 128), 0)
    blocks = dest_ref.shape[0]
    hots = [(index == dest_ref[k : k + 1, :]).astype(F32) for k in range(blocks)]
    hot16 = jnp.concatenate([hot.astype(BF16) for hot in hots], axis=0)
    before = nn(hot16, upper)
    full = nn(hot16, ones)
    carry = jnp.zeros((128, 128), F32)
    high, low, slots = [], [], []
    for k in range(blocks):
        rank = jnp.sum(hots[k] * (before[128 * k : 128 * k + 128] + carry), axis=0, keepdims=True)
        carry = carry + full[128 * k : 128 * k + 128]
        rank = rank.astype(I32)
        place_v[k : k + 1, :] = dest_ref[k : k + 1, :] * BLK + rank
        floe = floe_ref[k : k + 1, :] + 1
        slots.append((index == rank).astype(F32).astype(BF16))
        high.append((hots[k] * (floe >> 6).astype(F32)).astype(BF16))
        low.append((hots[k] * (floe & 63).astype(F32)).astype(BF16))
    slots = jnp.concatenate(slots, axis=1)
    ids = 64.0 * nt(jnp.concatenate(high, axis=1), slots) + nt(jnp.concatenate(low, axis=1), slots)
    ids_v[...] = ids
    copy = pltpu.make_async_copy(place_v, place_s, sem)
    copy.start()

    @pl.loop(0, out_ref.shape[0] // 128)
    def _(i):
        out_ref[pl.ds(pl.multiple_of(i * 128, 128), 128), :] = jnp.zeros((128, 128), F32)

    copy.wait()

    @pl.loop(0, rows_ref.shape[0] // 128)
    def _(k):
        for j in range(128):
            out_ref[pl.ds(place_s[k, j], 1), :] = rows_ref[pl.ds(k * 128 + j, 1), :]

    for d in range(DEVS):
        out_ref[d * BLK + CAP : d * BLK + CAP + 1, :] = ids_v[d : d + 1, :]


def ocean_kernel(rows_ref, resp_ref, out_ref, acc_ref, ids_ref):
    groups = DEVS // 16
    lane = lax.broadcasted_iota(I32, (groups, 128), 1)
    blocks = [jnp.zeros((groups, 128), F32) for _ in range(5)]
    for j in range(16):
        ids = rows_ref[pl.ds(j * BLK + CAP, groups, stride=16 * BLK), :]
        shift = (CAP * j) % 128
        if shift:
            ids = pltpu.roll(ids, shift, 1)
        for b in range(5):
            if CAP * j < 128 * b + 128 and CAP * j + CAP > 128 * b:
                place = lane + (128 * b - CAP * j)
                blocks[b] = jnp.where((place >= 0) & (place < CAP), ids, blocks[b])
    for b in range(5):
        ids_ref[b] = blocks[b]
    base16 = lax.broadcasted_iota(I32, (16, 128), 0).astype(F32)
    one, zero = jnp.ones((16, 128), BF16), jnp.zeros((16, 128), BF16)

    rows = jnp.concatenate([rows_ref[BLK * j : BLK * j + CAP, :] for j in range(DEVS)], axis=0)
    high = rows.astype(BF16)
    low = (rows - high.astype(F32)).astype(BF16)
    both = jnp.concatenate([high, low], axis=1)
    ids = [ids_ref[b, h : h + 1, :] for h in range(groups) for b in range(5)]
    for part in range(8):
        cols = []
        for row in ids:
            rel = jnp.broadcast_to(row - (part * 256 + 1.0), (16, 128)).astype(BF16)
            cols.append(
                jnp.concatenate(
                    [jnp.where((base16 + 16.0 * k).astype(BF16) == rel, one, zero) for k in range(16)], axis=0
                )
            )
        acc_ref[part * 256 : part * 256 + 256, :] = nn(jnp.concatenate(cols, axis=1), both)

    out_ref[...] = jnp.zeros_like(out_ref)
    srow = lax.broadcasted_iota(I32, (16, 128), 0)
    slane = lax.broadcasted_iota(I32, (16, 128), 1)
    pick = (((srow == 0) & (slane < NB)) | ((srow == 1) & (slane >= NB))).astype(F32).astype(BF16)
    inner = (slane >= H) & (slane < H + FY)

    for part in range(8):
        at = part * 256
        total = acc_ref[pl.ds(at, 256), 0:128] + acc_ref[pl.ds(at, 256), 128:256]
        resp = resp_ref[pl.ds(at, 256), :]
        a, b, c = split3(total * jnp.concatenate([resp, resp], axis=1))
        force = nt(pick, a.astype(BF16)) + nt(pick, b.astype(BF16)) + nt(pick, c.astype(BF16))
        for j in range(4):
            piece = force[:, (j // 2) * 128 : (j // 2) * 128 + 128]
            piece = pltpu.roll(piece, (H - 64 * (j % 2)) % 128, 1)
            piece = jnp.where(inner, piece, 0.0)
            for k in range(2):
                out_ref[k, part * 4 + j + H : part * 4 + j + H + 1, :] = piece[k : k + 1]


def put_shift(left_ref, plane_ref, now_ref):
    for k in range(2):
        plane_ref[0:R, :] = now_ref[k]
        for j, part in enumerate(split3(jnp.transpose(plane_ref[...])[0:CP])):
            left_ref[3 * k + j] = part


def contact_chunk(c, half_at, words_ref, tiles_ref, left_ref, b_ref, acc_ref):
    word = words_ref[pl.ds(c, 1), :]
    ok = word >= 0
    rows = jnp.concatenate([(word >> 7) & 63, (word >> 20) & 63], axis=1)
    cols = jnp.concatenate([word & 127, (word >> 13) & 127], axis=1)
    code = (word >> 28) & 7
    code9 = code + (code >= 4).astype(I32)
    step = (code9 >= 3).astype(I32) + (code9 >= 6).astype(I32)
    dirx = (step - 1).astype(F32)
    diry = (code9 - 3 * step - 1).astype(F32)
    row_hot = (lax.broadcasted_iota(I32, (RK, 256), 0) == rows).astype(F32)
    row_hot16 = row_hot.astype(BF16)
    col_hot = lax.broadcasted_iota(I32, (CP, 256), 0) == cols
    lanes = lax.broadcasted_iota(I32, (128, 256), 0) == cols
    diffs = []
    for k in range(2):
        left = jnp.concatenate([left_ref[3 * k + j, :, 0:RK] for j in range(3)], axis=0)
        part = nn(left.astype(BF16), row_hot16)
        part = part[0:CP] + part[CP : 2 * CP] + part[2 * CP : 3 * CP]
        part = jnp.sum(jnp.where(col_hot, part, 0.0), axis=0, keepdims=True)
        diffs.append(part[:, 0:128] - part[:, 128:256])
    dx = (dirx - diffs[0]) * SC
    dy = (diry - diffs[1]) * SC
    px = tiles_ref[c, 2] + dx
    py = tiles_ref[c, 3] + dy
    b_ref[0] = 2.0 * px
    b_ref[1] = 2.0 * py
    b_ref[2] = -(px * px + py * py)
    turns = jnp.where(c == half_at, TILE // 64, TILE // 32)

    @pl.when(c == half_at)
    def _():
        left_half = lax.broadcasted_iota(I32, (64, 128), 1) < 64
        for k in range(3):
            b_ref[k, 0:64, :] = jnp.where(left_half, b_ref[k, 0:64, :], b_ref[k, 64:128, :])

    force_x = jnp.zeros((8, 128), F32)
    force_y = jnp.zeros((8, 128), F32)
    back_x = jnp.zeros((8, 128), F32)
    back_y = jnp.zeros((8, 128), F32)
    for half in range(2):
        ax = [tiles_ref[c, 0, half * 64 + 8 * k : half * 64 + 8 * k + 8, :] for k in range(8)]
        ay = [tiles_ref[c, 1, half * 64 + 8 * k : half * 64 + 8 * k + 8, :] for k in range(8)]
        na = [-(x * x + y * y) for x, y in zip(ax, ay)]

        def body(i, carry):
            sums, bx_sum, by_sum = carry
            sums = list(sums)
            for j in range(32):
                w = i * 32 + j
                bx = jnp.broadcast_to(b_ref[0, pl.ds(w, 1), :], (8, 128))
                by = jnp.broadcast_to(b_ref[1, pl.ds(w, 1), :], (8, 128))
                nb = jnp.broadcast_to(b_ref[2, pl.ds(w, 1), :], (8, 128))
                weights = [jnp.exp2((ax[k] * bx + ay[k] * by) + (na[k] + nb)) for k in range(8)]
                sums = [s + t for s, t in zip(sums, weights)]
                while len(weights) > 1:
                    weights = [weights[k] + weights[k + 1] for k in range(0, len(weights), 2)]
                bx_sum = bx_sum + weights[0] * bx
                by_sum = by_sum + weights[0] * by
            return tuple(sums), bx_sum, by_sum

        sums, back_x, back_y = lax.fori_loop(
            0, turns, body, (tuple(jnp.zeros((8, 128), F32) for _ in range(8)), back_x, back_y)
        )
        for k in range(8):
            force_x = force_x + ax[k] * sums[k]
            force_y = force_y + ay[k] * sums[k]
    fx = jnp.sum(force_x - 0.5 * back_x, axis=0, keepdims=True) * (1.0 / SC)
    fy = jnp.sum(force_y - 0.5 * back_y, axis=0, keepdims=True) * (1.0 / SC)
    parts = split3(jnp.where(ok, fx, 0.0)) + split3(jnp.where(ok, fy, 0.0))
    spread = [row_hot[0:RP] * jnp.concatenate([part, -part], axis=1) for part in parts]
    acc_ref[...] += nt(jnp.concatenate(spread, axis=0).astype(BF16), lanes.astype(F32).astype(BF16))


def acc_plane(acc_ref, k):
    at = 3 * RP * k
    return acc_ref[at : at + R, :] + acc_ref[at + RP : at + RP + R, :] + acc_ref[at + 2 * RP : at + 2 * RP + R, :]


def code_steps(code):
    code9 = code + (code >= 4).astype(I32)
    step = (code9 >= 3).astype(I32) + (code9 >= 6).astype(I32)
    return step - 1, code9 - 3 * step - 1


def pair_words(local, code, mine, theirs, count, di, dj, extra):
    step_x, step_y = code_steps(code)
    row = (local >> 6) + di * FX
    col = (local & 63) + dj * FY
    prow = row + step_x
    pcol = col + step_y
    row_all = prow + lax.axis_index("gx") * FX
    col_all = pcol + lax.axis_index("gy") * FY
    ok = lax.broadcasted_iota(I32, local.shape, 1) < count
    ok = ok & (row_all >= 0) & (row_all < lax.axis_size("gx") * FX)
    ok = ok & (col_all >= 0) & (col_all < lax.axis_size("gy") * FY)
    if extra:
        near = (row >= -1) & (row <= FX) & (col >= -1) & (col <= FY)
        ok = ok & (near | ((prow >= -1) & (prow <= FX) & (pcol >= -1) & (pcol <= FY)))
    word = (row + H) * 128 + col + H + (((prow + H) * 128 + pcol + H) << 13)
    return jnp.where(ok, word + (mine << 26) + (theirs << 27) + (code << 28), -1)


def first_kernel(
    count_ref, own_ref, lists_ref, state_ref, outline_ref, north_ref, south_ref, west_ref, east_ref,
    tiles_out, words_out, count_out, force_out,
    table, tiles, stage, place_v, place_s, left_ref, plane_ref, b_ref, acc_ref, sems, tile_sems,
):
    copies = []
    for q in range(4):
        lanes = slice(q * 128, q * 128 + 128)
        for k, (source, target) in enumerate((
            (outline_ref, table.at[q, H : H + FX, 8 : 8 + FY, :]),
            (north_ref, table.at[q, 0:H, 8 : 8 + FY, :]),
            (south_ref, table.at[q, H + FX : R, 8 : 8 + FY, :]),
            (west_ref, table.at[q, :, 0:8, :]),
            (east_ref, table.at[q, :, 8 + FY : 16 + FY, :]),
        )):
            copies.append(pltpu.make_async_copy(source.at[:, :, lanes], target, sems.at[5 * q + k]))
    for copy in copies:
        copy.start()
    live = count_ref[0, 0]
    word = pair_words(*[own_ref[k : k + 1, :] for k in range(4)], live, 0, 0, False)
    words_out[...] = jnp.full(words_out.shape, -1, I32)
    for b in range(4):
        words_out[b : b + 1, :] = word[:, 128 * b : 128 * b + 128]
    mine = (live + 127) >> 7
    number = lax.broadcasted_iota(I32, (8, PMAX), 0)
    di, dj = jnp.zeros((8, PMAX), I32), jnp.zeros((8, PMAX), I32)
    for k, (i, j) in enumerate(NEIGH):
        di = jnp.where(number == k, i, di)
        dj = jnp.where(number == k, j, dj)
    word = pair_words(*[lists_ref[k].astype(I32) for k in range(5)], di, dj, True)
    flags = (word >= 0).astype(F32)
    upper = (
        lax.broadcasted_iota(I32, (PMAX, PMAX), 0) < lax.broadcasted_iota(I32, (PMAX, PMAX), 1)
    ).astype(F32).astype(BF16)
    rank = nn(flags.astype(BF16), upper)
    base = jnp.zeros((1, 1), F32)
    ranks = []
    for k in range(8):
        ranks.append(jnp.where(flags[k : k + 1] > 0.0, rank[k : k + 1] + base, -1.0).astype(I32))
        base = base + jnp.sum(flags[k : k + 1], axis=1, keepdims=True)
    found_all = jnp.sum(flags).astype(I32)
    extra = (found_all + 127) >> 7
    total = mine + extra
    whole = (found_all + 63) >> 7
    slot = lax.broadcasted_iota(I32, (128, PMAX), 0)
    srow = lax.broadcasted_iota(I32, (16, PMAX), 0)
    pieces = []
    for k in range(8):
        one = word[k : k + 1]
        piece = jnp.where(srow == 0, one & 255, jnp.where(srow == 1, (one >> 8) & 255, 0))
        piece = jnp.where(srow == 2, (one >> 16) & 255, jnp.where(srow == 3, (one >> 24) & 127, piece))
        piece = jnp.where(srow == 4, 1, piece)
        pieces.append(piece.astype(F32).astype(BF16))

    @pl.loop(0, extra)
    def _(i):
        found = jnp.zeros((16, 128), F32)
        want = jnp.where(i >= whole, slot & 63, slot)
        for k in range(8):
            found = found + nt(pieces[k], (want == ranks[k] - i * 128).astype(F32).astype(BF16))
        found = found.astype(I32)
        value = found[0:1] + (found[1:2] << 8) + (found[2:3] << 16) + (found[3:4] << 24)
        words_out[pl.ds(mine + i, 1), :] = jnp.where(found[4:5] > 0, value, -1)

    word = jnp.maximum(words_out[...], 0)
    own = ((word >> 7) & 63) * TW + (word & 127) + PADC
    other = ((word >> 20) & 63) * TW + ((word >> 13) & 127) + PADC
    place_v[0] = own + ((word >> 26) & 1) * (R * TW)
    place_v[1] = other + ((word >> 27) & 1) * (R * TW)
    copy = pltpu.make_async_copy(place_v, place_s, sems.at[20])
    copy.start()
    count_out[0] = total
    count_out[1] = jnp.where(extra > whole, total - 1, -1)
    for piece in copies:
        piece.wait()
    copy.wait()
    flat = table.reshape(4 * R * TW, 128)

    @pl.loop(0, total)
    def _(c):
        @pl.loop(0, 16)
        def _(i):
            for j in range(8):
                at = i * 8 + j
                own = place_s[0, c, at]
                other = place_s[1, c, at]
                stage[0, pl.ds(at, 1), :] = flat[pl.ds(own, 1), :]
                stage[1, pl.ds(at, 1), :] = flat[pl.ds(own + 2 * R * TW, 1), :]
                stage[2, pl.ds(at, 1), :] = flat[pl.ds(other, 1), :]
                stage[3, pl.ds(at, 1), :] = flat[pl.ds(other + 2 * R * TW, 1), :]

        for k in range(4):
            tiles[c, k] = jnp.transpose(stage[k]) * SC
        pltpu.make_async_copy(tiles.at[c], tiles_out.at[c], tile_sems.at[c]).start()

    plane_ref[...] = jnp.zeros_like(plane_ref)
    put_shift(left_ref, plane_ref, state_ref)
    acc_ref[...] = jnp.zeros_like(acc_ref)

    @pl.loop(0, mine)
    def _(c):
        contact_chunk(c, -1, words_out, tiles, left_ref, b_ref, acc_ref)

    for k in range(2):
        force_out[k] = acc_plane(acc_ref, k)

    @pl.loop(0, total)
    def _(c):
        pltpu.make_async_copy(tiles.at[c], tiles_out.at[c], tile_sems.at[c]).wait()


def later_kernel(
    count_ref, force_ref, state_ref, words_ref, tiles_in, vel_out, shift_out,
    tiles, left_ref, plane_ref, b_ref, acc_ref, now_ref, tile_sems,
):
    total = count_ref[0]
    half_at = count_ref[1]

    @pl.loop(0, total)
    def _(c):
        pltpu.make_async_copy(tiles_in.at[c], tiles.at[c], tile_sems.at[c]).start()

    now_ref[...] = state_ref[...]

    def update(forces):
        scale = DT / now_ref[4]
        for k in range(2):
            vel = now_ref[2 + k]
            vel = vel + (forces[k] - DRAG * vel) * scale
            now_ref[2 + k] = vel
            now_ref[k] = now_ref[k] + DT * vel

    update([force_ref[0], force_ref[1]])
    plane_ref[...] = jnp.zeros_like(plane_ref)

    @pl.loop(0, total)
    def _(c):
        pltpu.make_async_copy(tiles_in.at[c], tiles.at[c], tile_sems.at[c]).wait()

    @pl.loop(1, STEPS)
    def _(step):
        put_shift(left_ref, plane_ref, now_ref)
        acc_ref[...] = jnp.zeros_like(acc_ref)

        @pl.loop(0, total)
        def _(c):
            contact_chunk(c, half_at, words_ref, tiles, left_ref, b_ref, acc_ref)

        update([acc_plane(acc_ref, k) + force_ref[2 + k] for k in range(2)])

    for out, base in ((shift_out, 0), (vel_out, 2)):
        for k in range(2):
            plane_ref[0:R, :] = pltpu.roll(now_ref[base + k], 128 - H, 1)
            for r in range(FX):
                out[r, k : k + 1, :] = plane_ref[r + H : r + H + 1, 0:FY]


def moved(x, axis, up):
    count = lax.axis_size(axis)
    pairs = [(i, i + 1) if up else (i + 1, i) for i in range(count - 1)]
    return lax.ppermute(x, axis, pairs)


def as_rows(x, rows):
    flat = x.reshape(-1)
    return jnp.pad(flat, (0, rows * 512 - flat.shape[0])).reshape(rows, 512)


def shards(
    outline, centres, velocity, mass, response, pairs, pair_count, forcing, ocean_dest, ocean_floe
):
    rows_dev = forcing.shape[0]
    send = pl.pallas_call(
        send_kernel,
        name="send_rows",
        out_shape=jax.ShapeDtypeStruct((DEVS * BLK, 128), F32),
        in_specs=[vspec()] * 3,
        out_specs=vspec(),
        scratch_shapes=[
            pltpu.VMEM((rows_dev // 128, 128), I32),
            pltpu.VMEM((DEVS, 128), F32),
            pltpu.SMEM((rows_dev // 128, 128), I32),
            pltpu.SemaphoreType.DMA,
        ],
        compiler_params=params(),
        cost_estimate=pl.CostEstimate(flops=100000000, bytes_accessed=4 << 20, transcendentals=0),
    )(ocean_dest.reshape(rows_dev // 128, 128), ocean_floe.reshape(rows_dev // 128, 128), forcing)
    pair_rows = jnp.transpose(pairs[0, 0], (1, 0))
    up, down, state = pl.pallas_call(
        pack_kernel,
        name="pack_rows",
        out_shape=[jax.ShapeDtypeStruct((PACK, 512), F32)] * 2 + [jax.ShapeDtypeStruct((5, FX, FY), F32)],
        in_specs=[sspec()] + [vspec()] * 4 + [aspec()],
        out_specs=[vspec()] * 3,
        scratch_shapes=[pltpu.SemaphoreType.DMA((2 * H,))],
        compiler_params=params(),
        cost_estimate=pl.CostEstimate(flops=1000000, bytes_accessed=1 << 20, transcendentals=0),
    )(pair_count, pair_rows, jnp.transpose(centres, (0, 2, 1)), jnp.transpose(velocity, (0, 2, 1)), mass, outline)

    def unpack_x(got):
        at = H * FY
        return (
            got[:at].reshape(H, FY, 512),
            got[at + 5 : at + 5 + 5 * H, :FY].reshape(5, H, FY),
            got[at : at + 5],
        )

    north_o, north_s, north_l = unpack_x(moved(up, "gx", True))
    south_o, south_s, south_l = unpack_x(moved(down, "gx", False))
    tall = jnp.concatenate([north_s, state, south_s], axis=1)
    own_l = up[H * FY : H * FY + 5]

    def pack_y(lo):
        cols = jnp.concatenate(
            [north_o[:, lo : lo + H], outline[:, lo : lo + H], south_o[:, lo : lo + H]], axis=0
        )
        return jnp.concatenate(
            [cols.reshape(R * H, 512), as_rows(tall[:, :, lo : lo + H], 1), north_l, own_l, south_l], axis=0
        )

    def unpack_y(got):
        return (
            got[: R * H].reshape(R, H, 512),
            got[R * H].reshape(-1)[: 5 * R * H].reshape(5, R, H),
            got[R * H + 1 : R * H + 16],
        )

    west, east, send = lax.optimization_barrier(
        (moved(pack_y(FY - H), "gy", True), moved(pack_y(0), "gy", False), send)
    )
    got = lax.all_to_all(
        send.reshape(DEVS, 1, BLK * 128), ("gx", "gy"), split_axis=0, concat_axis=0, tiled=True
    )
    west_o, west_s, west_l = unpack_y(west)
    east_o, east_s, east_l = unpack_y(east)
    west_o = jnp.pad(west_o, ((0, 0), (8 - H, 0), (0, 0)))
    east_o = jnp.pad(east_o, ((0, 0), (0, 8 - H), (0, 0)))
    wide = jnp.concatenate([west_s, tall, east_s], axis=2)
    wide = jnp.pad(wide, ((0, 0), (0, 0), (0, 128 - FY - 2 * H)))
    weight = jnp.where(wide[4:5] == 0.0, 1.0, wide[4:5])
    wide = jnp.concatenate([wide[:4], weight], axis=0)
    others = [north_l, south_l] + [block[5 * k : 5 * k + 5] for block in (west_l, east_l) for k in (0, 1, 2)]
    others = jnp.stack(others, axis=1)
    chunk_scratch = [
        pltpu.VMEM((6, CP, 128), F32),
        pltpu.VMEM((128, 128), F32),
        pltpu.VMEM((3, 128, 128), F32),
        pltpu.VMEM((6 * RP, 128), F32),
    ]
    tiles, words, counts, contact = pl.pallas_call(
        first_kernel,
        out_shape=[
            jax.ShapeDtypeStruct((NCH, 4, 128, 128), F32),
            jax.ShapeDtypeStruct((NCH, 128), I32),
            jax.ShapeDtypeStruct((2,), I32),
            jax.ShapeDtypeStruct((2, R, 128), F32),
        ],
        in_specs=[sspec(), vspec(), vspec(), vspec()] + [aspec()] * 5,
        out_specs=[aspec(), vspec(), sspec(), vspec()],
        scratch_shapes=[
            pltpu.VMEM((4, R, TW, 128), F32),
            pltpu.VMEM((NCH, 4, 128, 128), F32),
            pltpu.VMEM((4, 128, 128), F32),
            pltpu.VMEM((2, NCH, 128), I32),
            pltpu.SMEM((2, NCH, 128), I32),
            *chunk_scratch,
            pltpu.SemaphoreType.DMA((21,)),
            pltpu.SemaphoreType.DMA((NCH,)),
        ],
        compiler_params=params(),
        name="first_step",
        cost_estimate=pl.CostEstimate(flops=500000000, bytes_accessed=8 << 20, transcendentals=8 << 20),
    )(pair_count, pair_rows, others, wide, outline, north_o, south_o, west_o, east_o)

    ocean = pl.pallas_call(
        ocean_kernel,
        name="ocean_sum",
        out_shape=jax.ShapeDtypeStruct((2, R, 128), F32),
        in_specs=[vspec()] * 2,
        out_specs=vspec(),
        scratch_shapes=[
            pltpu.VMEM((FX * FY, 256), F32),
            pltpu.VMEM((5, DEVS // 16, 128), F32),
        ],
        compiler_params=params(),
        cost_estimate=pl.CostEstimate(flops=5000000000, bytes_accessed=5 << 20, transcendentals=0),
    )(got.reshape(DEVS * BLK, 128), response.reshape(FX * FY, NB))

    force = jnp.concatenate([contact + ocean, ocean], axis=0)
    w = 2 * H - 1
    low, high = moved(force[:, FX : FX + w], "gx", True), moved(force[:, 1 : 1 + w], "gx", False)
    force = force + jnp.pad(low, ((0, 0), (0, R - w), (0, 0))) + jnp.pad(high, ((0, 0), (R - w, 0), (0, 0)))
    low, high = moved(force[:, :, FY : FY + w], "gy", True), moved(force[:, :, 1 : 1 + w], "gy", False)
    c = FY + 2 * H
    force = force + jnp.pad(low, ((0, 0), (0, 0), (0, 128 - w))) + jnp.pad(high, ((0, 0), (0, 0), (c - w, 128 - c)))

    vel, shift = pl.pallas_call(
        later_kernel,
        name="later_steps",
        out_shape=[jax.ShapeDtypeStruct((FX, 2, FY), F32)] * 2,
        in_specs=[sspec(), vspec(), vspec(), vspec(), aspec()],
        out_specs=[vspec()] * 2,
        scratch_shapes=[
            pltpu.VMEM((NCH, 4, 128, 128), F32),
            *chunk_scratch,
            pltpu.VMEM((5, R, 128), F32),
            pltpu.SemaphoreType.DMA((NCH,)),
        ],
        compiler_params=params(),
        cost_estimate=pl.CostEstimate(flops=500000000, bytes_accessed=4 << 20, transcendentals=16 << 20),
    )(counts, force, wide, words, tiles)
    return jnp.transpose(vel, (0, 2, 1)), jnp.transpose(shift, (0, 2, 1))


def solution(mesh):
    return jax.shard_map(
        shards,
        mesh=mesh,
        in_specs=(
            P("gx", "gy", None),
            P("gx", "gy", None),
            P("gx", "gy", None),
            P("gx", "gy"),
            P("gx", "gy", None),
            P("gx", "gy", None, None),
            P("gx", "gy"),
            P(("gx", "gy"), None),
            P(("gx", "gy"), None),
            P(("gx", "gy")),
        ),
        out_specs=(P("gx", "gy", None), P("gx", "gy", None)),
        check_vma=False,
    )
```

```python
import math

import jax
import jax.numpy as jnp
from jax import lax
from jax.experimental import pallas as pl
from jax.experimental.pallas import tpu as pltpu
from jax.sharding import PartitionSpec as P

FX, FY, V, TILE, NB, PMAX = 32, 64, 256, 128, 64, 512
DEVS, CAP, BLK = 128, 40, 41
STEPS = 3
DT, DRAG = 0.1, 0.5
H = 2
R = FX + 2 * H
RP = 40
PACK = H * FY + 16
RK = 48
CP = 72
TW = FY + 16
PADC = 8 - H
NCH = 9 * PMAX // 128
OWN = PMAX // 128
NEIGH = ((0, 0), (-1, 0), (1, 0), (-1, -1), (0, -1), (1, -1), (-1, 1), (0, 1), (1, 1))
SC = math.sqrt(100.0 * math.log2(math.e))
F32, BF16, I32 = jnp.float32, jnp.bfloat16, jnp.int32
VMEM_BYTES = 52 * 1024 * 1024


def params():
    return pltpu.CompilerParams(vmem_limit_bytes=VMEM_BYTES)


def vspec():
    return pl.BlockSpec(memory_space=pltpu.VMEM)


def sspec():
    return pl.BlockSpec(memory_space=pltpu.SMEM)


def aspec():
    return pl.BlockSpec(memory_space=pl.ANY)


def nt(a, b):
    return lax.dot_general(a, b, (((1,), (1,)), ((), ())), preferred_element_type=F32)


def nn(a, b):
    return jnp.dot(a, b, preferred_element_type=F32)


def split3(x):
    a = x.astype(BF16).astype(F32)
    b = (x - a).astype(BF16).astype(F32)
    return a, b, (x - a - b).astype(BF16).astype(F32)


def pack_kernel(count_ref, pairs_ref, centres_ref, velocity_ref, mass_ref, outline_ref, up_ref, down_ref, state_ref, sems):
    copies = []
    for k, (out, lo) in enumerate(((up_ref, FX - H), (down_ref, 0))):
        for h in range(H):
            target = out.at[h * FY : h * FY + FY, :]
            copies.append(pltpu.make_async_copy(outline_ref.at[lo + h], target, sems.at[k * H + h]))
    for copy in copies:
        copy.start()
    at = H * FY
    tail = jnp.zeros((11, 512), F32)
    count = jnp.full((1, 512), count_ref[0, 0], I32).astype(F32)
    for k in range(2):
        state_ref[k] = centres_ref[:, k, :]
        state_ref[2 + k] = velocity_ref[:, k, :]
    state_ref[4] = mass_ref[...]
    for out, lo in ((up_ref, FX - H), (down_ref, 0)):
        out[at : at + 4, :] = pairs_ref[...].astype(F32)
        out[at + 4 : at + 5, :] = count
        out[at + 5 : at + 16, :] = tail
        for k in range(5):
            out[at + 5 + k * H : at + 5 + k * H + H, 0:FY] = state_ref[k, lo : lo + H, :]
    for copy in copies:
        copy.wait()


def send_kernel(dest_ref, floe_ref, rows_ref, out_ref, place_v, ids_v, place_s, sem):
    upper = (
        lax.broadcasted_iota(I32, (128, 128), 0) < lax.broadcasted_iota(I32, (128, 128), 1)
    ).astype(F32).astype(BF16)
    ones = jnp.ones((128, 128), BF16)
    index = lax.broadcasted_iota(I32, (128, 128), 0)
    blocks = dest_ref.shape[0]
    hots = [(index == dest_ref[k : k + 1, :]).astype(F32) for k in range(blocks)]
    hot16 = jnp.concatenate([hot.astype(BF16) for hot in hots], axis=0)
    before = nn(hot16, upper)
    full = nn(hot16, ones)
    carry = jnp.zeros((128, 128), F32)
    high, low, slots = [], [], []
    for k in range(blocks):
        rank = jnp.sum(hots[k] * (before[128 * k : 128 * k + 128] + carry), axis=0, keepdims=True)
        carry = carry + full[128 * k : 128 * k + 128]
        rank = rank.astype(I32)
        place_v[k : k + 1, :] = dest_ref[k : k + 1, :] * BLK + rank
        floe = floe_ref[k : k + 1, :] + 1
        slots.append((index == rank).astype(F32).astype(BF16))
        high.append((hots[k] * (floe >> 6).astype(F32)).astype(BF16))
        low.append((hots[k] * (floe & 63).astype(F32)).astype(BF16))
    slots = jnp.concatenate(slots, axis=1)
    ids = 64.0 * nt(jnp.concatenate(high, axis=1), slots) + nt(jnp.concatenate(low, axis=1), slots)
    ids_v[...] = ids
    copy = pltpu.make_async_copy(place_v, place_s, sem)
    copy.start()

    @pl.loop(0, out_ref.shape[0] // 128)
    def _(i):
        out_ref[pl.ds(pl.multiple_of(i * 128, 128), 128), :] = jnp.zeros((128, 128), F32)

    copy.wait()

    @pl.loop(0, rows_ref.shape[0] // 128)
    def _(k):
        for j in range(128):
            out_ref[pl.ds(place_s[k, j], 1), :] = rows_ref[pl.ds(k * 128 + j, 1), :]

    for d in range(DEVS):
        out_ref[d * BLK + CAP : d * BLK + CAP + 1, :] = ids_v[d : d + 1, :]


def ocean_kernel(rows_ref, resp_ref, out_ref, acc_ref, ids_ref):
    groups = DEVS // 16
    lane = lax.broadcasted_iota(I32, (groups, 128), 1)
    blocks = [jnp.zeros((groups, 128), F32) for _ in range(5)]
    for j in range(16):
        ids = rows_ref[pl.ds(j * BLK + CAP, groups, stride=16 * BLK), :]
        shift = (CAP * j) % 128
        if shift:
            ids = pltpu.roll(ids, shift, 1)
        for b in range(5):
            if CAP * j < 128 * b + 128 and CAP * j + CAP > 128 * b:
                place = lane + (128 * b - CAP * j)
                blocks[b] = jnp.where((place >= 0) & (place < CAP), ids, blocks[b])
    for b in range(5):
        ids_ref[b] = blocks[b]
    base16 = lax.broadcasted_iota(I32, (16, 128), 0).astype(F32)
    one, zero = jnp.ones((16, 128), BF16), jnp.zeros((16, 128), BF16)

    rows = jnp.concatenate([rows_ref[BLK * j : BLK * j + CAP, :] for j in range(DEVS)], axis=0)
    high = rows.astype(BF16)
    low = (rows - high.astype(F32)).astype(BF16)
    both = jnp.concatenate([high, low], axis=1)
    ids = [ids_ref[b, h : h + 1, :] for h in range(groups) for b in range(5)]
    for part in range(8):
        cols = []
        for row in ids:
            rel = jnp.broadcast_to(row - (part * 256 + 1.0), (16, 128)).astype(BF16)
            cols.append(
                jnp.concatenate(
                    [jnp.where((base16 + 16.0 * k).astype(BF16) == rel, one, zero) for k in range(16)], axis=0
                )
            )
        acc_ref[part * 256 : part * 256 + 256, :] = nn(jnp.concatenate(cols, axis=1), both)

    out_ref[...] = jnp.zeros_like(out_ref)
    srow = lax.broadcasted_iota(I32, (16, 128), 0)
    slane = lax.broadcasted_iota(I32, (16, 128), 1)
    pick = (((srow == 0) & (slane < NB)) | ((srow == 1) & (slane >= NB))).astype(F32).astype(BF16)
    inner = (slane >= H) & (slane < H + FY)

    for part in range(8):
        at = part * 256
        total = acc_ref[pl.ds(at, 256), 0:128] + acc_ref[pl.ds(at, 256), 128:256]
        resp = resp_ref[pl.ds(at, 256), :]
        a, b, c = split3(total * jnp.concatenate([resp, resp], axis=1))
        force = nt(pick, a.astype(BF16)) + nt(pick, b.astype(BF16)) + nt(pick, c.astype(BF16))
        for j in range(4):
            piece = force[:, (j // 2) * 128 : (j // 2) * 128 + 128]
            piece = pltpu.roll(piece, (H - 64 * (j % 2)) % 128, 1)
            piece = jnp.where(inner, piece, 0.0)
            for k in range(2):
                out_ref[k, part * 4 + j + H : part * 4 + j + H + 1, :] = piece[k : k + 1]


def put_shift(left_ref, plane_ref, planes):
    for k in range(2):
        plane_ref[0:R, :] = planes[k]
        for j, part in enumerate(split3(jnp.transpose(plane_ref[...])[0:CP])):
            left_ref[3 * k + j] = part


def contact_chunk(c, half_at, live, words_ref, tiles_ref, left_ref, b_ref, acc_ref):
    word = words_ref[pl.ds(c, 1), :]
    lane = lax.broadcasted_iota(I32, (1, 128), 1)
    ok = (word >= 0) & (c * 128 + jnp.where(c == half_at, lane & 63, lane) < live)
    rows = jnp.concatenate([(word >> 7) & 63, (word >> 20) & 63], axis=1)
    cols = jnp.concatenate([word & 127, (word >> 13) & 127], axis=1)
    code = (word >> 28) & 7
    code9 = code + (code >= 4).astype(I32)
    step = (code9 >= 3).astype(I32) + (code9 >= 6).astype(I32)
    dirx = (step - 1).astype(F32)
    diry = (code9 - 3 * step - 1).astype(F32)
    row_hot = (lax.broadcasted_iota(I32, (RK, 256), 0) == rows).astype(F32)
    row_hot16 = row_hot.astype(BF16)
    col_hot = lax.broadcasted_iota(I32, (CP, 256), 0) == cols
    lanes = lax.broadcasted_iota(I32, (128, 256), 0) == cols
    diffs = []
    for k in range(2):
        left = jnp.concatenate([left_ref[3 * k + j, :, 0:RK] for j in range(3)], axis=0)
        part = nn(left.astype(BF16), row_hot16)
        part = part[0:CP] + part[CP : 2 * CP] + part[2 * CP : 3 * CP]
        part = jnp.sum(jnp.where(col_hot, part, 0.0), axis=0, keepdims=True)
        diffs.append(part[:, 0:128] - part[:, 128:256])
    dx = (dirx - diffs[0]) * SC
    dy = (diry - diffs[1]) * SC
    px = tiles_ref[c, 2] + dx
    py = tiles_ref[c, 3] + dy
    b_ref[0] = 2.0 * px
    b_ref[1] = 2.0 * py
    b_ref[2] = -(px * px + py * py)
    turns = jnp.where(c == half_at, TILE // 64, TILE // 32)

    @pl.when(c == half_at)
    def _():
        left_half = lax.broadcasted_iota(I32, (64, 128), 1) < 64
        for k in range(3):
            b_ref[k, 0:64, :] = jnp.where(left_half, b_ref[k, 0:64, :], b_ref[k, 64:128, :])

    force_x = jnp.zeros((8, 128), F32)
    force_y = jnp.zeros((8, 128), F32)
    back_x = jnp.zeros((8, 128), F32)
    back_y = jnp.zeros((8, 128), F32)
    for half in range(2):
        ax = [tiles_ref[c, 0, half * 64 + 8 * k : half * 64 + 8 * k + 8, :] for k in range(8)]
        ay = [tiles_ref[c, 1, half * 64 + 8 * k : half * 64 + 8 * k + 8, :] for k in range(8)]
        na = [-(x * x + y * y) for x, y in zip(ax, ay)]

        def body(i, carry):
            sums, bx_sum, by_sum = carry
            sums = list(sums)
            for j in range(32):
                w = i * 32 + j
                bx = jnp.broadcast_to(b_ref[0, pl.ds(w, 1), :], (8, 128))
                by = jnp.broadcast_to(b_ref[1, pl.ds(w, 1), :], (8, 128))
                nb = jnp.broadcast_to(b_ref[2, pl.ds(w, 1), :], (8, 128))
                weights = [jnp.exp2((ax[k] * bx + ay[k] * by) + (na[k] + nb)) for k in range(8)]
                sums = [s + t for s, t in zip(sums, weights)]
                while len(weights) > 1:
                    weights = [weights[k] + weights[k + 1] for k in range(0, len(weights), 2)]
                bx_sum = bx_sum + weights[0] * bx
                by_sum = by_sum + weights[0] * by
            return tuple(sums), bx_sum, by_sum

        sums, back_x, back_y = lax.fori_loop(
            0, turns, body, (tuple(jnp.zeros((8, 128), F32) for _ in range(8)), back_x, back_y)
        )
        for k in range(8):
            force_x = force_x + ax[k] * sums[k]
            force_y = force_y + ay[k] * sums[k]
    fx = jnp.sum(force_x - 0.5 * back_x, axis=0, keepdims=True) * (1.0 / SC)
    fy = jnp.sum(force_y - 0.5 * back_y, axis=0, keepdims=True) * (1.0 / SC)
    parts = split3(jnp.where(ok, fx, 0.0)) + split3(jnp.where(ok, fy, 0.0))
    spread = [row_hot[0:RP] * jnp.concatenate([part, -part], axis=1) for part in parts]
    acc_ref[...] += nt(jnp.concatenate(spread, axis=0).astype(BF16), lanes.astype(F32).astype(BF16))


def acc_plane(acc_ref, k):
    at = 3 * RP * k
    return acc_ref[at : at + R, :] + acc_ref[at + RP : at + RP + R, :] + acc_ref[at + 2 * RP : at + 2 * RP + R, :]


def code_steps(code):
    code9 = code + (code >= 4).astype(I32)
    step = (code9 >= 3).astype(I32) + (code9 >= 6).astype(I32)
    return step - 1, code9 - 3 * step - 1


def pair_words(local, code, mine, theirs, count, di, dj):
    step_x, step_y = code_steps(code)
    row = (local >> 6) + di * FX
    col = (local & 63) + dj * FY
    prow = row + step_x
    pcol = col + step_y
    row_all = prow + lax.axis_index("gx") * FX
    col_all = pcol + lax.axis_index("gy") * FY
    live = lax.broadcasted_iota(I32, local.shape, 1) < count
    live = live & (row_all >= 0) & (row_all < lax.axis_size("gx") * FX)
    live = live & (col_all >= 0) & (col_all < lax.axis_size("gy") * FY)
    inside = (prow >= 0) & (prow < FX) & (pcol >= 0) & (pcol < FY)
    near = (row >= -1) & (row <= FX) & (col >= -1) & (col <= FY)
    near = near | ((prow >= -1) & (prow <= FX) & (pcol >= -1) & (pcol <= FY))
    word = (row + H) * 128 + col + H + (((prow + H) * 128 + pcol + H) << 13)
    return word + (mine << 26) + (theirs << 27) + (code << 28), live, inside, near


def load_tiles(c, place_s, flat, size, stage, tiles):
    @pl.loop(0, 16)
    def _(i):
        for j in range(8):
            at = i * 8 + j
            own = place_s[0, c, at]
            other = place_s[1, c, at]
            stage[0, pl.ds(at, 1), :] = flat[pl.ds(own, 1), :]
            stage[1, pl.ds(at, 1), :] = flat[pl.ds(own + 2 * size, 1), :]
            stage[2, pl.ds(at, 1), :] = flat[pl.ds(other, 1), :]
            stage[3, pl.ds(at, 1), :] = flat[pl.ds(other + 2 * size, 1), :]

    for k in range(4):
        tiles[c, k] = jnp.transpose(stage[k]) * SC


def inner_kernel(
    count_ref, own_ref, state_ref, outline_ref, tiles, words_out, force_out,
    table, stage, place_v, place_s, left_ref, plane_ref, b_ref, acc_ref, sems,
):
    copies = []
    for q in range(4):
        source = outline_ref.at[:, :, slice(q * 128, q * 128 + 128)]
        copies.append(pltpu.make_async_copy(source, table.at[q], sems.at[q]))
    for copy in copies:
        copy.start()
    live = count_ref[0, 0]
    fields = [own_ref[k : k + 1, :] for k in range(4)]
    word, ok, inside, _ = pair_words(*fields, live, 0, 0)
    word = jnp.where(ok & inside, word, -1)
    for b in range(OWN):
        words_out[b : b + 1, :] = word[:, 128 * b : 128 * b + 128]
    word = jnp.maximum(words_out[...], H * 128 + H + ((H * 128 + H) << 13))
    own = (((word >> 7) & 63) - H) * FY + (word & 127) - H
    other = (((word >> 20) & 63) - H) * FY + ((word >> 13) & 127) - H
    place_v[0] = own + ((word >> 26) & 1) * (FX * FY)
    place_v[1] = other + ((word >> 27) & 1) * (FX * FY)
    copy = pltpu.make_async_copy(place_v, place_s, sems.at[4])
    copy.start()
    plane_ref[...] = jnp.zeros_like(plane_ref)
    acc_ref[...] = jnp.zeros_like(acc_ref)
    edge = jnp.zeros((FX, 128 - FY), F32)
    planes = []
    for k in range(2):
        plane = pltpu.roll(jnp.concatenate([state_ref[k], edge], axis=1), H, 1)
        ends = jnp.zeros((H, 128), F32)
        planes.append(jnp.concatenate([ends, plane, ends], axis=0))
    put_shift(left_ref, plane_ref, planes)
    for piece in copies:
        piece.wait()
    copy.wait()
    flat = table.reshape(4 * FX * FY, 128)

    @pl.loop(0, (live + 127) >> 7)
    def _(c):
        load_tiles(c, place_s, flat, FX * FY, stage, tiles)
        contact_chunk(c, -1, PMAX, words_out, tiles, left_ref, b_ref, acc_ref)

    for k in range(2):
        force_out[k] = acc_plane(acc_ref, k)


def edge_kernel(
    lists_ref, state_ref, outline_ref, north_ref, south_ref, west_ref, east_ref,
    tiles_out, words_out, count_out, force_out,
    table, tiles, stage, place_v, place_s, left_ref, plane_ref, b_ref, acc_ref, sems, tile_sems,
):
    copies = []
    for q in range(4):
        lanes = slice(q * 128, q * 128 + 128)
        for k, (source, target) in enumerate((
            (outline_ref, table.at[q, H : H + FX, 8 : 8 + FY, :]),
            (north_ref, table.at[q, 0:H, 8 : 8 + FY, :]),
            (south_ref, table.at[q, H + FX : R, 8 : 8 + FY, :]),
            (west_ref, table.at[q, :, 0:8, :]),
            (east_ref, table.at[q, :, 8 + FY : 16 + FY, :]),
        )):
            copies.append(pltpu.make_async_copy(source.at[:, :, lanes], target, sems.at[5 * q + k]))
    for copy in copies:
        copy.start()
    lists = len(NEIGH)
    number = lax.broadcasted_iota(I32, (lists, PMAX), 0)
    di, dj = jnp.zeros((lists, PMAX), I32), jnp.zeros((lists, PMAX), I32)
    for k, (i, j) in enumerate(NEIGH):
        di = jnp.where(number == k, i, di)
        dj = jnp.where(number == k, j, dj)
    word, ok, inside, near = pair_words(*[lists_ref[k].astype(I32) for k in range(5)], di, dj)
    ok = ok & near & ((number > 0) | ~inside)
    flags = jnp.where(ok, 1.0, 0.0)
    upper = (
        lax.broadcasted_iota(I32, (PMAX, PMAX), 0) < lax.broadcasted_iota(I32, (PMAX, PMAX), 1)
    ).astype(F32).astype(BF16)
    rank = nn(flags.astype(BF16), upper)
    base = jnp.zeros((1, 1), F32)
    ranks = []
    for k in range(lists):
        ranks.append(jnp.where(flags[k : k + 1] > 0.0, rank[k : k + 1] + base, -1.0).astype(I32))
        base = base + jnp.sum(flags[k : k + 1], axis=1, keepdims=True)
    found_all = jnp.sum(flags).astype(I32)
    mine = jnp.sum(flags[0:1]).astype(I32)
    total = (found_all + 127) >> 7
    whole = (found_all + 63) >> 7
    half_at = jnp.where(total > whole, total - 1, -1)
    words_out[...] = jnp.full(words_out.shape, -1, I32)
    slot = lax.broadcasted_iota(I32, (128, PMAX), 0)
    srow = lax.broadcasted_iota(I32, (16, PMAX), 0)
    pieces = []
    for k in range(lists):
        one = word[k : k + 1]
        piece = jnp.where(srow == 0, one & 255, jnp.where(srow == 1, (one >> 8) & 255, 0))
        piece = jnp.where(srow == 2, (one >> 16) & 255, jnp.where(srow == 3, (one >> 24) & 127, piece))
        piece = jnp.where(srow == 4, 1, piece)
        pieces.append(piece.astype(F32).astype(BF16))

    @pl.loop(0, total)
    def _(i):
        found = jnp.zeros((16, 128), F32)
        want = jnp.where(i >= whole, slot & 63, slot)
        for k in range(lists):
            found = found + nt(pieces[k], (want == ranks[k] - i * 128).astype(F32).astype(BF16))
        found = found.astype(I32)
        value = found[0:1] + (found[1:2] << 8) + (found[2:3] << 16) + (found[3:4] << 24)
        words_out[pl.ds(i, 1), :] = jnp.where(found[4:5] > 0, value, -1)

    word = jnp.maximum(words_out[...], 0)
    own = ((word >> 7) & 63) * TW + (word & 127) + PADC
    other = ((word >> 20) & 63) * TW + ((word >> 13) & 127) + PADC
    place_v[0] = own + ((word >> 26) & 1) * (R * TW)
    place_v[1] = other + ((word >> 27) & 1) * (R * TW)
    copy = pltpu.make_async_copy(place_v, place_s, sems.at[20])
    copy.start()
    count_out[0] = total
    count_out[1] = half_at
    plane_ref[...] = jnp.zeros_like(plane_ref)
    acc_ref[...] = jnp.zeros_like(acc_ref)
    put_shift(left_ref, plane_ref, [state_ref[0], state_ref[1]])
    for piece in copies:
        piece.wait()
    copy.wait()
    flat = table.reshape(4 * R * TW, 128)

    @pl.loop(0, total)
    def _(c):
        load_tiles(c, place_s, flat, R * TW, stage, tiles)
        pltpu.make_async_copy(tiles.at[c], tiles_out.at[c], tile_sems.at[c]).start()

    @pl.loop(0, (mine + 127) >> 7)
    def _(c):
        contact_chunk(c, half_at, mine, words_out, tiles, left_ref, b_ref, acc_ref)

    for k in range(2):
        force_out[k] = acc_plane(acc_ref, k)

    @pl.loop(0, total)
    def _(c):
        pltpu.make_async_copy(tiles.at[c], tiles_out.at[c], tile_sems.at[c]).wait()


def later_kernel(
    live_ref, count_ref, force_ref, state_ref, words_in, edge_words, tiles_in, edge_tiles, vel_out, shift_out,
    words_ref, tiles, left_ref, plane_ref, b_ref, acc_ref, now_ref, tile_sems,
):
    inner = (live_ref[0, 0] + 127) >> 7
    total = count_ref[0] + inner
    half_at = jnp.where(count_ref[1] >= 0, count_ref[1] + OWN, -1)

    @pl.loop(0, inner)
    def _(c):
        pltpu.make_async_copy(tiles_in.at[c], tiles.at[c], tile_sems.at[c]).start()

    @pl.loop(0, total - inner)
    def _(c):
        pltpu.make_async_copy(edge_tiles.at[c], tiles.at[c + OWN], tile_sems.at[c + OWN]).start()

    words_ref[0:OWN, :] = words_in[0:OWN, :]
    words_ref[OWN : OWN + NCH, :] = edge_words[...]
    now_ref[...] = state_ref[...]

    def update(forces):
        scale = DT / now_ref[4]
        for k in range(2):
            vel = now_ref[2 + k]
            vel = vel + (forces[k] - DRAG * vel) * scale
            now_ref[2 + k] = vel
            now_ref[k] = now_ref[k] + DT * vel

    update([force_ref[0], force_ref[1]])
    plane_ref[...] = jnp.zeros_like(plane_ref)

    @pl.loop(0, inner)
    def _(c):
        pltpu.make_async_copy(tiles_in.at[c], tiles.at[c], tile_sems.at[c]).wait()

    @pl.loop(0, total - inner)
    def _(c):
        pltpu.make_async_copy(edge_tiles.at[c], tiles.at[c + OWN], tile_sems.at[c + OWN]).wait()

    @pl.loop(1, STEPS)
    def _(step):
        put_shift(left_ref, plane_ref, [now_ref[0], now_ref[1]])
        acc_ref[...] = jnp.zeros_like(acc_ref)

        @pl.loop(0, total)
        def _(i):
            c = jnp.where(i < inner, i, i - inner + OWN)
            contact_chunk(c, half_at, 2 * NCH * 128, words_ref, tiles, left_ref, b_ref, acc_ref)

        update([acc_plane(acc_ref, k) + force_ref[2 + k] for k in range(2)])

    for out, base in ((shift_out, 0), (vel_out, 2)):
        for k in range(2):
            plane_ref[0:R, :] = pltpu.roll(now_ref[base + k], 128 - H, 1)
            for r in range(FX):
                out[r, k : k + 1, :] = plane_ref[r + H : r + H + 1, 0:FY]


def moved(x, axis, up):
    count = lax.axis_size(axis)
    pairs = [(i, i + 1) if up else (i + 1, i) for i in range(count - 1)]
    return lax.ppermute(x, axis, pairs)


def as_rows(x, rows):
    flat = x.reshape(-1)
    return jnp.pad(flat, (0, rows * 512 - flat.shape[0])).reshape(rows, 512)


def shards(
    outline, centres, velocity, mass, response, pairs, pair_count, forcing, ocean_dest, ocean_floe
):
    rows_dev = forcing.shape[0]
    send = pl.pallas_call(
        send_kernel,
        name="send_rows",
        out_shape=jax.ShapeDtypeStruct((DEVS * BLK, 128), F32),
        in_specs=[vspec()] * 3,
        out_specs=vspec(),
        scratch_shapes=[
            pltpu.VMEM((rows_dev // 128, 128), I32),
            pltpu.VMEM((DEVS, 128), F32),
            pltpu.SMEM((rows_dev // 128, 128), I32),
            pltpu.SemaphoreType.DMA,
        ],
        compiler_params=params(),
        cost_estimate=pl.CostEstimate(flops=100000000, bytes_accessed=4 << 20, transcendentals=0),
    )(ocean_dest.reshape(rows_dev // 128, 128), ocean_floe.reshape(rows_dev // 128, 128), forcing)
    pair_rows = jnp.transpose(pairs[0, 0], (1, 0))
    mass, send = lax.optimization_barrier((mass, send))
    got = lax.all_to_all(
        send.reshape(DEVS, 1, BLK * 128), ("gx", "gy"), split_axis=0, concat_axis=0, tiled=True
    )
    up, down, state = pl.pallas_call(
        pack_kernel,
        name="pack_rows",
        out_shape=[jax.ShapeDtypeStruct((PACK, 512), F32)] * 2 + [jax.ShapeDtypeStruct((5, FX, FY), F32)],
        in_specs=[sspec()] + [vspec()] * 4 + [aspec()],
        out_specs=[vspec()] * 3,
        scratch_shapes=[pltpu.SemaphoreType.DMA((2 * H,))],
        compiler_params=params(),
        cost_estimate=pl.CostEstimate(flops=1000000, bytes_accessed=1 << 20, transcendentals=0),
    )(pair_count, pair_rows, jnp.transpose(centres, (0, 2, 1)), jnp.transpose(velocity, (0, 2, 1)), mass, outline)

    def unpack_x(got):
        at = H * FY
        return (
            got[:at].reshape(H, FY, 512),
            got[at + 5 : at + 5 + 5 * H, :FY].reshape(5, H, FY),
            got[at : at + 5],
        )

    chunk_scratch = [
        pltpu.VMEM((6, CP, 128), F32),
        pltpu.VMEM((128, 128), F32),
        pltpu.VMEM((3, 128, 128), F32),
        pltpu.VMEM((6 * RP, 128), F32),
    ]
    tiles, words, contact = pl.pallas_call(
        inner_kernel,
        name="inner_pairs",
        out_shape=[
            jax.ShapeDtypeStruct((OWN, 4, 128, 128), F32),
            jax.ShapeDtypeStruct((OWN, 128), I32),
            jax.ShapeDtypeStruct((2, R, 128), F32),
        ],
        in_specs=[sspec(), vspec(), vspec(), aspec()],
        out_specs=[vspec()] * 3,
        scratch_shapes=[
            pltpu.VMEM((4, FX, FY, 128), F32),
            pltpu.VMEM((4, 128, 128), F32),
            pltpu.VMEM((2, OWN, 128), I32),
            pltpu.SMEM((2, OWN, 128), I32),
            *chunk_scratch,
            pltpu.SemaphoreType.DMA((5,)),
        ],
        compiler_params=params(),
        cost_estimate=pl.CostEstimate(flops=500000000, bytes_accessed=8 << 20, transcendentals=8 << 20),
    )(pair_count, pair_rows, state, outline)
    north, south, contact = lax.optimization_barrier((moved(up, "gx", True), moved(down, "gx", False), contact))
    north_o, north_s, north_l = unpack_x(north)
    south_o, south_s, south_l = unpack_x(south)
    tall = jnp.concatenate([north_s, state, south_s], axis=1)
    own_l = up[H * FY : H * FY + 5]

    def pack_y(lo):
        cols = jnp.concatenate(
            [north_o[:, lo : lo + H], outline[:, lo : lo + H], south_o[:, lo : lo + H]], axis=0
        )
        return jnp.concatenate(
            [cols.reshape(R * H, 512), as_rows(tall[:, :, lo : lo + H], 1), north_l, own_l, south_l], axis=0
        )

    def unpack_y(got):
        return (
            got[: R * H].reshape(R, H, 512),
            got[R * H].reshape(-1)[: 5 * R * H].reshape(5, R, H),
            got[R * H + 1 : R * H + 16],
        )

    west, east, got = lax.optimization_barrier((pack_y(FY - H), pack_y(0), got))
    west, east = moved(west, "gy", True), moved(east, "gy", False)
    ocean = pl.pallas_call(
        ocean_kernel,
        name="ocean_sum",
        out_shape=jax.ShapeDtypeStruct((2, R, 128), F32),
        in_specs=[vspec()] * 2,
        out_specs=vspec(),
        scratch_shapes=[
            pltpu.VMEM((FX * FY, 256), F32),
            pltpu.VMEM((5, DEVS // 16, 128), F32),
        ],
        compiler_params=params(),
        cost_estimate=pl.CostEstimate(flops=5000000000, bytes_accessed=5 << 20, transcendentals=0),
    )(got.reshape(DEVS * BLK, 128), response.reshape(FX * FY, NB))
    west, east, ocean = lax.optimization_barrier((west, east, ocean))
    west_o, west_s, west_l = unpack_y(west)
    east_o, east_s, east_l = unpack_y(east)
    west_o = jnp.pad(west_o, ((0, 0), (8 - H, 0), (0, 0)))
    east_o = jnp.pad(east_o, ((0, 0), (0, 8 - H), (0, 0)))
    wide = jnp.concatenate([west_s, tall, east_s], axis=2)
    wide = jnp.pad(wide, ((0, 0), (0, 0), (0, 128 - FY - 2 * H)))
    weight = jnp.where(wide[4:5] == 0.0, 1.0, wide[4:5])
    wide = jnp.concatenate([wide[:4], weight], axis=0)
    others = [own_l, north_l, south_l] + [block[5 * k : 5 * k + 5] for block in (west_l, east_l) for k in (0, 1, 2)]
    others = jnp.stack(others, axis=1)
    edge_tiles, edge_words, counts, edge_contact = pl.pallas_call(
        edge_kernel,
        out_shape=[
            jax.ShapeDtypeStruct((NCH, 4, 128, 128), F32),
            jax.ShapeDtypeStruct((NCH, 128), I32),
            jax.ShapeDtypeStruct((2,), I32),
            jax.ShapeDtypeStruct((2, R, 128), F32),
        ],
        in_specs=[vspec()] * 2 + [aspec()] * 5,
        out_specs=[aspec(), vspec(), sspec(), vspec()],
        scratch_shapes=[
            pltpu.VMEM((4, R, TW, 128), F32),
            pltpu.VMEM((NCH, 4, 128, 128), F32),
            pltpu.VMEM((4, 128, 128), F32),
            pltpu.VMEM((2, NCH, 128), I32),
            pltpu.SMEM((2, NCH, 128), I32),
            *chunk_scratch,
            pltpu.SemaphoreType.DMA((21,)),
            pltpu.SemaphoreType.DMA((NCH,)),
        ],
        compiler_params=params(),
        name="edge_pairs",
        cost_estimate=pl.CostEstimate(flops=500000000, bytes_accessed=8 << 20, transcendentals=8 << 20),
    )(others, wide, outline, north_o, south_o, west_o, east_o)

    force = jnp.concatenate([contact + edge_contact + ocean, ocean], axis=0)
    w = 2 * H - 1
    low, high = moved(force[:, FX : FX + w], "gx", True), moved(force[:, 1 : 1 + w], "gx", False)
    force = force + jnp.pad(low, ((0, 0), (0, R - w), (0, 0))) + jnp.pad(high, ((0, 0), (R - w, 0), (0, 0)))
    low, high = moved(force[:, :, FY : FY + w], "gy", True), moved(force[:, :, 1 : 1 + w], "gy", False)
    c = FY + 2 * H
    force = force + jnp.pad(low, ((0, 0), (0, 0), (0, 128 - w))) + jnp.pad(high, ((0, 0), (0, 0), (c - w, 128 - c)))

    vel, shift = pl.pallas_call(
        later_kernel,
        name="later_steps",
        out_shape=[jax.ShapeDtypeStruct((FX, 2, FY), F32)] * 2,
        in_specs=[sspec(), sspec()] + [vspec()] * 4 + [aspec()] * 2,
        out_specs=[vspec()] * 2,
        scratch_shapes=[
            pltpu.VMEM((OWN + NCH, 128), I32),
            pltpu.VMEM((OWN + NCH, 4, 128, 128), F32),
            *chunk_scratch,
            pltpu.VMEM((5, R, 128), F32),
            pltpu.SemaphoreType.DMA((OWN + NCH,)),
        ],
        compiler_params=params(),
        cost_estimate=pl.CostEstimate(flops=500000000, bytes_accessed=4 << 20, transcendentals=16 << 20),
    )(pair_count, counts, force, wide, words, edge_words, tiles, edge_tiles)
    return jnp.transpose(vel, (0, 2, 1)), jnp.transpose(shift, (0, 2, 1))


def solution(mesh):
    return jax.shard_map(
        shards,
        mesh=mesh,
        in_specs=(
            P("gx", "gy", None),
            P("gx", "gy", None),
            P("gx", "gy", None),
            P("gx", "gy"),
            P("gx", "gy", None),
            P("gx", "gy", None, None),
            P("gx", "gy"),
            P(("gx", "gy"), None),
            P(("gx", "gy"), None),
            P(("gx", "gy")),
        ),
        out_specs=(P("gx", "gy", None), P("gx", "gy", None)),
        check_vma=False,
    )
```

```python
import math

import jax
import jax.numpy as jnp
from jax import lax
from jax.experimental import pallas as pl
from jax.experimental.pallas import tpu as pltpu
from jax.sharding import PartitionSpec as P

FX, FY, V, TILE, NB, PMAX = 32, 64, 256, 128, 64, 512
DEVS, CAP, BLK = 128, 40, 41
STEPS = 3
DT, DRAG = 0.1, 0.5
H = 2
R = FX + 2 * H
RP = 40
PACK = H * FY + 16
SIDE = R * H + 16
RK = 48
CP = 72
TW = FY + 16
PADC = 8 - H
NCH = 9 * PMAX // 128
OWN = PMAX // 128
NEIGH = ((0, 0), (-1, 0), (1, 0), (-1, -1), (0, -1), (1, -1), (-1, 1), (0, 1), (1, 1))
SC = math.sqrt(100.0 * math.log2(math.e))
F32, BF16, I32 = jnp.float32, jnp.bfloat16, jnp.int32
VMEM_BYTES = 52 * 1024 * 1024


def params(size=VMEM_BYTES):
    return pltpu.CompilerParams(vmem_limit_bytes=size)


def vspec():
    return pl.BlockSpec(memory_space=pltpu.VMEM)


def sspec():
    return pl.BlockSpec(memory_space=pltpu.SMEM)


def aspec():
    return pl.BlockSpec(memory_space=pl.ANY)


def nt(a, b):
    return lax.dot_general(a, b, (((1,), (1,)), ((), ())), preferred_element_type=F32)


def nn(a, b):
    return jnp.dot(a, b, preferred_element_type=F32)


def split3(x):
    a = x.astype(BF16).astype(F32)
    b = (x - a).astype(BF16).astype(F32)
    return a, b, (x - a - b).astype(BF16).astype(F32)


def pack_kernel(count_ref, pairs_ref, centres_ref, velocity_ref, mass_ref, outline_ref, up_ref, down_ref, state_ref, sems):
    copies = []
    for k, (out, lo) in enumerate(((up_ref, FX - H), (down_ref, 0))):
        for h in range(H):
            target = out.at[h * FY : h * FY + FY, :]
            copies.append(pltpu.make_async_copy(outline_ref.at[lo + h], target, sems.at[k * H + h]))
    for copy in copies:
        copy.start()
    at = H * FY
    tail = jnp.zeros((11, 512), F32)
    count = jnp.full((1, 512), count_ref[0, 0], I32).astype(F32)
    for k in range(2):
        state_ref[k] = centres_ref[:, k, :]
        state_ref[2 + k] = velocity_ref[:, k, :]
    state_ref[4] = mass_ref[...]
    for out, lo in ((up_ref, FX - H), (down_ref, 0)):
        out[at : at + 4, :] = pairs_ref[...].astype(F32)
        out[at + 4 : at + 5, :] = count
        out[at + 5 : at + 16, :] = tail
        for k in range(5):
            out[at + 5 + k * H : at + 5 + k * H + H, 0:FY] = state_ref[k, lo : lo + H, :]
    for copy in copies:
        copy.wait()


def turn_kernel(own_ref, north_ref, south_ref, state_ref, last_ref, first_ref, west_ref, east_ref):
    at, top = H * FY, R * H
    edge = jnp.zeros((FX, 128 - FY), F32)
    lane = lax.broadcasted_iota(I32, (R, 128), 1)
    planes = []
    for k in range(5):
        rows = jnp.concatenate([state_ref[k], edge], axis=1)
        place = at + 5 + k * H
        ends = [ref[place : place + H, 0:128] for ref in (north_ref, south_ref)]
        planes.append(jnp.concatenate([ends[0], rows, ends[1]], axis=0))
    for out, cols, lo in ((west_ref, last_ref, FY - H), (east_ref, first_ref, 0)):
        for h in range(H):
            out[h * H : h * H + H, :] = north_ref[h * FY + lo : h * FY + lo + H, :]
            low = top - H * H + h * H
            out[low : low + H, :] = south_ref[h * FY + lo : h * FY + lo + H, :]
        out[H * H : H * H + FX * H, :] = cols[...]
        for k, ref in enumerate((north_ref, own_ref, south_ref)):
            out[top + 5 * k : top + 5 * k + 5, :] = ref[at : at + 5, :]
        out[top + 15 : top + 16, :] = jnp.zeros((1, 512), F32)
        block = jnp.zeros((R, 128), F32)
        for k in range(5):
            turned = pltpu.roll(planes[k], (H * k - lo) % 128, 1)
            block = jnp.where((lane >= H * k) & (lane < H * k + H), turned, block)
        out[SIDE : SIDE + R, :] = jnp.concatenate([block, jnp.zeros((R, 384), F32)], axis=1)


def send_kernel(dest_in, floe_in, rows_in, out_ref, dest_ref, floe_ref, rows_ref, place_v, ids_v, place_s, sem, sems):
    ins = [
        pltpu.make_async_copy(source, target, sems.at[k])
        for k, (source, target) in enumerate(((dest_in, dest_ref), (floe_in, floe_ref), (rows_in, rows_ref)))
    ]
    for copy in ins:
        copy.start()
    upper = (
        lax.broadcasted_iota(I32, (128, 128), 0) < lax.broadcasted_iota(I32, (128, 128), 1)
    ).astype(F32).astype(BF16)
    ones = jnp.ones((128, 128), BF16)
    index = lax.broadcasted_iota(I32, (128, 128), 0)
    ins[0].wait()
    ins[1].wait()
    blocks = dest_ref.shape[0]
    hots = [(index == dest_ref[k : k + 1, :]).astype(F32) for k in range(blocks)]
    hot16 = jnp.concatenate([hot.astype(BF16) for hot in hots], axis=0)
    before = nn(hot16, upper)
    full = nn(hot16, ones)
    carry = jnp.zeros((128, 128), F32)
    high, low, slots = [], [], []
    for k in range(blocks):
        rank = jnp.sum(hots[k] * (before[128 * k : 128 * k + 128] + carry), axis=0, keepdims=True)
        carry = carry + full[128 * k : 128 * k + 128]
        rank = rank.astype(I32)
        place_v[k : k + 1, :] = dest_ref[k : k + 1, :] * BLK + rank
        floe = floe_ref[k : k + 1, :] + 1
        slots.append((index == rank).astype(F32).astype(BF16))
        high.append((hots[k] * (floe >> 6).astype(F32)).astype(BF16))
        low.append((hots[k] * (floe & 63).astype(F32)).astype(BF16))
    slots = jnp.concatenate(slots, axis=1)
    ids = 64.0 * nt(jnp.concatenate(high, axis=1), slots) + nt(jnp.concatenate(low, axis=1), slots)
    ids_v[...] = ids
    copy = pltpu.make_async_copy(place_v, place_s, sem)
    copy.start()

    @pl.loop(0, out_ref.shape[0] // 128)
    def _(i):
        out_ref[pl.ds(pl.multiple_of(i * 128, 128), 128), :] = jnp.zeros((128, 128), F32)

    copy.wait()
    ins[2].wait()

    @pl.loop(0, rows_ref.shape[0] // 128)
    def _(k):
        for j in range(128):
            out_ref[pl.ds(place_s[k, j], 1), :] = rows_ref[pl.ds(k * 128 + j, 1), :]

    for d in range(DEVS):
        out_ref[d * BLK + CAP : d * BLK + CAP + 1, :] = ids_v[d : d + 1, :]


def ocean_kernel(rows_ref, resp_ref, out_ref, acc_ref, ids_ref):
    groups = DEVS // 16
    lane = lax.broadcasted_iota(I32, (groups, 128), 1)
    blocks = [jnp.zeros((groups, 128), F32) for _ in range(5)]
    for j in range(16):
        ids = rows_ref[pl.ds(j * BLK + CAP, groups, stride=16 * BLK), :]
        shift = (CAP * j) % 128
        if shift:
            ids = pltpu.roll(ids, shift, 1)
        for b in range(5):
            if CAP * j < 128 * b + 128 and CAP * j + CAP > 128 * b:
                place = lane + (128 * b - CAP * j)
                blocks[b] = jnp.where((place >= 0) & (place < CAP), ids, blocks[b])
    for b in range(5):
        ids_ref[b] = blocks[b]
    base16 = lax.broadcasted_iota(I32, (16, 128), 0).astype(F32)
    one, zero = jnp.ones((16, 128), BF16), jnp.zeros((16, 128), BF16)

    rows = jnp.concatenate([rows_ref[BLK * j : BLK * j + CAP, :] for j in range(DEVS)], axis=0)
    high = rows.astype(BF16)
    low = (rows - high.astype(F32)).astype(BF16)
    both = jnp.concatenate([high, low], axis=1)
    ids = [ids_ref[b, h : h + 1, :] for h in range(groups) for b in range(5)]
    for part in range(8):
        cols = []
        for row in ids:
            rel = jnp.broadcast_to(row - (part * 256 + 1.0), (16, 128)).astype(BF16)
            cols.append(
                jnp.concatenate(
                    [jnp.where((base16 + 16.0 * k).astype(BF16) == rel, one, zero) for k in range(16)], axis=0
                )
            )
        acc_ref[part * 256 : part * 256 + 256, :] = nn(jnp.concatenate(cols, axis=1), both)

    out_ref[...] = jnp.zeros_like(out_ref)
    srow = lax.broadcasted_iota(I32, (16, 128), 0)
    slane = lax.broadcasted_iota(I32, (16, 128), 1)
    pick = (((srow == 0) & (slane < NB)) | ((srow == 1) & (slane >= NB))).astype(F32).astype(BF16)
    inner = (slane >= H) & (slane < H + FY)

    for part in range(8):
        at = part * 256
        total = acc_ref[pl.ds(at, 256), 0:128] + acc_ref[pl.ds(at, 256), 128:256]
        resp = resp_ref[pl.ds(at, 256), :]
        a, b, c = split3(total * jnp.concatenate([resp, resp], axis=1))
        force = nt(pick, a.astype(BF16)) + nt(pick, b.astype(BF16)) + nt(pick, c.astype(BF16))
        for j in range(4):
            piece = force[:, (j // 2) * 128 : (j // 2) * 128 + 128]
            piece = pltpu.roll(piece, (H - 64 * (j % 2)) % 128, 1)
            piece = jnp.where(inner, piece, 0.0)
            for k in range(2):
                out_ref[k, part * 4 + j + H : part * 4 + j + H + 1, :] = piece[k : k + 1]


def put_shift(left_ref, plane_ref, planes):
    for k in range(2):
        plane_ref[0:R, :] = planes[k]
        for j, part in enumerate(split3(jnp.transpose(plane_ref[...])[0:CP])):
            left_ref[3 * k + j] = part


def contact_chunk(c, half_at, live, words_ref, tiles_ref, left_ref, b_ref, acc_ref):
    word = words_ref[pl.ds(c, 1), :]
    lane = lax.broadcasted_iota(I32, (1, 128), 1)
    ok = (word >= 0) & (c * 128 + jnp.where(c == half_at, lane & 63, lane) < live)
    rows = jnp.concatenate([(word >> 7) & 63, (word >> 20) & 63], axis=1)
    cols = jnp.concatenate([word & 127, (word >> 13) & 127], axis=1)
    code = (word >> 28) & 7
    code9 = code + (code >= 4).astype(I32)
    step = (code9 >= 3).astype(I32) + (code9 >= 6).astype(I32)
    dirx = (step - 1).astype(F32)
    diry = (code9 - 3 * step - 1).astype(F32)
    row_hot = (lax.broadcasted_iota(I32, (RK, 256), 0) == rows).astype(F32)
    row_hot16 = row_hot.astype(BF16)
    col_hot = lax.broadcasted_iota(I32, (CP, 256), 0) == cols
    lanes = lax.broadcasted_iota(I32, (128, 256), 0) == cols
    diffs = []
    for k in range(2):
        left = jnp.concatenate([left_ref[3 * k + j, :, 0:RK] for j in range(3)], axis=0)
        part = nn(left.astype(BF16), row_hot16)
        part = part[0:CP] + part[CP : 2 * CP] + part[2 * CP : 3 * CP]
        part = jnp.sum(jnp.where(col_hot, part, 0.0), axis=0, keepdims=True)
        diffs.append(part[:, 0:128] - part[:, 128:256])
    dx = (dirx - diffs[0]) * SC
    dy = (diry - diffs[1]) * SC
    px = tiles_ref[c, 2] + dx
    py = tiles_ref[c, 3] + dy
    b_ref[0] = 2.0 * px
    b_ref[1] = 2.0 * py
    b_ref[2] = -(px * px + py * py)
    turns = jnp.where(c == half_at, TILE // 64, TILE // 32)

    @pl.when(c == half_at)
    def _():
        left_half = lax.broadcasted_iota(I32, (64, 128), 1) < 64
        for k in range(3):
            b_ref[k, 0:64, :] = jnp.where(left_half, b_ref[k, 0:64, :], b_ref[k, 64:128, :])

    force_x = jnp.zeros((8, 128), F32)
    force_y = jnp.zeros((8, 128), F32)
    back_x = jnp.zeros((8, 128), F32)
    back_y = jnp.zeros((8, 128), F32)
    for half in range(2):
        ax = [tiles_ref[c, 0, half * 64 + 8 * k : half * 64 + 8 * k + 8, :] for k in range(8)]
        ay = [tiles_ref[c, 1, half * 64 + 8 * k : half * 64 + 8 * k + 8, :] for k in range(8)]
        na = [-(x * x + y * y) for x, y in zip(ax, ay)]

        def body(i, carry):
            sums, bx_sum, by_sum = carry
            sums = list(sums)
            for j in range(32):
                w = i * 32 + j
                bx = jnp.broadcast_to(b_ref[0, pl.ds(w, 1), :], (8, 128))
                by = jnp.broadcast_to(b_ref[1, pl.ds(w, 1), :], (8, 128))
                nb = jnp.broadcast_to(b_ref[2, pl.ds(w, 1), :], (8, 128))
                weights = [jnp.exp2((ax[k] * bx + ay[k] * by) + (na[k] + nb)) for k in range(8)]
                sums = [s + t for s, t in zip(sums, weights)]
                while len(weights) > 1:
                    weights = [weights[k] + weights[k + 1] for k in range(0, len(weights), 2)]
                bx_sum = bx_sum + weights[0] * bx
                by_sum = by_sum + weights[0] * by
            return tuple(sums), bx_sum, by_sum

        sums, back_x, back_y = lax.fori_loop(
            0, turns, body, (tuple(jnp.zeros((8, 128), F32) for _ in range(8)), back_x, back_y)
        )
        for k in range(8):
            force_x = force_x + ax[k] * sums[k]
            force_y = force_y + ay[k] * sums[k]
    fx = jnp.sum(force_x - 0.5 * back_x, axis=0, keepdims=True) * (1.0 / SC)
    fy = jnp.sum(force_y - 0.5 * back_y, axis=0, keepdims=True) * (1.0 / SC)
    parts = split3(jnp.where(ok, fx, 0.0)) + split3(jnp.where(ok, fy, 0.0))
    spread = [row_hot[0:RP] * jnp.concatenate([part, -part], axis=1) for part in parts]
    acc_ref[...] += nt(jnp.concatenate(spread, axis=0).astype(BF16), lanes.astype(F32).astype(BF16))


def acc_plane(acc_ref, k):
    at = 3 * RP * k
    return acc_ref[at : at + R, :] + acc_ref[at + RP : at + RP + R, :] + acc_ref[at + 2 * RP : at + 2 * RP + R, :]


def code_steps(code):
    code9 = code + (code >= 4).astype(I32)
    step = (code9 >= 3).astype(I32) + (code9 >= 6).astype(I32)
    return step - 1, code9 - 3 * step - 1


def pair_words(local, code, mine, theirs, count, di, dj):
    step_x, step_y = code_steps(code)
    row = (local >> 6) + di * FX
    col = (local & 63) + dj * FY
    prow = row + step_x
    pcol = col + step_y
    row_all = prow + lax.axis_index("gx") * FX
    col_all = pcol + lax.axis_index("gy") * FY
    live = lax.broadcasted_iota(I32, local.shape, 1) < count
    live = live & (row_all >= 0) & (row_all < lax.axis_size("gx") * FX)
    live = live & (col_all >= 0) & (col_all < lax.axis_size("gy") * FY)
    inside = (prow >= 0) & (prow < FX) & (pcol >= 0) & (pcol < FY)
    near = (row >= -1) & (row <= FX) & (col >= -1) & (col <= FY)
    near = near | ((prow >= -1) & (prow <= FX) & (pcol >= -1) & (pcol <= FY))
    word = (row + H) * 128 + col + H + (((prow + H) * 128 + pcol + H) << 13)
    return word + (mine << 26) + (theirs << 27) + (code << 28), live, inside, near


def load_tiles(c, place_s, flat, size, stage, tiles):
    @pl.loop(0, 16)
    def _(i):
        for j in range(8):
            at = i * 8 + j
            own = place_s[0, c, at]
            other = place_s[1, c, at]
            stage[0, pl.ds(at, 1), :] = flat[pl.ds(own, 1), :]
            stage[1, pl.ds(at, 1), :] = flat[pl.ds(own + 2 * size, 1), :]
            stage[2, pl.ds(at, 1), :] = flat[pl.ds(other, 1), :]
            stage[3, pl.ds(at, 1), :] = flat[pl.ds(other + 2 * size, 1), :]

    for k in range(4):
        tiles[c, k] = jnp.transpose(stage[k]) * SC


def inner_kernel(
    count_ref, own_ref, state_ref, outline_ref, tiles, words_out, force_out, last_ref, first_ref,
    table, stage, place_v, place_s, left_ref, plane_ref, b_ref, acc_ref, sems,
):
    copies = []
    for q in range(4):
        source = outline_ref.at[:, :, slice(q * 128, q * 128 + 128)]
        copies.append(pltpu.make_async_copy(source, table.at[q], sems.at[q]))
    for copy in copies:
        copy.start()
    live = count_ref[0, 0]
    fields = [own_ref[k : k + 1, :] for k in range(4)]
    word, ok, inside, _ = pair_words(*fields, live, 0, 0)
    word = jnp.where(ok & inside, word, -1)
    for b in range(OWN):
        words_out[b : b + 1, :] = word[:, 128 * b : 128 * b + 128]
    word = jnp.maximum(words_out[...], H * 128 + H + ((H * 128 + H) << 13))
    own = (((word >> 7) & 63) - H) * FY + (word & 127) - H
    other = (((word >> 20) & 63) - H) * FY + ((word >> 13) & 127) - H
    place_v[0] = own + ((word >> 26) & 1) * (FX * FY)
    place_v[1] = other + ((word >> 27) & 1) * (FX * FY)
    copy = pltpu.make_async_copy(place_v, place_s, sems.at[4])
    copy.start()
    plane_ref[...] = jnp.zeros_like(plane_ref)
    acc_ref[...] = jnp.zeros_like(acc_ref)
    edge = jnp.zeros((FX, 128 - FY), F32)
    planes = []
    for k in range(2):
        plane = pltpu.roll(jnp.concatenate([state_ref[k], edge], axis=1), H, 1)
        ends = jnp.zeros((H, 128), F32)
        planes.append(jnp.concatenate([ends, plane, ends], axis=0))
    put_shift(left_ref, plane_ref, planes)
    for piece in copies:
        piece.wait()
    copy.wait()
    for out, lo in ((last_ref, FY - H), (first_ref, 0)):
        for r in range(FX):
            for q in range(4):
                out[r * H : r * H + H, q * 128 : q * 128 + 128] = table[q, r, lo : lo + H, :]
    flat = table.reshape(4 * FX * FY, 128)

    @pl.loop(0, (live + 127) >> 7)
    def _(c):
        load_tiles(c, place_s, flat, FX * FY, stage, tiles)
        contact_chunk(c, -1, PMAX, words_out, tiles, left_ref, b_ref, acc_ref)

    for k in range(2):
        force_out[k] = acc_plane(acc_ref, k)


def edge_kernel(
    own_ref, state_ref, outline_ref, north_ref, south_ref, west_ref, east_ref,
    tiles_out, words_out, count_out, force_out, wide_ref,
    table, tiles, stage, place_v, place_s, left_ref, plane_ref, b_ref, acc_ref, sems, tile_sems,
):
    copies = []
    for q in range(4):
        lanes = slice(q * 128, q * 128 + 128)
        target = table.at[q, H : H + FX, 8 : 8 + FY, :]
        copies.append(pltpu.make_async_copy(outline_ref.at[:, :, lanes], target, sems.at[3 * q]))
        for h in range(H):
            table[q, h, 8 : 8 + FY, :] = north_ref[h * FY : h * FY + FY, lanes]
            table[q, H + FX + h, 8 : 8 + FY, :] = south_ref[h * FY : h * FY + FY, lanes]
        for r in range(R):
            table[q, r, PADC:8, :] = west_ref[r * H : r * H + H, lanes]
            table[q, r, 8 + FY : 8 + FY + H, :] = east_ref[r * H : r * H + H, lanes]
    for copy in copies:
        copy.start()
    edge = jnp.zeros((FX, 128 - FY), F32)

    lane = lax.broadcasted_iota(I32, (R, 128), 1)
    inside = (lane >= H) & (lane < H + FY)
    for k in range(5):
        at = H * FY + 5 + k * H
        rows = jnp.concatenate([state_ref[k], edge], axis=1)
        rows = jnp.concatenate([north_ref[at : at + H, 0:128], rows, south_ref[at : at + H, 0:128]], axis=0)
        left = pltpu.roll(west_ref[SIDE : SIDE + R, 0:128], (-H * k) % 128, 1)
        right = pltpu.roll(east_ref[SIDE : SIDE + R, 0:128], (H + FY - H * k) % 128, 1)
        plane = jnp.where(inside, pltpu.roll(rows, H, 1), jnp.where(lane < H, left, right))
        plane = jnp.where(lane < FY + 2 * H, plane, 0.0)
        wide_ref[k] = jnp.where(plane == 0.0, 1.0, plane) if k == 4 else plane
    top = R * H
    heads = [
        (own_ref, H * FY), (north_ref, H * FY), (south_ref, H * FY), (west_ref, top), (west_ref, top + 5),
        (west_ref, top + 10), (east_ref, top), (east_ref, top + 5), (east_ref, top + 10),
    ]
    fields = [
        jnp.concatenate([ref[at + k : at + k + 1, :] for ref, at in heads], axis=0).astype(I32) for k in range(5)
    ]
    lists = len(NEIGH)
    number = lax.broadcasted_iota(I32, (lists, PMAX), 0)
    di, dj = jnp.zeros((lists, PMAX), I32), jnp.zeros((lists, PMAX), I32)
    for k, (i, j) in enumerate(NEIGH):
        di = jnp.where(number == k, i, di)
        dj = jnp.where(number == k, j, dj)
    word, ok, inside, near = pair_words(*fields, di, dj)
    ok = ok & near & ((number > 0) | ~inside)
    flags = jnp.where(ok, 1.0, 0.0)
    upper = (
        lax.broadcasted_iota(I32, (PMAX, PMAX), 0) < lax.broadcasted_iota(I32, (PMAX, PMAX), 1)
    ).astype(F32).astype(BF16)
    rank = nn(flags.astype(BF16), upper)
    base = jnp.zeros((1, 1), F32)
    ranks = []
    for k in range(lists):
        ranks.append(jnp.where(flags[k : k + 1] > 0.0, rank[k : k + 1] + base, -1.0).astype(I32))
        base = base + jnp.sum(flags[k : k + 1], axis=1, keepdims=True)
    found_all = jnp.sum(flags).astype(I32)
    mine = jnp.sum(flags[0:1]).astype(I32)
    total = (found_all + 127) >> 7
    whole = (found_all + 63) >> 7
    half_at = jnp.where(total > whole, total - 1, -1)
    words_out[...] = jnp.full(words_out.shape, -1, I32)
    slot = lax.broadcasted_iota(I32, (128, PMAX), 0)
    srow = lax.broadcasted_iota(I32, (16, PMAX), 0)
    pieces = []
    for k in range(lists):
        one = word[k : k + 1]
        piece = jnp.where(srow == 0, one & 255, jnp.where(srow == 1, (one >> 8) & 255, 0))
        piece = jnp.where(srow == 2, (one >> 16) & 255, jnp.where(srow == 3, (one >> 24) & 127, piece))
        piece = jnp.where(srow == 4, 1, piece)
        pieces.append(piece.astype(F32).astype(BF16))

    @pl.loop(0, total)
    def _(i):
        found = jnp.zeros((16, 128), F32)
        want = jnp.where(i >= whole, slot & 63, slot)
        for k in range(lists):
            found = found + nt(pieces[k], (want == ranks[k] - i * 128).astype(F32).astype(BF16))
        found = found.astype(I32)
        value = found[0:1] + (found[1:2] << 8) + (found[2:3] << 16) + (found[3:4] << 24)
        words_out[pl.ds(i, 1), :] = jnp.where(found[4:5] > 0, value, -1)

    word = jnp.maximum(words_out[...], 0)
    own = ((word >> 7) & 63) * TW + (word & 127) + PADC
    other = ((word >> 20) & 63) * TW + ((word >> 13) & 127) + PADC
    place_v[0] = own + ((word >> 26) & 1) * (R * TW)
    place_v[1] = other + ((word >> 27) & 1) * (R * TW)
    copy = pltpu.make_async_copy(place_v, place_s, sems.at[20])
    copy.start()
    count_out[0] = total
    count_out[1] = half_at
    plane_ref[...] = jnp.zeros_like(plane_ref)
    acc_ref[...] = jnp.zeros_like(acc_ref)
    put_shift(left_ref, plane_ref, [wide_ref[0], wide_ref[1]])
    for piece in copies:
        piece.wait()

    copy.wait()
    flat = table.reshape(4 * R * TW, 128)

    @pl.loop(0, total)
    def _(c):
        load_tiles(c, place_s, flat, R * TW, stage, tiles)
        pltpu.make_async_copy(tiles.at[c], tiles_out.at[c], tile_sems.at[c]).start()

    @pl.loop(0, (mine + 127) >> 7)
    def _(c):
        contact_chunk(c, half_at, mine, words_out, tiles, left_ref, b_ref, acc_ref)

    for k in range(2):
        force_out[k] = acc_plane(acc_ref, k)

    @pl.loop(0, total)
    def _(c):
        pltpu.make_async_copy(tiles.at[c], tiles_out.at[c], tile_sems.at[c]).wait()


def later_kernel(
    live_ref, count_ref, force_ref, state_ref, words_in, edge_words, tiles_in, edge_tiles, vel_out, shift_out,
    words_ref, tiles, left_ref, plane_ref, b_ref, acc_ref, now_ref, tile_sems,
):
    inner = (live_ref[0, 0] + 127) >> 7
    total = count_ref[0] + inner
    half_at = jnp.where(count_ref[1] >= 0, count_ref[1] + OWN, -1)

    @pl.loop(0, inner)
    def _(c):
        pltpu.make_async_copy(tiles_in.at[c], tiles.at[c], tile_sems.at[c]).start()

    @pl.loop(0, total - inner)
    def _(c):
        pltpu.make_async_copy(edge_tiles.at[c], tiles.at[c + OWN], tile_sems.at[c + OWN]).start()

    words_ref[0:OWN, :] = words_in[0:OWN, :]
    words_ref[OWN : OWN + NCH, :] = edge_words[...]
    now_ref[...] = state_ref[...]

    def update(forces):
        scale = DT / now_ref[4]
        for k in range(2):
            vel = now_ref[2 + k]
            vel = vel + (forces[k] - DRAG * vel) * scale
            now_ref[2 + k] = vel
            now_ref[k] = now_ref[k] + DT * vel

    update([force_ref[0], force_ref[1]])
    plane_ref[...] = jnp.zeros_like(plane_ref)

    @pl.loop(0, inner)
    def _(c):
        pltpu.make_async_copy(tiles_in.at[c], tiles.at[c], tile_sems.at[c]).wait()

    @pl.loop(0, total - inner)
    def _(c):
        pltpu.make_async_copy(edge_tiles.at[c], tiles.at[c + OWN], tile_sems.at[c + OWN]).wait()

    @pl.loop(1, STEPS)
    def _(step):
        put_shift(left_ref, plane_ref, [now_ref[0], now_ref[1]])
        acc_ref[...] = jnp.zeros_like(acc_ref)

        @pl.loop(0, total)
        def _(i):
            c = jnp.where(i < inner, i, i - inner + OWN)
            contact_chunk(c, half_at, 2 * NCH * 128, words_ref, tiles, left_ref, b_ref, acc_ref)

        update([acc_plane(acc_ref, k) + force_ref[2 + k] for k in range(2)])

    for out, base in ((shift_out, 0), (vel_out, 2)):
        for k in range(2):
            plane_ref[0:R, :] = pltpu.roll(now_ref[base + k], 128 - H, 1)
            for r in range(FX):
                out[r, k : k + 1, :] = plane_ref[r + H : r + H + 1, 0:FY]


def moved(x, axis, up):
    count = lax.axis_size(axis)
    pairs = [(i, i + 1) if up else (i + 1, i) for i in range(count - 1)]
    return lax.ppermute(x, axis, pairs)


def shards(
    outline, centres, velocity, mass, response, pairs, pair_count, forcing, ocean_dest, ocean_floe
):
    rows_dev = forcing.shape[0]
    send = pl.pallas_call(
        send_kernel,
        name="send_rows",
        out_shape=jax.ShapeDtypeStruct((DEVS * BLK, 128), F32),
        in_specs=[pl.BlockSpec(memory_space=pltpu.HBM)] * 3,
        out_specs=vspec(),
        scratch_shapes=[
            pltpu.VMEM((rows_dev // 128, 128), I32),
            pltpu.VMEM((rows_dev // 128, 128), I32),
            pltpu.VMEM((rows_dev, 128), F32),
            pltpu.VMEM((rows_dev // 128, 128), I32),
            pltpu.VMEM((DEVS, 128), F32),
            pltpu.SMEM((rows_dev // 128, 128), I32),
            pltpu.SemaphoreType.DMA,
            pltpu.SemaphoreType.DMA((3,)),
        ],
        compiler_params=params(63 << 20),
        cost_estimate=pl.CostEstimate(flops=100000000, bytes_accessed=4 << 20, transcendentals=0),
    )(ocean_dest.reshape(rows_dev // 128, 128), ocean_floe.reshape(rows_dev // 128, 128), forcing)
    pair_rows = jnp.transpose(pairs[0, 0], (1, 0))
    mass, send = lax.optimization_barrier((mass, send))
    got = lax.all_to_all(
        send.reshape(DEVS, 1, BLK * 128), ("gx", "gy"), split_axis=0, concat_axis=0, tiled=True
    )
    up, down, state = pl.pallas_call(
        pack_kernel,
        name="pack_rows",
        out_shape=[jax.ShapeDtypeStruct((PACK, 512), F32)] * 2 + [jax.ShapeDtypeStruct((5, FX, FY), F32)],
        in_specs=[sspec()] + [vspec()] * 4 + [aspec()],
        out_specs=[vspec()] * 3,
        scratch_shapes=[pltpu.SemaphoreType.DMA((2 * H,))],
        compiler_params=params(),
        cost_estimate=pl.CostEstimate(flops=1000000, bytes_accessed=1 << 20, transcendentals=0),
    )(pair_count, pair_rows, jnp.transpose(centres, (0, 2, 1)), jnp.transpose(velocity, (0, 2, 1)), mass, outline)

    chunk_scratch = [
        pltpu.VMEM((6, CP, 128), F32),
        pltpu.VMEM((128, 128), F32),
        pltpu.VMEM((3, 128, 128), F32),
        pltpu.VMEM((6 * RP, 128), F32),
    ]
    tiles, words, contact, last, first = pl.pallas_call(
        inner_kernel,
        name="inner_pairs",
        out_shape=[
            jax.ShapeDtypeStruct((OWN, 4, 128, 128), F32),
            jax.ShapeDtypeStruct((OWN, 128), I32),
            jax.ShapeDtypeStruct((2, R, 128), F32),
            jax.ShapeDtypeStruct((FX * H, 512), F32),
            jax.ShapeDtypeStruct((FX * H, 512), F32),
        ],
        in_specs=[sspec(), vspec(), vspec(), aspec()],
        out_specs=[vspec()] * 5,
        scratch_shapes=[
            pltpu.VMEM((4, FX, FY, 128), F32),
            pltpu.VMEM((4, 128, 128), F32),
            pltpu.VMEM((2, OWN, 128), I32),
            pltpu.SMEM((2, OWN, 128), I32),
            *chunk_scratch,
            pltpu.SemaphoreType.DMA((5,)),
        ],
        compiler_params=params(),
        cost_estimate=pl.CostEstimate(flops=500000000, bytes_accessed=8 << 20, transcendentals=8 << 20),
    )(pair_count, pair_rows, state, outline)
    north, south, contact = lax.optimization_barrier((moved(up, "gx", True), moved(down, "gx", False), contact))
    west, east = pl.pallas_call(
        turn_kernel,
        name="pack_columns",
        out_shape=[jax.ShapeDtypeStruct((SIDE + R, 512), F32)] * 2,
        in_specs=[vspec()] * 6,
        out_specs=[vspec()] * 2,
        compiler_params=params(),
        cost_estimate=pl.CostEstimate(flops=1000000, bytes_accessed=1 << 20, transcendentals=0),
    )(up, north, south, state, last, first)
    west, east, got = lax.optimization_barrier((west, east, got))
    west, east = moved(west, "gy", True), moved(east, "gy", False)
    ocean = pl.pallas_call(
        ocean_kernel,
        name="ocean_sum",
        out_shape=jax.ShapeDtypeStruct((2, R, 128), F32),
        in_specs=[vspec()] * 2,
        out_specs=vspec(),
        scratch_shapes=[
            pltpu.VMEM((FX * FY, 256), F32),
            pltpu.VMEM((5, DEVS // 16, 128), F32),
        ],
        compiler_params=params(),
        cost_estimate=pl.CostEstimate(flops=5000000000, bytes_accessed=5 << 20, transcendentals=0),
    )(got.reshape(DEVS * BLK, 128), response.reshape(FX * FY, NB))
    west, east, ocean = lax.optimization_barrier((west, east, ocean))
    edge_tiles, edge_words, counts, edge_contact, wide = pl.pallas_call(
        edge_kernel,
        out_shape=[
            jax.ShapeDtypeStruct((NCH, 4, 128, 128), F32),
            jax.ShapeDtypeStruct((NCH, 128), I32),
            jax.ShapeDtypeStruct((2,), I32),
            jax.ShapeDtypeStruct((2, R, 128), F32),
            jax.ShapeDtypeStruct((5, R, 128), F32),
        ],
        in_specs=[vspec()] * 2 + [aspec()] + [vspec()] * 4,
        out_specs=[aspec(), vspec(), sspec(), vspec(), vspec()],
        scratch_shapes=[
            pltpu.VMEM((4, R, TW, 128), F32),
            pltpu.VMEM((NCH, 4, 128, 128), F32),
            pltpu.VMEM((4, 128, 128), F32),
            pltpu.VMEM((2, NCH, 128), I32),
            pltpu.SMEM((2, NCH, 128), I32),
            *chunk_scratch,
            pltpu.SemaphoreType.DMA((21,)),
            pltpu.SemaphoreType.DMA((NCH,)),
        ],
        compiler_params=params(),
        name="edge_pairs",
        cost_estimate=pl.CostEstimate(flops=500000000, bytes_accessed=8 << 20, transcendentals=8 << 20),
    )(up, state, outline, north, south, west, east)

    force = jnp.concatenate([contact + edge_contact + ocean, ocean], axis=0)
    w = 2 * H - 1
    low, high = moved(force[:, FX : FX + w], "gx", True), moved(force[:, 1 : 1 + w], "gx", False)
    force = force + jnp.pad(low, ((0, 0), (0, R - w), (0, 0))) + jnp.pad(high, ((0, 0), (R - w, 0), (0, 0)))
    low, high = moved(force[:, :, FY : FY + w], "gy", True), moved(force[:, :, 1 : 1 + w], "gy", False)
    c = FY + 2 * H
    force = force + jnp.pad(low, ((0, 0), (0, 0), (0, 128 - w))) + jnp.pad(high, ((0, 0), (0, 0), (c - w, 128 - c)))

    vel, shift = pl.pallas_call(
        later_kernel,
        name="later_steps",
        out_shape=[jax.ShapeDtypeStruct((FX, 2, FY), F32)] * 2,
        in_specs=[sspec(), sspec()] + [vspec()] * 4 + [aspec()] * 2,
        out_specs=[vspec()] * 2,
        scratch_shapes=[
            pltpu.VMEM((OWN + NCH, 128), I32),
            pltpu.VMEM((OWN + NCH, 4, 128, 128), F32),
            *chunk_scratch,
            pltpu.VMEM((5, R, 128), F32),
            pltpu.SemaphoreType.DMA((OWN + NCH,)),
        ],
        compiler_params=params(),
        cost_estimate=pl.CostEstimate(flops=500000000, bytes_accessed=4 << 20, transcendentals=16 << 20),
    )(pair_count, counts, force, wide, words, edge_words, tiles, edge_tiles)
    return jnp.transpose(vel, (0, 2, 1)), jnp.transpose(shift, (0, 2, 1))


def solution(mesh):
    return jax.shard_map(
        shards,
        mesh=mesh,
        in_specs=(
            P("gx", "gy", None),
            P("gx", "gy", None),
            P("gx", "gy", None),
            P("gx", "gy"),
            P("gx", "gy", None),
            P("gx", "gy", None, None),
            P("gx", "gy"),
            P(("gx", "gy"), None),
            P(("gx", "gy"), None),
            P(("gx", "gy")),
        ),
        out_specs=(P("gx", "gy", None), P("gx", "gy", None)),
        check_vma=False,
    )
```

```python
import math

import jax
import jax.numpy as jnp
from jax import lax
from jax.experimental import pallas as pl
from jax.experimental.pallas import tpu as pltpu
from jax.sharding import PartitionSpec as P

FX, FY, V, TILE, NB, PMAX = 32, 64, 256, 128, 64, 512
DEVS, CAP, BLK = 128, 40, 41
STEPS = 3
DT, DRAG = 0.1, 0.5
H = 2
R = FX + 2 * H
RP = 40
PACK = H * FY + 16
SIDE = R * H + 16
RK = 48
CP = 72
TW = FY + 16
PADC = 8 - H
NCH = 9 * PMAX // 128
OWN = PMAX // 128
NEIGH = ((0, 0), (-1, 0), (1, 0), (-1, -1), (0, -1), (1, -1), (-1, 1), (0, 1), (1, 1))
SC = math.sqrt(100.0 * math.log2(math.e))
F32, BF16, I32 = jnp.float32, jnp.bfloat16, jnp.int32
VMEM_BYTES = 52 * 1024 * 1024


def params(size=VMEM_BYTES):
    return pltpu.CompilerParams(vmem_limit_bytes=size)


def vspec():
    return pl.BlockSpec(memory_space=pltpu.VMEM)


def sspec():
    return pl.BlockSpec(memory_space=pltpu.SMEM)


def aspec():
    return pl.BlockSpec(memory_space=pl.ANY)


def nt(a, b):
    return lax.dot_general(a, b, (((1,), (1,)), ((), ())), preferred_element_type=F32)


def nn(a, b):
    return jnp.dot(a, b, preferred_element_type=F32)


def split3(x):
    a = x.astype(BF16).astype(F32)
    b = (x - a).astype(BF16).astype(F32)
    return a, b, (x - a - b).astype(BF16).astype(F32)


def pack_kernel(count_ref, pairs_ref, centres_ref, velocity_ref, mass_ref, outline_ref, up_ref, down_ref, state_ref, sems):
    copies = []
    for k, (out, lo) in enumerate(((up_ref, FX - H), (down_ref, 0))):
        for h in range(H):
            target = out.at[h * FY : h * FY + FY, :]
            copies.append(pltpu.make_async_copy(outline_ref.at[lo + h], target, sems.at[k * H + h]))
    for copy in copies:
        copy.start()
    at = H * FY
    tail = jnp.zeros((11, 512), F32)
    count = jnp.full((1, 512), count_ref[0, 0], I32).astype(F32)
    for k in range(2):
        state_ref[k] = centres_ref[:, k, :]
        state_ref[2 + k] = velocity_ref[:, k, :]
    state_ref[4] = mass_ref[...]
    for out, lo in ((up_ref, FX - H), (down_ref, 0)):
        out[at : at + 4, :] = pairs_ref[...].astype(F32)
        out[at + 4 : at + 5, :] = count
        out[at + 5 : at + 16, :] = tail
        for k in range(5):
            out[at + 5 + k * H : at + 5 + k * H + H, 0:FY] = state_ref[k, lo : lo + H, :]
    for copy in copies:
        copy.wait()


def turn_kernel(own_ref, north_ref, south_ref, state_ref, last_ref, first_ref, west_ref, east_ref):
    at, top = H * FY, R * H
    edge = jnp.zeros((FX, 128 - FY), F32)
    lane = lax.broadcasted_iota(I32, (R, 128), 1)
    planes = []
    for k in range(5):
        rows = jnp.concatenate([state_ref[k], edge], axis=1)
        place = at + 5 + k * H
        ends = [ref[place : place + H, 0:128] for ref in (north_ref, south_ref)]
        planes.append(jnp.concatenate([ends[0], rows, ends[1]], axis=0))
    for out, cols, lo in ((west_ref, last_ref, FY - H), (east_ref, first_ref, 0)):
        for h in range(H):
            out[h * H : h * H + H, :] = north_ref[h * FY + lo : h * FY + lo + H, :]
            low = top - H * H + h * H
            out[low : low + H, :] = south_ref[h * FY + lo : h * FY + lo + H, :]
        out[H * H : H * H + FX * H, :] = cols[...]
        for k, ref in enumerate((north_ref, own_ref, south_ref)):
            out[top + 5 * k : top + 5 * k + 5, :] = ref[at : at + 5, :]
        out[top + 15 : top + 16, :] = jnp.zeros((1, 512), F32)
        block = jnp.zeros((R, 128), F32)
        for k in range(5):
            turned = pltpu.roll(planes[k], (H * k - lo) % 128, 1)
            block = jnp.where((lane >= H * k) & (lane < H * k + H), turned, block)
        out[SIDE : SIDE + R, :] = jnp.concatenate([block, jnp.zeros((R, 384), F32)], axis=1)


def send_kernel(dest_in, floe_in, rows_in, out_ref, dest_ref, floe_ref, rows_ref, place_v, ids_v, place_s, sem, sems):
    ins = [
        pltpu.make_async_copy(source, target, sems.at[k])
        for k, (source, target) in enumerate(((dest_in, dest_ref), (floe_in, floe_ref), (rows_in, rows_ref)))
    ]
    for copy in ins:
        copy.start()
    upper = (
        lax.broadcasted_iota(I32, (128, 128), 0) < lax.broadcasted_iota(I32, (128, 128), 1)
    ).astype(F32).astype(BF16)
    ones = jnp.ones((128, 128), BF16)
    index = lax.broadcasted_iota(I32, (128, 128), 0)
    @pl.loop(0, out_ref.shape[0] // 128)
    def _(i):
        out_ref[pl.ds(pl.multiple_of(i * 128, 128), 128), :] = jnp.zeros((128, 128), F32)

    ins[0].wait()
    ins[1].wait()
    blocks = dest_ref.shape[0]
    hots = [(index == dest_ref[k : k + 1, :]).astype(F32) for k in range(blocks)]
    hot16 = jnp.concatenate([hot.astype(BF16) for hot in hots], axis=0)
    before = nn(hot16, upper)
    full = nn(hot16, ones)
    carry = jnp.zeros((128, 128), F32)
    high, low, slots = [], [], []
    for k in range(blocks):
        rank = jnp.sum(hots[k] * (before[128 * k : 128 * k + 128] + carry), axis=0, keepdims=True)
        carry = carry + full[128 * k : 128 * k + 128]
        rank = rank.astype(I32)
        place_v[k : k + 1, :] = dest_ref[k : k + 1, :] * BLK + rank
        floe = floe_ref[k : k + 1, :] + 1
        slots.append((index == rank).astype(F32).astype(BF16))
        high.append((hots[k] * (floe >> 6).astype(F32)).astype(BF16))
        low.append((hots[k] * (floe & 63).astype(F32)).astype(BF16))
    slots = jnp.concatenate(slots, axis=1)
    ids = 64.0 * nt(jnp.concatenate(high, axis=1), slots) + nt(jnp.concatenate(low, axis=1), slots)
    ids_v[...] = ids
    copy = pltpu.make_async_copy(place_v, place_s, sem)
    copy.start()

    copy.wait()
    ins[2].wait()

    @pl.loop(0, rows_ref.shape[0] // 128)
    def _(k):
        for j in range(128):
            out_ref[pl.ds(place_s[k, j], 1), :] = rows_ref[pl.ds(k * 128 + j, 1), :]

    for d in range(DEVS):
        out_ref[d * BLK + CAP : d * BLK + CAP + 1, :] = ids_v[d : d + 1, :]


def ocean_kernel(rows_ref, resp_ref, out_ref, acc_ref, ids_ref):
    groups = DEVS // 16
    lane = lax.broadcasted_iota(I32, (groups, 128), 1)
    blocks = [jnp.zeros((groups, 128), F32) for _ in range(5)]
    for j in range(16):
        ids = rows_ref[pl.ds(j * BLK + CAP, groups, stride=16 * BLK), :]
        shift = (CAP * j) % 128
        if shift:
            ids = pltpu.roll(ids, shift, 1)
        for b in range(5):
            if CAP * j < 128 * b + 128 and CAP * j + CAP > 128 * b:
                place = lane + (128 * b - CAP * j)
                blocks[b] = jnp.where((place >= 0) & (place < CAP), ids, blocks[b])
    for b in range(5):
        ids_ref[b] = blocks[b]
    base16 = lax.broadcasted_iota(I32, (16, 128), 0).astype(F32)
    one, zero = jnp.ones((16, 128), BF16), jnp.zeros((16, 128), BF16)

    rows = jnp.concatenate([rows_ref[BLK * j : BLK * j + CAP, :] for j in range(DEVS)], axis=0)
    high = rows.astype(BF16)
    low = (rows - high.astype(F32)).astype(BF16)
    both = jnp.concatenate([high, low], axis=1)
    ids = [ids_ref[b, h : h + 1, :] for h in range(groups) for b in range(5)]
    for part in range(8):
        cols = []
        for row in ids:
            rel = jnp.broadcast_to(row - (part * 256 + 1.0), (16, 128)).astype(BF16)
            cols.append(
                jnp.concatenate(
                    [jnp.where((base16 + 16.0 * k).astype(BF16) == rel, one, zero) for k in range(16)], axis=0
                )
            )
        acc_ref[part * 256 : part * 256 + 256, :] = nn(jnp.concatenate(cols, axis=1), both)

    out_ref[...] = jnp.zeros_like(out_ref)
    srow = lax.broadcasted_iota(I32, (16, 128), 0)
    slane = lax.broadcasted_iota(I32, (16, 128), 1)
    pick = (((srow == 0) & (slane < NB)) | ((srow == 1) & (slane >= NB))).astype(F32).astype(BF16)
    inner = (slane >= H) & (slane < H + FY)

    for part in range(8):
        at = part * 256
        total = acc_ref[pl.ds(at, 256), 0:128] + acc_ref[pl.ds(at, 256), 128:256]
        resp = resp_ref[pl.ds(at, 256), :]
        a, b, c = split3(total * jnp.concatenate([resp, resp], axis=1))
        force = nt(pick, a.astype(BF16)) + nt(pick, b.astype(BF16)) + nt(pick, c.astype(BF16))
        for j in range(4):
            piece = force[:, (j // 2) * 128 : (j // 2) * 128 + 128]
            piece = pltpu.roll(piece, (H - 64 * (j % 2)) % 128, 1)
            piece = jnp.where(inner, piece, 0.0)
            for k in range(2):
                out_ref[k, part * 4 + j + H : part * 4 + j + H + 1, :] = piece[k : k + 1]


def put_shift(left_ref, plane_ref, planes):
    for k in range(2):
        plane_ref[0:R, :] = planes[k]
        for j, part in enumerate(split3(jnp.transpose(plane_ref[...])[0:CP])):
            left_ref[3 * k + j] = part


def look_up(word, left_ref):
    count = word.shape[1]
    rows = jnp.concatenate([(word >> 7) & 63, (word >> 20) & 63], axis=1)
    cols = jnp.concatenate([word & 127, (word >> 13) & 127], axis=1)
    step_x, step_y = code_steps((word >> 28) & 7)
    row_hot16 = (lax.broadcasted_iota(I32, (RK, 2 * count), 0) == rows).astype(F32).astype(BF16)
    col_hot = lax.broadcasted_iota(I32, (CP, 2 * count), 0) == cols
    offsets = []
    for k, step in enumerate((step_x, step_y)):
        left = jnp.concatenate([left_ref[3 * k + j, :, 0:RK] for j in range(3)], axis=0)
        part = nn(left.astype(BF16), row_hot16)
        part = part[0:CP] + part[CP : 2 * CP] + part[2 * CP : 3 * CP]
        part = jnp.sum(jnp.where(col_hot, part, 0.0), axis=0, keepdims=True)
        offsets.append((step.astype(F32) - (part[:, 0:count] - part[:, count : 2 * count])) * SC)
    return offsets


def add_forces(word, ok, fx, fy, acc_ref):
    rows = jnp.concatenate([(word >> 7) & 63, (word >> 20) & 63], axis=1)
    cols = jnp.concatenate([word & 127, (word >> 13) & 127], axis=1)
    row_hot = (lax.broadcasted_iota(I32, (RP, rows.shape[1]), 0) == rows).astype(F32)
    col_hot = (lax.broadcasted_iota(I32, (128, rows.shape[1]), 0) == cols).astype(F32).astype(BF16)
    parts = split3(jnp.where(ok, fx, 0.0)) + split3(jnp.where(ok, fy, 0.0))
    spread = [row_hot * jnp.concatenate([part, -part], axis=1) for part in parts]
    acc_ref[...] += nt(jnp.concatenate(spread, axis=0).astype(BF16), col_hot)


def chunk_forces(c, half, dx, dy, tiles_ref, b_ref):
    px = tiles_ref[c, 2] + dx
    py = tiles_ref[c, 3] + dy
    b_ref[0] = 2.0 * px
    b_ref[1] = 2.0 * py
    b_ref[2] = -(px * px + py * py)
    turns = jnp.where(half, TILE // 64, TILE // 32)

    @pl.when(half)
    def _():
        left_half = lax.broadcasted_iota(I32, (64, 128), 1) < 64
        for k in range(3):
            b_ref[k, 0:64, :] = jnp.where(left_half, b_ref[k, 0:64, :], b_ref[k, 64:128, :])

    force_x = jnp.zeros((8, 128), F32)
    force_y = jnp.zeros((8, 128), F32)
    back_x = jnp.zeros((8, 128), F32)
    back_y = jnp.zeros((8, 128), F32)
    for half in range(2):
        ax = [tiles_ref[c, 0, half * 64 + 8 * k : half * 64 + 8 * k + 8, :] for k in range(8)]
        ay = [tiles_ref[c, 1, half * 64 + 8 * k : half * 64 + 8 * k + 8, :] for k in range(8)]
        na = [-(x * x + y * y) for x, y in zip(ax, ay)]

        def body(i, carry):
            sums, bx_sum, by_sum = carry
            sums = list(sums)
            for j in range(32):
                w = i * 32 + j
                bx = jnp.broadcast_to(b_ref[0, pl.ds(w, 1), :], (8, 128))
                by = jnp.broadcast_to(b_ref[1, pl.ds(w, 1), :], (8, 128))
                nb = jnp.broadcast_to(b_ref[2, pl.ds(w, 1), :], (8, 128))
                weights = [jnp.exp2((ax[k] * bx + ay[k] * by) + (na[k] + nb)) for k in range(8)]
                sums = [s + t for s, t in zip(sums, weights)]
                while len(weights) > 1:
                    weights = [weights[k] + weights[k + 1] for k in range(0, len(weights), 2)]
                bx_sum = bx_sum + weights[0] * bx
                by_sum = by_sum + weights[0] * by
            return tuple(sums), bx_sum, by_sum

        sums, back_x, back_y = lax.fori_loop(
            0, turns, body, (tuple(jnp.zeros((8, 128), F32) for _ in range(8)), back_x, back_y)
        )
        for k in range(8):
            force_x = force_x + ax[k] * sums[k]
            force_y = force_y + ay[k] * sums[k]
    fx = jnp.sum(force_x - 0.5 * back_x, axis=0, keepdims=True) * (1.0 / SC)
    fy = jnp.sum(force_y - 0.5 * back_y, axis=0, keepdims=True) * (1.0 / SC)
    return fx, fy


def contact_chunk(c, half_at, live, words_ref, tiles_ref, left_ref, b_ref, acc_ref):
    word = words_ref[pl.ds(c, 1), :]
    lane = lax.broadcasted_iota(I32, (1, 128), 1)
    ok = (word >= 0) & (c * 128 + jnp.where(c == half_at, lane & 63, lane) < live)
    dx, dy = look_up(word, left_ref)
    fx, fy = chunk_forces(c, c == half_at, dx, dy, tiles_ref, b_ref)
    add_forces(word, ok, fx, fy, acc_ref)


def acc_plane(acc_ref, k):
    at = 3 * RP * k
    return acc_ref[at : at + R, :] + acc_ref[at + RP : at + RP + R, :] + acc_ref[at + 2 * RP : at + 2 * RP + R, :]


def code_steps(code):
    code9 = code + (code >= 4).astype(I32)
    step = (code9 >= 3).astype(I32) + (code9 >= 6).astype(I32)
    return step - 1, code9 - 3 * step - 1


def pair_words(local, code, mine, theirs, count, di, dj):
    step_x, step_y = code_steps(code)
    row = (local >> 6) + di * FX
    col = (local & 63) + dj * FY
    prow = row + step_x
    pcol = col + step_y
    row_all = prow + lax.axis_index("gx") * FX
    col_all = pcol + lax.axis_index("gy") * FY
    live = lax.broadcasted_iota(I32, local.shape, 1) < count
    live = live & (row_all >= 0) & (row_all < lax.axis_size("gx") * FX)
    live = live & (col_all >= 0) & (col_all < lax.axis_size("gy") * FY)
    inside = (prow >= 0) & (prow < FX) & (pcol >= 0) & (pcol < FY)
    near = (row >= -1) & (row <= FX) & (col >= -1) & (col <= FY)
    near = near | ((prow >= -1) & (prow <= FX) & (pcol >= -1) & (pcol <= FY))
    word = (row + H) * 128 + col + H + (((prow + H) * 128 + pcol + H) << 13)
    return word + (mine << 26) + (theirs << 27) + (code << 28), live, inside, near


def load_tiles(c, place_s, flat, size, stage, tiles):
    @pl.loop(0, 16)
    def _(i):
        for j in range(8):
            at = i * 8 + j
            own = place_s[0, c, at]
            other = place_s[1, c, at]
            stage[0, pl.ds(at, 1), :] = flat[pl.ds(own, 1), :]
            stage[1, pl.ds(at, 1), :] = flat[pl.ds(own + 2 * size, 1), :]
            stage[2, pl.ds(at, 1), :] = flat[pl.ds(other, 1), :]
            stage[3, pl.ds(at, 1), :] = flat[pl.ds(other + 2 * size, 1), :]

    for k in range(4):
        tiles[c, k] = jnp.transpose(stage[k]) * SC


def inner_kernel(
    count_ref, own_ref, state_ref, outline_ref, tiles, words_out, force_out, last_ref, first_ref,
    table, stage, place_v, place_s, left_ref, plane_ref, b_ref, acc_ref, sems,
):
    copies = []
    for q in range(4):
        source = outline_ref.at[:, :, slice(q * 128, q * 128 + 128)]
        copies.append(pltpu.make_async_copy(source, table.at[q], sems.at[q]))
    for copy in copies:
        copy.start()
    live = count_ref[0, 0]
    fields = [own_ref[k : k + 1, :] for k in range(4)]
    word, ok, inside, _ = pair_words(*fields, live, 0, 0)
    word = jnp.where(ok & inside, word, -1)
    for b in range(OWN):
        words_out[b : b + 1, :] = word[:, 128 * b : 128 * b + 128]
    word = jnp.maximum(words_out[...], H * 128 + H + ((H * 128 + H) << 13))
    own = (((word >> 7) & 63) - H) * FY + (word & 127) - H
    other = (((word >> 20) & 63) - H) * FY + ((word >> 13) & 127) - H
    place_v[0] = own + ((word >> 26) & 1) * (FX * FY)
    place_v[1] = other + ((word >> 27) & 1) * (FX * FY)
    copy = pltpu.make_async_copy(place_v, place_s, sems.at[4])
    copy.start()
    plane_ref[...] = jnp.zeros_like(plane_ref)
    acc_ref[...] = jnp.zeros_like(acc_ref)
    edge = jnp.zeros((FX, 128 - FY), F32)
    planes = []
    for k in range(2):
        plane = pltpu.roll(jnp.concatenate([state_ref[k], edge], axis=1), H, 1)
        ends = jnp.zeros((H, 128), F32)
        planes.append(jnp.concatenate([ends, plane, ends], axis=0))
    put_shift(left_ref, plane_ref, planes)
    for piece in copies:
        piece.wait()
    copy.wait()
    for out, lo in ((last_ref, FY - H), (first_ref, 0)):
        for r in range(FX):
            for q in range(4):
                out[r * H : r * H + H, q * 128 : q * 128 + 128] = table[q, r, lo : lo + H, :]
    flat = table.reshape(4 * FX * FY, 128)

    @pl.loop(0, (live + 127) >> 7)
    def _(c):
        load_tiles(c, place_s, flat, FX * FY, stage, tiles)
        contact_chunk(c, -1, PMAX, words_out, tiles, left_ref, b_ref, acc_ref)

    for k in range(2):
        force_out[k] = acc_plane(acc_ref, k)


def edge_kernel(
    own_ref, state_ref, outline_ref, north_ref, south_ref, west_ref, east_ref,
    tiles_out, words_out, count_out, force_out, wide_ref,
    table, tiles, stage, place_v, place_s, left_ref, plane_ref, b_ref, acc_ref, sems, tile_sems,
):
    copies = []
    for q in range(4):
        lanes = slice(q * 128, q * 128 + 128)
        target = table.at[q, H : H + FX, 8 : 8 + FY, :]
        copies.append(pltpu.make_async_copy(outline_ref.at[:, :, lanes], target, sems.at[3 * q]))
        for h in range(H):
            table[q, h, 8 : 8 + FY, :] = north_ref[h * FY : h * FY + FY, lanes]
            table[q, H + FX + h, 8 : 8 + FY, :] = south_ref[h * FY : h * FY + FY, lanes]
        for r in range(R):
            table[q, r, PADC:8, :] = west_ref[r * H : r * H + H, lanes]
            table[q, r, 8 + FY : 8 + FY + H, :] = east_ref[r * H : r * H + H, lanes]
    for copy in copies:
        copy.start()
    edge = jnp.zeros((FX, 128 - FY), F32)

    lane = lax.broadcasted_iota(I32, (R, 128), 1)
    inside = (lane >= H) & (lane < H + FY)
    for k in range(5):
        at = H * FY + 5 + k * H
        rows = jnp.concatenate([state_ref[k], edge], axis=1)
        rows = jnp.concatenate([north_ref[at : at + H, 0:128], rows, south_ref[at : at + H, 0:128]], axis=0)
        left = pltpu.roll(west_ref[SIDE : SIDE + R, 0:128], (-H * k) % 128, 1)
        right = pltpu.roll(east_ref[SIDE : SIDE + R, 0:128], (H + FY - H * k) % 128, 1)
        plane = jnp.where(inside, pltpu.roll(rows, H, 1), jnp.where(lane < H, left, right))
        plane = jnp.where(lane < FY + 2 * H, plane, 0.0)
        wide_ref[k] = jnp.where(plane == 0.0, 1.0, plane) if k == 4 else plane
    top = R * H
    heads = [
        (own_ref, H * FY), (north_ref, H * FY), (south_ref, H * FY), (west_ref, top), (west_ref, top + 5),
        (west_ref, top + 10), (east_ref, top), (east_ref, top + 5), (east_ref, top + 10),
    ]
    fields = [
        jnp.concatenate([ref[at + k : at + k + 1, :] for ref, at in heads], axis=0).astype(I32) for k in range(5)
    ]
    lists = len(NEIGH)
    number = lax.broadcasted_iota(I32, (lists, PMAX), 0)
    di, dj = jnp.zeros((lists, PMAX), I32), jnp.zeros((lists, PMAX), I32)
    for k, (i, j) in enumerate(NEIGH):
        di = jnp.where(number == k, i, di)
        dj = jnp.where(number == k, j, dj)
    word, ok, inside, near = pair_words(*fields, di, dj)
    ok = ok & near & ((number > 0) | ~inside)
    flags = jnp.where(ok, 1.0, 0.0)
    upper = (
        lax.broadcasted_iota(I32, (PMAX, PMAX), 0) < lax.broadcasted_iota(I32, (PMAX, PMAX), 1)
    ).astype(F32).astype(BF16)
    rank = nn(flags.astype(BF16), upper)
    base = jnp.zeros((1, 1), F32)
    ranks = []
    for k in range(lists):
        ranks.append(jnp.where(flags[k : k + 1] > 0.0, rank[k : k + 1] + base, -1.0).astype(I32))
        base = base + jnp.sum(flags[k : k + 1], axis=1, keepdims=True)
    found_all = jnp.sum(flags).astype(I32)
    mine = jnp.sum(flags[0:1]).astype(I32)
    total = (found_all + 127) >> 7
    whole = (found_all + 63) >> 7
    half_at = jnp.where(total > whole, total - 1, -1)
    words_out[...] = jnp.full(words_out.shape, -1, I32)
    slot = lax.broadcasted_iota(I32, (128, PMAX), 0)
    srow = lax.broadcasted_iota(I32, (16, PMAX), 0)
    pieces = []
    for k in range(lists):
        one = word[k : k + 1]
        piece = jnp.where(srow == 0, one & 255, jnp.where(srow == 1, (one >> 8) & 255, 0))
        piece = jnp.where(srow == 2, (one >> 16) & 255, jnp.where(srow == 3, (one >> 24) & 127, piece))
        piece = jnp.where(srow == 4, 1, piece)
        pieces.append(piece.astype(F32).astype(BF16))

    @pl.loop(0, total)
    def _(i):
        found = jnp.zeros((16, 128), F32)
        want = jnp.where(i >= whole, slot & 63, slot)
        for k in range(lists):
            found = found + nt(pieces[k], (want == ranks[k] - i * 128).astype(F32).astype(BF16))
        found = found.astype(I32)
        value = found[0:1] + (found[1:2] << 8) + (found[2:3] << 16) + (found[3:4] << 24)
        words_out[pl.ds(i, 1), :] = jnp.where(found[4:5] > 0, value, -1)

    word = jnp.maximum(words_out[...], 0)
    own = ((word >> 7) & 63) * TW + (word & 127) + PADC
    other = ((word >> 20) & 63) * TW + ((word >> 13) & 127) + PADC
    place_v[0] = own + ((word >> 26) & 1) * (R * TW)
    place_v[1] = other + ((word >> 27) & 1) * (R * TW)
    copy = pltpu.make_async_copy(place_v, place_s, sems.at[20])
    copy.start()
    count_out[0] = total
    count_out[1] = half_at
    plane_ref[...] = jnp.zeros_like(plane_ref)
    acc_ref[...] = jnp.zeros_like(acc_ref)
    put_shift(left_ref, plane_ref, [wide_ref[0], wide_ref[1]])
    for piece in copies:
        piece.wait()

    copy.wait()
    flat = table.reshape(4 * R * TW, 128)

    @pl.loop(0, total)
    def _(c):
        load_tiles(c, place_s, flat, R * TW, stage, tiles)
        pltpu.make_async_copy(tiles.at[c], tiles_out.at[c], tile_sems.at[c]).start()

    @pl.loop(0, (mine + 127) >> 7)
    def _(c):
        contact_chunk(c, half_at, mine, words_out, tiles, left_ref, b_ref, acc_ref)

    for k in range(2):
        force_out[k] = acc_plane(acc_ref, k)

    @pl.loop(0, total)
    def _(c):
        pltpu.make_async_copy(tiles.at[c], tiles_out.at[c], tile_sems.at[c]).wait()


def later_kernel(
    live_ref, count_ref, force_ref, state_ref, words_in, edge_words, tiles_in, edge_tiles, vel_out, shift_out,
    words_ref, tiles, left_ref, plane_ref, b_ref, acc_ref, now_ref, move_ref, tile_sems,
):
    inner = (live_ref[0, 0] + 127) >> 7
    total = count_ref[0] + inner
    half_at = jnp.where(count_ref[1] >= 0, count_ref[1] + OWN, -1)

    @pl.loop(0, inner)
    def _(c):
        pltpu.make_async_copy(tiles_in.at[c], tiles.at[c], tile_sems.at[c]).start()

    @pl.loop(0, total - inner)
    def _(c):
        pltpu.make_async_copy(edge_tiles.at[c], tiles.at[c + OWN], tile_sems.at[c + OWN]).start()

    words_ref[0:OWN, :] = words_in[0:OWN, :]
    words_ref[OWN : OWN + NCH, :] = edge_words[...]
    words_ref[OWN + NCH : OWN + NCH + 8, :] = jnp.full((8, 128), -1, I32)
    now_ref[...] = state_ref[...]

    def update(forces):
        scale = DT / now_ref[4]
        for k in range(2):
            vel = now_ref[2 + k]
            vel = vel + (forces[k] - DRAG * vel) * scale
            now_ref[2 + k] = vel
            now_ref[k] = now_ref[k] + DT * vel

    update([force_ref[0], force_ref[1]])
    plane_ref[...] = jnp.zeros_like(plane_ref)

    move_ref[...] = jnp.zeros_like(move_ref)
    twos = (total + 1) >> 1

    def spot(i):
        return jnp.where(i < inner, i, i - inner + OWN)

    def two_words(i):
        return jnp.concatenate([words_ref[pl.ds(spot(2 * i + j), 1), :] for j in range(2)], axis=1)

    @pl.loop(1, STEPS)
    def _(step):
        put_shift(left_ref, plane_ref, [now_ref[0], now_ref[1]])
        acc_ref[...] = jnp.zeros_like(acc_ref)

        @pl.loop(0, twos)
        def _(i):
            for k, offset in enumerate(look_up(two_words(i), left_ref)):
                for j in range(2):
                    move_ref[k, pl.ds(2 * i + j, 1), :] = offset[:, 128 * j : 128 * j + 128]

        @pl.when(step == 1)
        def _():
            @pl.loop(0, inner)
            def _(c):
                pltpu.make_async_copy(tiles_in.at[c], tiles.at[c], tile_sems.at[c]).wait()

            @pl.loop(0, total - inner)
            def _(c):
                pltpu.make_async_copy(edge_tiles.at[c], tiles.at[c + OWN], tile_sems.at[c + OWN]).wait()

        @pl.loop(0, total)
        def _(i):
            c = spot(i)
            dx, dy = [move_ref[k, pl.ds(i, 1), :] for k in range(2)]
            fx, fy = chunk_forces(c, c == half_at, dx, dy, tiles, b_ref)
            move_ref[2, pl.ds(i, 1), :] = fx
            move_ref[3, pl.ds(i, 1), :] = fy

        @pl.loop(0, twos)
        def _(i):
            word = two_words(i)
            fx, fy = [
                jnp.concatenate([move_ref[k, pl.ds(2 * i + j, 1), :] for j in range(2)], axis=1) for k in (2, 3)
            ]
            add_forces(word, word >= 0, fx, fy, acc_ref)

        update([acc_plane(acc_ref, k) + force_ref[2 + k] for k in range(2)])

    for out, base in ((shift_out, 0), (vel_out, 2)):
        for k in range(2):
            plane_ref[0:R, :] = pltpu.roll(now_ref[base + k], 128 - H, 1)
            for r in range(FX):
                out[r, k : k + 1, :] = plane_ref[r + H : r + H + 1, 0:FY]


def moved(x, axis, up):
    count = lax.axis_size(axis)
    pairs = [(i, i + 1) if up else (i + 1, i) for i in range(count - 1)]
    return lax.ppermute(x, axis, pairs)


def shards(
    outline, centres, velocity, mass, response, pairs, pair_count, forcing, ocean_dest, ocean_floe
):
    rows_dev = forcing.shape[0]
    send = pl.pallas_call(
        send_kernel,
        name="send_rows",
        out_shape=jax.ShapeDtypeStruct((DEVS * BLK, 128), F32),
        in_specs=[pl.BlockSpec(memory_space=pltpu.HBM)] * 3,
        out_specs=vspec(),
        scratch_shapes=[
            pltpu.VMEM((rows_dev // 128, 128), I32),
            pltpu.VMEM((rows_dev // 128, 128), I32),
            pltpu.VMEM((rows_dev, 128), F32),
            pltpu.VMEM((rows_dev // 128, 128), I32),
            pltpu.VMEM((DEVS, 128), F32),
            pltpu.SMEM((rows_dev // 128, 128), I32),
            pltpu.SemaphoreType.DMA,
            pltpu.SemaphoreType.DMA((3,)),
        ],
        compiler_params=params(63 << 20),
        cost_estimate=pl.CostEstimate(flops=100000000, bytes_accessed=4 << 20, transcendentals=0),
    )(ocean_dest.reshape(rows_dev // 128, 128), ocean_floe.reshape(rows_dev // 128, 128), forcing)
    pair_rows = jnp.transpose(pairs[0, 0], (1, 0))
    mass, send = lax.optimization_barrier((mass, send))
    got = lax.all_to_all(
        send.reshape(DEVS, 1, BLK * 128), ("gx", "gy"), split_axis=0, concat_axis=0, tiled=True
    )
    up, down, state = pl.pallas_call(
        pack_kernel,
        name="pack_rows",
        out_shape=[jax.ShapeDtypeStruct((PACK, 512), F32)] * 2 + [jax.ShapeDtypeStruct((5, FX, FY), F32)],
        in_specs=[sspec()] + [vspec()] * 4 + [aspec()],
        out_specs=[vspec()] * 3,
        scratch_shapes=[pltpu.SemaphoreType.DMA((2 * H,))],
        compiler_params=params(),
        cost_estimate=pl.CostEstimate(flops=1000000, bytes_accessed=1 << 20, transcendentals=0),
    )(pair_count, pair_rows, jnp.transpose(centres, (0, 2, 1)), jnp.transpose(velocity, (0, 2, 1)), mass, outline)

    chunk_scratch = [
        pltpu.VMEM((6, CP, 128), F32),
        pltpu.VMEM((128, 128), F32),
        pltpu.VMEM((3, 128, 128), F32),
        pltpu.VMEM((6 * RP, 128), F32),
    ]
    tiles, words, contact, last, first = pl.pallas_call(
        inner_kernel,
        name="inner_pairs",
        out_shape=[
            jax.ShapeDtypeStruct((OWN, 4, 128, 128), F32),
            jax.ShapeDtypeStruct((OWN, 128), I32),
            jax.ShapeDtypeStruct((2, R, 128), F32),
            jax.ShapeDtypeStruct((FX * H, 512), F32),
            jax.ShapeDtypeStruct((FX * H, 512), F32),
        ],
        in_specs=[sspec(), vspec(), vspec(), aspec()],
        out_specs=[vspec()] * 5,
        scratch_shapes=[
            pltpu.VMEM((4, FX, FY, 128), F32),
            pltpu.VMEM((4, 128, 128), F32),
            pltpu.VMEM((2, OWN, 128), I32),
            pltpu.SMEM((2, OWN, 128), I32),
            *chunk_scratch,
            pltpu.SemaphoreType.DMA((5,)),
        ],
        compiler_params=params(),
        cost_estimate=pl.CostEstimate(flops=500000000, bytes_accessed=8 << 20, transcendentals=8 << 20),
    )(pair_count, pair_rows, state, outline)
    north, south, contact = lax.optimization_barrier((moved(up, "gx", True), moved(down, "gx", False), contact))
    west, east = pl.pallas_call(
        turn_kernel,
        name="pack_columns",
        out_shape=[jax.ShapeDtypeStruct((SIDE + R, 512), F32)] * 2,
        in_specs=[vspec()] * 6,
        out_specs=[vspec()] * 2,
        compiler_params=params(),
        cost_estimate=pl.CostEstimate(flops=1000000, bytes_accessed=1 << 20, transcendentals=0),
    )(up, north, south, state, last, first)
    west, east, got = lax.optimization_barrier((west, east, got))
    west, east = moved(west, "gy", True), moved(east, "gy", False)
    ocean = pl.pallas_call(
        ocean_kernel,
        name="ocean_sum",
        out_shape=jax.ShapeDtypeStruct((2, R, 128), F32),
        in_specs=[vspec()] * 2,
        out_specs=vspec(),
        scratch_shapes=[
            pltpu.VMEM((FX * FY, 256), F32),
            pltpu.VMEM((5, DEVS // 16, 128), F32),
        ],
        compiler_params=params(),
        cost_estimate=pl.CostEstimate(flops=5000000000, bytes_accessed=5 << 20, transcendentals=0),
    )(got.reshape(DEVS * BLK, 128), response.reshape(FX * FY, NB))
    west, east, ocean = lax.optimization_barrier((west, east, ocean))
    edge_tiles, edge_words, counts, edge_contact, wide = pl.pallas_call(
        edge_kernel,
        out_shape=[
            jax.ShapeDtypeStruct((NCH, 4, 128, 128), F32),
            jax.ShapeDtypeStruct((NCH, 128), I32),
            jax.ShapeDtypeStruct((2,), I32),
            jax.ShapeDtypeStruct((2, R, 128), F32),
            jax.ShapeDtypeStruct((5, R, 128), F32),
        ],
        in_specs=[vspec()] * 2 + [aspec()] + [vspec()] * 4,
        out_specs=[aspec(), vspec(), sspec(), vspec(), vspec()],
        scratch_shapes=[
            pltpu.VMEM((4, R, TW, 128), F32),
            pltpu.VMEM((NCH, 4, 128, 128), F32),
            pltpu.VMEM((4, 128, 128), F32),
            pltpu.VMEM((2, NCH, 128), I32),
            pltpu.SMEM((2, NCH, 128), I32),
            *chunk_scratch,
            pltpu.SemaphoreType.DMA((21,)),
            pltpu.SemaphoreType.DMA((NCH,)),
        ],
        compiler_params=params(),
        name="edge_pairs",
        cost_estimate=pl.CostEstimate(flops=500000000, bytes_accessed=8 << 20, transcendentals=8 << 20),
    )(up, state, outline, north, south, west, east)

    force = jnp.concatenate([contact + edge_contact + ocean, ocean], axis=0)
    w = 2 * H - 1
    low, high = moved(force[:, FX : FX + w], "gx", True), moved(force[:, 1 : 1 + w], "gx", False)
    force = force + jnp.pad(low, ((0, 0), (0, R - w), (0, 0))) + jnp.pad(high, ((0, 0), (R - w, 0), (0, 0)))
    low, high = moved(force[:, :, FY : FY + w], "gy", True), moved(force[:, :, 1 : 1 + w], "gy", False)
    c = FY + 2 * H
    force = force + jnp.pad(low, ((0, 0), (0, 0), (0, 128 - w))) + jnp.pad(high, ((0, 0), (0, 0), (c - w, 128 - c)))

    vel, shift = pl.pallas_call(
        later_kernel,
        name="later_steps",
        out_shape=[jax.ShapeDtypeStruct((FX, 2, FY), F32)] * 2,
        in_specs=[sspec(), sspec()] + [vspec()] * 4 + [aspec()] * 2,
        out_specs=[vspec()] * 2,
        scratch_shapes=[
            pltpu.VMEM((OWN + NCH + 8, 128), I32),
            pltpu.VMEM((OWN + NCH, 4, 128, 128), F32),
            *chunk_scratch,
            pltpu.VMEM((5, R, 128), F32),
            pltpu.VMEM((4, OWN + NCH + 8, 128), F32),
            pltpu.SemaphoreType.DMA((OWN + NCH,)),
        ],
        compiler_params=params(),
        cost_estimate=pl.CostEstimate(flops=500000000, bytes_accessed=4 << 20, transcendentals=16 << 20),
    )(pair_count, counts, force, wide, words, edge_words, tiles, edge_tiles)
    return jnp.transpose(vel, (0, 2, 1)), jnp.transpose(shift, (0, 2, 1))


def solution(mesh):
    return jax.shard_map(
        shards,
        mesh=mesh,
        in_specs=(
            P("gx", "gy", None),
            P("gx", "gy", None),
            P("gx", "gy", None),
            P("gx", "gy"),
            P("gx", "gy", None),
            P("gx", "gy", None, None),
            P("gx", "gy"),
            P(("gx", "gy"), None),
            P(("gx", "gy"), None),
            P(("gx", "gy")),
        ),
        out_specs=(P("gx", "gy", None), P("gx", "gy", None)),
        check_vma=False,
    )
```

```python
import math

import jax
import jax.numpy as jnp
from jax import lax
from jax.experimental import pallas as pl
from jax.experimental.pallas import tpu as pltpu
from jax.sharding import PartitionSpec as P

FX, FY, V, TILE, NB, PMAX = 32, 64, 256, 128, 64, 512
DEVS, CAP, BLK = 128, 40, 41
STEPS = 3
DT, DRAG = 0.1, 0.5
H = 2
R = FX + 2 * H
RP = 40
PACK = H * FY + 16
SIDE = R * H + 16
RK = 48
CP = 80
TW = FY + 16
PADC = 8 - H
NCH = 9 * PMAX // 128
OWN = PMAX // 128
NEIGH = ((0, 0), (-1, 0), (1, 0), (-1, -1), (0, -1), (1, -1), (-1, 1), (0, 1), (1, 1))
SC = math.sqrt(100.0 * math.log2(math.e))
F32, BF16, I32 = jnp.float32, jnp.bfloat16, jnp.int32
VMEM_BYTES = 52 * 1024 * 1024


def params(size=VMEM_BYTES):
    return pltpu.CompilerParams(vmem_limit_bytes=size)


def vspec():
    return pl.BlockSpec(memory_space=pltpu.VMEM)


def sspec():
    return pl.BlockSpec(memory_space=pltpu.SMEM)


def aspec():
    return pl.BlockSpec(memory_space=pl.ANY)


def nt(a, b):
    return lax.dot_general(a, b, (((1,), (1,)), ((), ())), preferred_element_type=F32)


def nn(a, b):
    return jnp.dot(a, b, preferred_element_type=F32)


def split3(x):
    a = x.astype(BF16).astype(F32)
    b = (x - a).astype(BF16).astype(F32)
    return a, b, (x - a - b).astype(BF16).astype(F32)


def pack_kernel(count_ref, pairs_ref, centres_ref, velocity_ref, mass_ref, outline_ref, up_ref, down_ref, state_ref, sems):
    copies = []
    for k, (out, lo) in enumerate(((up_ref, FX - H), (down_ref, 0))):
        for h in range(H):
            target = out.at[h * FY : h * FY + FY, :]
            copies.append(pltpu.make_async_copy(outline_ref.at[lo + h], target, sems.at[k * H + h]))
    for copy in copies:
        copy.start()
    at = H * FY
    tail = jnp.zeros((11, 512), F32)
    count = jnp.full((1, 512), count_ref[0, 0], I32).astype(F32)
    for k in range(2):
        state_ref[k] = centres_ref[:, k, :]
        state_ref[2 + k] = velocity_ref[:, k, :]
    state_ref[4] = mass_ref[...]
    for out, lo in ((up_ref, FX - H), (down_ref, 0)):
        out[at : at + 4, :] = pairs_ref[...].astype(F32)
        out[at + 4 : at + 5, :] = count
        out[at + 5 : at + 16, :] = tail
        for k in range(5):
            out[at + 5 + k * H : at + 5 + k * H + H, 0:FY] = state_ref[k, lo : lo + H, :]
    for copy in copies:
        copy.wait()


def turn_kernel(own_ref, north_ref, south_ref, state_ref, last_ref, first_ref, west_ref, east_ref):
    at, top = H * FY, R * H
    edge = jnp.zeros((FX, 128 - FY), F32)
    lane = lax.broadcasted_iota(I32, (R, 128), 1)
    planes = []
    for k in range(5):
        rows = jnp.concatenate([state_ref[k], edge], axis=1)
        place = at + 5 + k * H
        ends = [ref[place : place + H, 0:128] for ref in (north_ref, south_ref)]
        planes.append(jnp.concatenate([ends[0], rows, ends[1]], axis=0))
    for out, cols, lo in ((west_ref, last_ref, FY - H), (east_ref, first_ref, 0)):
        for h in range(H):
            out[h * H : h * H + H, :] = north_ref[h * FY + lo : h * FY + lo + H, :]
            low = top - H * H + h * H
            out[low : low + H, :] = south_ref[h * FY + lo : h * FY + lo + H, :]
        out[H * H : H * H + FX * H, :] = cols[...]
        for k, ref in enumerate((north_ref, own_ref, south_ref)):
            out[top + 5 * k : top + 5 * k + 5, :] = ref[at : at + 5, :]
        out[top + 15 : top + 16, :] = jnp.zeros((1, 512), F32)
        block = jnp.zeros((R, 128), F32)
        for k in range(5):
            turned = pltpu.roll(planes[k], (H * k - lo) % 128, 1)
            block = jnp.where((lane >= H * k) & (lane < H * k + H), turned, block)
        out[SIDE : SIDE + R, :] = jnp.concatenate([block, jnp.zeros((R, 384), F32)], axis=1)


def send_kernel(dest_in, floe_in, rows_in, out_ref, dest_ref, floe_ref, rows_ref, place_v, ids_v, place_s, sem, sems):
    ins = [
        pltpu.make_async_copy(source, target, sems.at[k])
        for k, (source, target) in enumerate(((dest_in, dest_ref), (floe_in, floe_ref), (rows_in, rows_ref)))
    ]
    for copy in ins:
        copy.start()
    upper = (
        lax.broadcasted_iota(I32, (128, 128), 0) < lax.broadcasted_iota(I32, (128, 128), 1)
    ).astype(F32).astype(BF16)
    ones = jnp.ones((128, 128), BF16)
    index = lax.broadcasted_iota(I32, (128, 128), 0)
    @pl.loop(0, out_ref.shape[0] // 128)
    def _(i):
        out_ref[pl.ds(pl.multiple_of(i * 128, 128), 128), :] = jnp.zeros((128, 128), F32)

    ins[0].wait()
    ins[1].wait()
    blocks = dest_ref.shape[0]
    hots = [(index == dest_ref[k : k + 1, :]).astype(F32) for k in range(blocks)]
    hot16 = jnp.concatenate([hot.astype(BF16) for hot in hots], axis=0)
    before = nn(hot16, upper)
    full = nn(hot16, ones)
    carry = jnp.zeros((128, 128), F32)
    high, low, slots = [], [], []
    for k in range(blocks):
        rank = jnp.sum(hots[k] * (before[128 * k : 128 * k + 128] + carry), axis=0, keepdims=True)
        carry = carry + full[128 * k : 128 * k + 128]
        rank = rank.astype(I32)
        place_v[k : k + 1, :] = dest_ref[k : k + 1, :] * BLK + rank
        floe = floe_ref[k : k + 1, :] + 1
        slots.append((index == rank).astype(F32).astype(BF16))
        high.append((hots[k] * (floe >> 6).astype(F32)).astype(BF16))
        low.append((hots[k] * (floe & 63).astype(F32)).astype(BF16))
    slots = jnp.concatenate(slots, axis=1)
    ids = 64.0 * nt(jnp.concatenate(high, axis=1), slots) + nt(jnp.concatenate(low, axis=1), slots)
    ids_v[...] = ids
    copy = pltpu.make_async_copy(place_v, place_s, sem)
    copy.start()

    copy.wait()
    ins[2].wait()

    @pl.loop(0, rows_ref.shape[0] // 128)
    def _(k):
        for j in range(128):
            out_ref[pl.ds(place_s[k, j], 1), :] = rows_ref[pl.ds(k * 128 + j, 1), :]

    for d in range(DEVS):
        out_ref[d * BLK + CAP : d * BLK + CAP + 1, :] = ids_v[d : d + 1, :]


def ocean_kernel(rows_ref, resp_ref, out_ref, acc_ref, ids_ref):
    groups = DEVS // 16
    lane = lax.broadcasted_iota(I32, (groups, 128), 1)
    blocks = [jnp.zeros((groups, 128), F32) for _ in range(5)]
    for j in range(16):
        ids = rows_ref[pl.ds(j * BLK + CAP, groups, stride=16 * BLK), :]
        shift = (CAP * j) % 128
        if shift:
            ids = pltpu.roll(ids, shift, 1)
        for b in range(5):
            if CAP * j < 128 * b + 128 and CAP * j + CAP > 128 * b:
                place = lane + (128 * b - CAP * j)
                blocks[b] = jnp.where((place >= 0) & (place < CAP), ids, blocks[b])
    for b in range(5):
        ids_ref[b] = blocks[b]
    base16 = lax.broadcasted_iota(I32, (16, 128), 0).astype(F32)
    one, zero = jnp.ones((16, 128), BF16), jnp.zeros((16, 128), BF16)

    rows = jnp.concatenate([rows_ref[BLK * j : BLK * j + CAP, :] for j in range(DEVS)], axis=0)
    high = rows.astype(BF16)
    low = (rows - high.astype(F32)).astype(BF16)
    both = jnp.concatenate([high, low], axis=1)
    ids = [ids_ref[b, h : h + 1, :] for h in range(groups) for b in range(5)]
    for part in range(8):
        cols = []
        for row in ids:
            rel = jnp.broadcast_to(row - (part * 256 + 1.0), (16, 128)).astype(BF16)
            cols.append(
                jnp.concatenate(
                    [jnp.where((base16 + 16.0 * k).astype(BF16) == rel, one, zero) for k in range(16)], axis=0
                )
            )
        acc_ref[part * 256 : part * 256 + 256, :] = nn(jnp.concatenate(cols, axis=1), both)

    out_ref[...] = jnp.zeros_like(out_ref)
    srow = lax.broadcasted_iota(I32, (16, 128), 0)
    slane = lax.broadcasted_iota(I32, (16, 128), 1)
    pick = (((srow == 0) & (slane < NB)) | ((srow == 1) & (slane >= NB))).astype(F32).astype(BF16)
    inner = (slane >= H) & (slane < H + FY)

    for part in range(8):
        at = part * 256
        total = acc_ref[pl.ds(at, 256), 0:128] + acc_ref[pl.ds(at, 256), 128:256]
        resp = resp_ref[pl.ds(at, 256), :]
        a, b, c = split3(total * jnp.concatenate([resp, resp], axis=1))
        force = nt(pick, a.astype(BF16)) + nt(pick, b.astype(BF16)) + nt(pick, c.astype(BF16))
        for j in range(4):
            piece = force[:, (j // 2) * 128 : (j // 2) * 128 + 128]
            piece = pltpu.roll(piece, (H - 64 * (j % 2)) % 128, 1)
            piece = jnp.where(inner, piece, 0.0)
            for k in range(2):
                out_ref[k, part * 4 + j + H : part * 4 + j + H + 1, :] = piece[k : k + 1]


def put_shift(left_ref, plane_ref, planes):
    for k in range(2):
        plane_ref[0:R, :] = planes[k]
        for j, part in enumerate(split3(jnp.transpose(plane_ref[...])[0:CP])):
            left_ref[3 * k + j] = part


def look_up(word, left_ref):
    count = word.shape[1]
    rows = jnp.concatenate([(word >> 7) & 63, (word >> 20) & 63], axis=1)
    cols = jnp.concatenate([word & 127, (word >> 13) & 127], axis=1)
    step_x, step_y = code_steps((word >> 28) & 7)
    row_hot16 = (lax.broadcasted_iota(I32, (RK, 2 * count), 0) == rows).astype(F32).astype(BF16)
    col_hot = lax.broadcasted_iota(I32, (CP, 2 * count), 0) == cols
    offsets = []
    for k, step in enumerate((step_x, step_y)):
        left = jnp.concatenate([left_ref[3 * k + j, :, 0:RK] for j in range(3)], axis=0)
        part = nn(left.astype(BF16), row_hot16)
        part = part[0:CP] + part[CP : 2 * CP] + part[2 * CP : 3 * CP]
        part = jnp.sum(jnp.where(col_hot, part, 0.0), axis=0, keepdims=True)
        offsets.append((step.astype(F32) - (part[:, 0:count] - part[:, count : 2 * count])) * SC)
    return offsets


def add_forces(word, ok, fx, fy, acc_ref):
    rows = jnp.concatenate([(word >> 7) & 63, (word >> 20) & 63], axis=1)
    cols = jnp.concatenate([word & 127, (word >> 13) & 127], axis=1)
    row_hot = (lax.broadcasted_iota(I32, (RP, rows.shape[1]), 0) == rows).astype(F32)
    col_hot = (lax.broadcasted_iota(I32, (128, rows.shape[1]), 0) == cols).astype(F32).astype(BF16)
    parts = split3(jnp.where(ok, fx, 0.0)) + split3(jnp.where(ok, fy, 0.0))
    spread = [row_hot * jnp.concatenate([part, -part], axis=1) for part in parts]
    acc_ref[...] += nt(jnp.concatenate(spread, axis=0).astype(BF16), col_hot)


def chunk_forces(c, half, dx, dy, tiles_ref, b_ref):
    px = tiles_ref[c, 2] + dx
    py = tiles_ref[c, 3] + dy
    b_ref[0] = 2.0 * px
    b_ref[1] = 2.0 * py
    b_ref[2] = -(px * px + py * py)
    turns = jnp.where(half, TILE // 64, TILE // 32)

    @pl.when(half)
    def _():
        left_half = lax.broadcasted_iota(I32, (64, 128), 1) < 64
        for k in range(3):
            b_ref[k, 0:64, :] = jnp.where(left_half, b_ref[k, 0:64, :], b_ref[k, 64:128, :])

    force_x = jnp.zeros((8, 128), F32)
    force_y = jnp.zeros((8, 128), F32)
    back_x = jnp.zeros((8, 128), F32)
    back_y = jnp.zeros((8, 128), F32)
    for half in range(2):
        ax = [tiles_ref[c, 0, half * 64 + 8 * k : half * 64 + 8 * k + 8, :] for k in range(8)]
        ay = [tiles_ref[c, 1, half * 64 + 8 * k : half * 64 + 8 * k + 8, :] for k in range(8)]
        na = [-(x * x + y * y) for x, y in zip(ax, ay)]

        def body(i, carry):
            sums, bx_sum, by_sum = carry
            sums = list(sums)
            for j in range(32):
                w = i * 32 + j
                bx = jnp.broadcast_to(b_ref[0, pl.ds(w, 1), :], (8, 128))
                by = jnp.broadcast_to(b_ref[1, pl.ds(w, 1), :], (8, 128))
                nb = jnp.broadcast_to(b_ref[2, pl.ds(w, 1), :], (8, 128))
                weights = [jnp.exp2((ax[k] * bx + ay[k] * by) + (na[k] + nb)) for k in range(8)]
                sums = [s + t for s, t in zip(sums, weights)]
                while len(weights) > 1:
                    weights = [weights[k] + weights[k + 1] for k in range(0, len(weights), 2)]
                bx_sum = bx_sum + weights[0] * bx
                by_sum = by_sum + weights[0] * by
            return tuple(sums), bx_sum, by_sum

        sums, back_x, back_y = lax.fori_loop(
            0, turns, body, (tuple(jnp.zeros((8, 128), F32) for _ in range(8)), back_x, back_y)
        )
        for k in range(8):
            force_x = force_x + ax[k] * sums[k]
            force_y = force_y + ay[k] * sums[k]
    fx = jnp.sum(force_x - 0.5 * back_x, axis=0, keepdims=True) * (1.0 / SC)
    fy = jnp.sum(force_y - 0.5 * back_y, axis=0, keepdims=True) * (1.0 / SC)
    return fx, fy


def contact_chunk(c, half_at, live, words_ref, tiles_ref, left_ref, b_ref, acc_ref):
    word = words_ref[pl.ds(c, 1), :]
    lane = lax.broadcasted_iota(I32, (1, 128), 1)
    ok = (word >= 0) & (c * 128 + jnp.where(c == half_at, lane & 63, lane) < live)
    dx, dy = look_up(word, left_ref)
    fx, fy = chunk_forces(c, c == half_at, dx, dy, tiles_ref, b_ref)
    add_forces(word, ok, fx, fy, acc_ref)


def acc_plane(acc_ref, k):
    at = 3 * RP * k
    return acc_ref[at : at + R, :] + acc_ref[at + RP : at + RP + R, :] + acc_ref[at + 2 * RP : at + 2 * RP + R, :]


def code_steps(code):
    code9 = code + (code >= 4).astype(I32)
    step = (code9 >= 3).astype(I32) + (code9 >= 6).astype(I32)
    return step - 1, code9 - 3 * step - 1


def pair_words(local, code, mine, theirs, count, di, dj):
    step_x, step_y = code_steps(code)
    row = (local >> 6) + di * FX
    col = (local & 63) + dj * FY
    prow = row + step_x
    pcol = col + step_y
    row_all = prow + lax.axis_index("gx") * FX
    col_all = pcol + lax.axis_index("gy") * FY
    live = lax.broadcasted_iota(I32, local.shape, 1) < count
    live = live & (row_all >= 0) & (row_all < lax.axis_size("gx") * FX)
    live = live & (col_all >= 0) & (col_all < lax.axis_size("gy") * FY)
    inside = (prow >= 0) & (prow < FX) & (pcol >= 0) & (pcol < FY)
    near = (row >= -1) & (row <= FX) & (col >= -1) & (col <= FY)
    near = near | ((prow >= -1) & (prow <= FX) & (pcol >= -1) & (pcol <= FY))
    word = (row + H) * 128 + col + H + (((prow + H) * 128 + pcol + H) << 13)
    return word + (mine << 26) + (theirs << 27) + (code << 28), live, inside, near


def load_tiles(c, place_s, flat, size, stage, tiles):
    @pl.loop(0, 16)
    def _(i):
        for j in range(8):
            at = i * 8 + j
            own = place_s[0, c, at]
            other = place_s[1, c, at]
            stage[0, pl.ds(at, 1), :] = flat[pl.ds(own, 1), :]
            stage[1, pl.ds(at, 1), :] = flat[pl.ds(own + 2 * size, 1), :]
            stage[2, pl.ds(at, 1), :] = flat[pl.ds(other, 1), :]
            stage[3, pl.ds(at, 1), :] = flat[pl.ds(other + 2 * size, 1), :]

    for k in range(4):
        tiles[c, k] = jnp.transpose(stage[k]) * SC


def inner_kernel(
    count_ref, own_ref, state_ref, outline_ref, tiles, words_out, force_out, last_ref, first_ref,
    table, stage, place_v, place_s, left_ref, plane_ref, b_ref, acc_ref, sems,
):
    copies = []
    for q in range(4):
        source = outline_ref.at[:, :, slice(q * 128, q * 128 + 128)]
        copies.append(pltpu.make_async_copy(source, table.at[q], sems.at[q]))
    for copy in copies:
        copy.start()
    live = count_ref[0, 0]
    fields = [own_ref[k : k + 1, :] for k in range(4)]
    word, ok, inside, _ = pair_words(*fields, live, 0, 0)
    word = jnp.where(ok & inside, word, -1)
    for b in range(OWN):
        words_out[b : b + 1, :] = word[:, 128 * b : 128 * b + 128]
    word = jnp.maximum(words_out[...], H * 128 + H + ((H * 128 + H) << 13))
    own = (((word >> 7) & 63) - H) * FY + (word & 127) - H
    other = (((word >> 20) & 63) - H) * FY + ((word >> 13) & 127) - H
    place_v[0] = own + ((word >> 26) & 1) * (FX * FY)
    place_v[1] = other + ((word >> 27) & 1) * (FX * FY)
    copy = pltpu.make_async_copy(place_v, place_s, sems.at[4])
    copy.start()
    plane_ref[...] = jnp.zeros_like(plane_ref)
    acc_ref[...] = jnp.zeros_like(acc_ref)
    edge = jnp.zeros((FX, 128 - FY), F32)
    planes = []
    for k in range(2):
        plane = pltpu.roll(jnp.concatenate([state_ref[k], edge], axis=1), H, 1)
        ends = jnp.zeros((H, 128), F32)
        planes.append(jnp.concatenate([ends, plane, ends], axis=0))
    put_shift(left_ref, plane_ref, planes)
    for piece in copies:
        piece.wait()
    copy.wait()
    for out, lo in ((last_ref, FY - H), (first_ref, 0)):
        for r in range(FX):
            for q in range(4):
                out[r * H : r * H + H, q * 128 : q * 128 + 128] = table[q, r, lo : lo + H, :]
    flat = table.reshape(4 * FX * FY, 128)

    @pl.loop(0, (live + 127) >> 7)
    def _(c):
        load_tiles(c, place_s, flat, FX * FY, stage, tiles)
        contact_chunk(c, -1, PMAX, words_out, tiles, left_ref, b_ref, acc_ref)

    for k in range(2):
        force_out[k] = acc_plane(acc_ref, k)


def edge_kernel(
    own_ref, state_ref, outline_ref, north_ref, south_ref, west_ref, east_ref,
    tiles_out, words_out, count_out, force_out, wide_ref,
    table, tiles, stage, place_v, place_s, left_ref, plane_ref, b_ref, acc_ref, sems, tile_sems,
):
    copies = []
    for q in range(4):
        lanes = slice(q * 128, q * 128 + 128)
        target = table.at[q, H : H + FX, 8 : 8 + FY, :]
        copies.append(pltpu.make_async_copy(outline_ref.at[:, :, lanes], target, sems.at[3 * q]))
        for h in range(H):
            table[q, h, 8 : 8 + FY, :] = north_ref[h * FY : h * FY + FY, lanes]
            table[q, H + FX + h, 8 : 8 + FY, :] = south_ref[h * FY : h * FY + FY, lanes]
        for r in range(R):
            table[q, r, PADC:8, :] = west_ref[r * H : r * H + H, lanes]
            table[q, r, 8 + FY : 8 + FY + H, :] = east_ref[r * H : r * H + H, lanes]
    for copy in copies:
        copy.start()
    edge = jnp.zeros((FX, 128 - FY), F32)

    lane = lax.broadcasted_iota(I32, (R, 128), 1)
    inside = (lane >= H) & (lane < H + FY)
    for k in range(5):
        at = H * FY + 5 + k * H
        rows = jnp.concatenate([state_ref[k], edge], axis=1)
        rows = jnp.concatenate([north_ref[at : at + H, 0:128], rows, south_ref[at : at + H, 0:128]], axis=0)
        left = pltpu.roll(west_ref[SIDE : SIDE + R, 0:128], (-H * k) % 128, 1)
        right = pltpu.roll(east_ref[SIDE : SIDE + R, 0:128], (H + FY - H * k) % 128, 1)
        plane = jnp.where(inside, pltpu.roll(rows, H, 1), jnp.where(lane < H, left, right))
        plane = jnp.where(lane < FY + 2 * H, plane, 0.0)
        wide_ref[k] = jnp.where(plane == 0.0, 1.0, plane) if k == 4 else plane
    top = R * H
    heads = [
        (own_ref, H * FY), (north_ref, H * FY), (south_ref, H * FY), (west_ref, top), (west_ref, top + 5),
        (west_ref, top + 10), (east_ref, top), (east_ref, top + 5), (east_ref, top + 10),
    ]
    fields = [
        jnp.concatenate([ref[at + k : at + k + 1, :] for ref, at in heads], axis=0).astype(I32) for k in range(5)
    ]
    lists = len(NEIGH)
    number = lax.broadcasted_iota(I32, (lists, PMAX), 0)
    di, dj = jnp.zeros((lists, PMAX), I32), jnp.zeros((lists, PMAX), I32)
    for k, (i, j) in enumerate(NEIGH):
        di = jnp.where(number == k, i, di)
        dj = jnp.where(number == k, j, dj)
    word, ok, inside, near = pair_words(*fields, di, dj)
    ok = ok & near & ((number > 0) | ~inside)
    flags = jnp.where(ok, 1.0, 0.0)
    upper = (
        lax.broadcasted_iota(I32, (PMAX, PMAX), 0) < lax.broadcasted_iota(I32, (PMAX, PMAX), 1)
    ).astype(F32).astype(BF16)
    padded = jnp.concatenate([flags, jnp.zeros((16 - lists, PMAX), F32)], axis=0)
    rank = nn(padded.astype(BF16), upper)
    base = jnp.zeros((1, 1), F32)
    ranks = []
    for k in range(lists):
        ranks.append(jnp.where(flags[k : k + 1] > 0.0, rank[k : k + 1] + base, -1.0).astype(I32))
        base = base + jnp.sum(flags[k : k + 1], axis=1, keepdims=True)
    found_all = jnp.sum(flags).astype(I32)
    mine = jnp.sum(flags[0:1]).astype(I32)
    total = (found_all + 127) >> 7
    whole = (found_all + 63) >> 7
    half_at = jnp.where(total > whole, total - 1, -1)
    words_out[...] = jnp.full(words_out.shape, -1, I32)
    slot = lax.broadcasted_iota(I32, (128, PMAX), 0)
    srow = lax.broadcasted_iota(I32, (16, PMAX), 0)
    pieces = []
    for k in range(lists):
        one = word[k : k + 1]
        piece = jnp.where(srow == 0, one & 255, jnp.where(srow == 1, (one >> 8) & 255, 0))
        piece = jnp.where(srow == 2, (one >> 16) & 255, jnp.where(srow == 3, (one >> 24) & 127, piece))
        piece = jnp.where(srow == 4, 1, piece)
        pieces.append(piece.astype(F32).astype(BF16))

    @pl.loop(0, total)
    def _(i):
        found = jnp.zeros((16, 128), F32)
        want = jnp.where(i >= whole, slot & 63, slot)
        for k in range(lists):
            found = found + nt(pieces[k], (want == ranks[k] - i * 128).astype(F32).astype(BF16))
        found = found.astype(I32)
        value = found[0:1] + (found[1:2] << 8) + (found[2:3] << 16) + (found[3:4] << 24)
        words_out[pl.ds(i, 1), :] = jnp.where(found[4:5] > 0, value, -1)

    word = jnp.maximum(words_out[...], 0)
    own = ((word >> 7) & 63) * TW + (word & 127) + PADC
    other = ((word >> 20) & 63) * TW + ((word >> 13) & 127) + PADC
    place_v[0] = own + ((word >> 26) & 1) * (R * TW)
    place_v[1] = other + ((word >> 27) & 1) * (R * TW)
    copy = pltpu.make_async_copy(place_v, place_s, sems.at[20])
    copy.start()
    count_out[0] = total
    count_out[1] = half_at
    plane_ref[...] = jnp.zeros_like(plane_ref)
    acc_ref[...] = jnp.zeros_like(acc_ref)
    put_shift(left_ref, plane_ref, [wide_ref[0], wide_ref[1]])
    for piece in copies:
        piece.wait()

    copy.wait()
    flat = table.reshape(4 * R * TW, 128)

    @pl.loop(0, total)
    def _(c):
        load_tiles(c, place_s, flat, R * TW, stage, tiles)
        pltpu.make_async_copy(tiles.at[c], tiles_out.at[c], tile_sems.at[c]).start()

    @pl.loop(0, (mine + 127) >> 7)
    def _(c):
        contact_chunk(c, half_at, mine, words_out, tiles, left_ref, b_ref, acc_ref)

    for k in range(2):
        force_out[k] = acc_plane(acc_ref, k)

    @pl.loop(0, total)
    def _(c):
        pltpu.make_async_copy(tiles.at[c], tiles_out.at[c], tile_sems.at[c]).wait()


def later_kernel(
    live_ref, count_ref, force_ref, state_ref, words_in, edge_words, tiles_in, edge_tiles, vel_out, shift_out,
    words_ref, tiles, left_ref, plane_ref, b_ref, acc_ref, now_ref, move_ref, tile_sems,
):
    inner = (live_ref[0, 0] + 127) >> 7
    total = count_ref[0] + inner
    half_at = jnp.where(count_ref[1] >= 0, count_ref[1] + OWN, -1)

    @pl.loop(0, inner)
    def _(c):
        pltpu.make_async_copy(tiles_in.at[c], tiles.at[c], tile_sems.at[c]).start()

    @pl.loop(0, total - inner)
    def _(c):
        pltpu.make_async_copy(edge_tiles.at[c], tiles.at[c + OWN], tile_sems.at[c + OWN]).start()

    words_ref[0:OWN, :] = words_in[0:OWN, :]
    words_ref[OWN : OWN + NCH, :] = edge_words[...]
    words_ref[OWN + NCH : OWN + NCH + 8, :] = jnp.full((8, 128), -1, I32)
    now_ref[...] = state_ref[...]

    def update(forces):
        scale = DT / now_ref[4]
        for k in range(2):
            vel = now_ref[2 + k]
            vel = vel + (forces[k] - DRAG * vel) * scale
            now_ref[2 + k] = vel
            now_ref[k] = now_ref[k] + DT * vel

    update([force_ref[0], force_ref[1]])
    plane_ref[...] = jnp.zeros_like(plane_ref)

    move_ref[...] = jnp.zeros_like(move_ref)
    twos = (total + 1) >> 1

    def spot(i):
        return jnp.where(i < inner, i, i - inner + OWN)

    def two_words(i):
        return jnp.concatenate([words_ref[pl.ds(spot(2 * i + j), 1), :] for j in range(2)], axis=1)

    @pl.loop(1, STEPS)
    def _(step):
        put_shift(left_ref, plane_ref, [now_ref[0], now_ref[1]])
        acc_ref[...] = jnp.zeros_like(acc_ref)

        @pl.loop(0, twos)
        def _(i):
            for k, offset in enumerate(look_up(two_words(i), left_ref)):
                for j in range(2):
                    move_ref[k, pl.ds(2 * i + j, 1), :] = offset[:, 128 * j : 128 * j + 128]

        @pl.when(step == 1)
        def _():
            @pl.loop(0, inner)
            def _(c):
                pltpu.make_async_copy(tiles_in.at[c], tiles.at[c], tile_sems.at[c]).wait()

            @pl.loop(0, total - inner)
            def _(c):
                pltpu.make_async_copy(edge_tiles.at[c], tiles.at[c + OWN], tile_sems.at[c + OWN]).wait()

        @pl.loop(0, total)
        def _(i):
            c = spot(i)
            dx, dy = [move_ref[k, pl.ds(i, 1), :] for k in range(2)]
            fx, fy = chunk_forces(c, c == half_at, dx, dy, tiles, b_ref)
            move_ref[2, pl.ds(i, 1), :] = fx
            move_ref[3, pl.ds(i, 1), :] = fy

        @pl.loop(0, twos)
        def _(i):
            word = two_words(i)
            fx, fy = [
                jnp.concatenate([move_ref[k, pl.ds(2 * i + j, 1), :] for j in range(2)], axis=1) for k in (2, 3)
            ]
            add_forces(word, word >= 0, fx, fy, acc_ref)

        update([acc_plane(acc_ref, k) + force_ref[2 + k] for k in range(2)])

    for out, base in ((shift_out, 0), (vel_out, 2)):
        for k in range(2):
            plane_ref[0:R, :] = pltpu.roll(now_ref[base + k], 128 - H, 1)
            for r in range(FX):
                out[r, k : k + 1, :] = plane_ref[r + H : r + H + 1, 0:FY]


def moved(x, axis, up):
    count = lax.axis_size(axis)
    pairs = [(i, i + 1) if up else (i + 1, i) for i in range(count - 1)]
    return lax.ppermute(x, axis, pairs)


def shards(
    outline, centres, velocity, mass, response, pairs, pair_count, forcing, ocean_dest, ocean_floe
):
    rows_dev = forcing.shape[0]
    send = pl.pallas_call(
        send_kernel,
        name="send_rows",
        out_shape=jax.ShapeDtypeStruct((DEVS * BLK, 128), F32),
        in_specs=[pl.BlockSpec(memory_space=pltpu.HBM)] * 3,
        out_specs=vspec(),
        scratch_shapes=[
            pltpu.VMEM((rows_dev // 128, 128), I32),
            pltpu.VMEM((rows_dev // 128, 128), I32),
            pltpu.VMEM((rows_dev, 128), F32),
            pltpu.VMEM((rows_dev // 128, 128), I32),
            pltpu.VMEM((DEVS, 128), F32),
            pltpu.SMEM((rows_dev // 128, 128), I32),
            pltpu.SemaphoreType.DMA,
            pltpu.SemaphoreType.DMA((3,)),
        ],
        compiler_params=params(63 << 20),
        cost_estimate=pl.CostEstimate(flops=100000000, bytes_accessed=4 << 20, transcendentals=0),
    )(ocean_dest.reshape(rows_dev // 128, 128), ocean_floe.reshape(rows_dev // 128, 128), forcing)
    pair_rows = jnp.transpose(pairs[0, 0], (1, 0))
    mass, send = lax.optimization_barrier((mass, send))
    got = lax.all_to_all(
        send.reshape(DEVS, 1, BLK * 128), ("gx", "gy"), split_axis=0, concat_axis=0, tiled=True
    )
    up, down, state = pl.pallas_call(
        pack_kernel,
        name="pack_rows",
        out_shape=[jax.ShapeDtypeStruct((PACK, 512), F32)] * 2 + [jax.ShapeDtypeStruct((5, FX, FY), F32)],
        in_specs=[sspec()] + [vspec()] * 4 + [aspec()],
        out_specs=[vspec()] * 3,
        scratch_shapes=[pltpu.SemaphoreType.DMA((2 * H,))],
        compiler_params=params(),
        cost_estimate=pl.CostEstimate(flops=1000000, bytes_accessed=1 << 20, transcendentals=0),
    )(pair_count, pair_rows, jnp.transpose(centres, (0, 2, 1)), jnp.transpose(velocity, (0, 2, 1)), mass, outline)

    chunk_scratch = [
        pltpu.VMEM((6, CP, 128), F32),
        pltpu.VMEM((128, 128), F32),
        pltpu.VMEM((3, 128, 128), F32),
        pltpu.VMEM((6 * RP, 128), F32),
    ]
    tiles, words, contact, last, first = pl.pallas_call(
        inner_kernel,
        name="inner_pairs",
        out_shape=[
            jax.ShapeDtypeStruct((OWN, 4, 128, 128), F32),
            jax.ShapeDtypeStruct((OWN, 128), I32),
            jax.ShapeDtypeStruct((2, R, 128), F32),
            jax.ShapeDtypeStruct((FX * H, 512), F32),
            jax.ShapeDtypeStruct((FX * H, 512), F32),
        ],
        in_specs=[sspec(), vspec(), vspec(), aspec()],
        out_specs=[vspec()] * 5,
        scratch_shapes=[
            pltpu.VMEM((4, FX, FY, 128), F32),
            pltpu.VMEM((4, 128, 128), F32),
            pltpu.VMEM((2, OWN, 128), I32),
            pltpu.SMEM((2, OWN, 128), I32),
            *chunk_scratch,
            pltpu.SemaphoreType.DMA((5,)),
        ],
        compiler_params=params(),
        cost_estimate=pl.CostEstimate(flops=500000000, bytes_accessed=8 << 20, transcendentals=8 << 20),
    )(pair_count, pair_rows, state, outline)
    north, south, contact = lax.optimization_barrier((moved(up, "gx", True), moved(down, "gx", False), contact))
    west, east = pl.pallas_call(
        turn_kernel,
        name="pack_columns",
        out_shape=[jax.ShapeDtypeStruct((SIDE + R, 512), F32)] * 2,
        in_specs=[vspec()] * 6,
        out_specs=[vspec()] * 2,
        compiler_params=params(),
        cost_estimate=pl.CostEstimate(flops=1000000, bytes_accessed=1 << 20, transcendentals=0),
    )(up, north, south, state, last, first)
    west, east, got = lax.optimization_barrier((west, east, got))
    west, east = moved(west, "gy", True), moved(east, "gy", False)
    ocean = pl.pallas_call(
        ocean_kernel,
        name="ocean_sum",
        out_shape=jax.ShapeDtypeStruct((2, R, 128), F32),
        in_specs=[vspec()] * 2,
        out_specs=vspec(),
        scratch_shapes=[
            pltpu.VMEM((FX * FY, 256), F32),
            pltpu.VMEM((5, DEVS // 16, 128), F32),
        ],
        compiler_params=params(),
        cost_estimate=pl.CostEstimate(flops=5000000000, bytes_accessed=5 << 20, transcendentals=0),
    )(got.reshape(DEVS * BLK, 128), response.reshape(FX * FY, NB))
    west, east, ocean = lax.optimization_barrier((west, east, ocean))
    edge_tiles, edge_words, counts, edge_contact, wide = pl.pallas_call(
        edge_kernel,
        out_shape=[
            jax.ShapeDtypeStruct((NCH, 4, 128, 128), F32),
            jax.ShapeDtypeStruct((NCH, 128), I32),
            jax.ShapeDtypeStruct((2,), I32),
            jax.ShapeDtypeStruct((2, R, 128), F32),
            jax.ShapeDtypeStruct((5, R, 128), F32),
        ],
        in_specs=[vspec()] * 2 + [aspec()] + [vspec()] * 4,
        out_specs=[aspec(), vspec(), sspec(), vspec(), vspec()],
        scratch_shapes=[
            pltpu.VMEM((4, R, TW, 128), F32),
            pltpu.VMEM((NCH, 4, 128, 128), F32),
            pltpu.VMEM((4, 128, 128), F32),
            pltpu.VMEM((2, NCH, 128), I32),
            pltpu.SMEM((2, NCH, 128), I32),
            *chunk_scratch,
            pltpu.SemaphoreType.DMA((21,)),
            pltpu.SemaphoreType.DMA((NCH,)),
        ],
        compiler_params=params(),
        name="edge_pairs",
        cost_estimate=pl.CostEstimate(flops=500000000, bytes_accessed=8 << 20, transcendentals=8 << 20),
    )(up, state, outline, north, south, west, east)

    force = jnp.concatenate([contact + edge_contact + ocean, ocean], axis=0)
    w = 2 * H - 1
    low, high = moved(force[:, FX : FX + w], "gx", True), moved(force[:, 1 : 1 + w], "gx", False)
    force = force + jnp.pad(low, ((0, 0), (0, R - w), (0, 0))) + jnp.pad(high, ((0, 0), (R - w, 0), (0, 0)))
    low, high = moved(force[:, :, FY : FY + w], "gy", True), moved(force[:, :, 1 : 1 + w], "gy", False)
    c = FY + 2 * H
    force = force + jnp.pad(low, ((0, 0), (0, 0), (0, 128 - w))) + jnp.pad(high, ((0, 0), (0, 0), (c - w, 128 - c)))

    vel, shift = pl.pallas_call(
        later_kernel,
        name="later_steps",
        out_shape=[jax.ShapeDtypeStruct((FX, 2, FY), F32)] * 2,
        in_specs=[sspec(), sspec()] + [vspec()] * 4 + [aspec()] * 2,
        out_specs=[vspec()] * 2,
        scratch_shapes=[
            pltpu.VMEM((OWN + NCH + 8, 128), I32),
            pltpu.VMEM((OWN + NCH, 4, 128, 128), F32),
            *chunk_scratch,
            pltpu.VMEM((5, R, 128), F32),
            pltpu.VMEM((4, OWN + NCH + 8, 128), F32),
            pltpu.SemaphoreType.DMA((OWN + NCH,)),
        ],
        compiler_params=params(),
        cost_estimate=pl.CostEstimate(flops=500000000, bytes_accessed=4 << 20, transcendentals=16 << 20),
    )(pair_count, counts, force, wide, words, edge_words, tiles, edge_tiles)
    return jnp.transpose(vel, (0, 2, 1)), jnp.transpose(shift, (0, 2, 1))


def solution(mesh):
    return jax.shard_map(
        shards,
        mesh=mesh,
        in_specs=(
            P("gx", "gy", None),
            P("gx", "gy", None),
            P("gx", "gy", None),
            P("gx", "gy"),
            P("gx", "gy", None),
            P("gx", "gy", None, None),
            P("gx", "gy"),
            P(("gx", "gy"), None),
            P(("gx", "gy"), None),
            P(("gx", "gy")),
        ),
        out_specs=(P("gx", "gy", None), P("gx", "gy", None)),
        check_vma=False,
    )
```
